32 devices in a mesh: segment: 4 (over x, core), grp: 4 (over z), sp: 2 (over y).
Axes of the slice: x: 2, y: 2, z: 4, core: 2. Of those that a mesh axis runs over, the one named last changes fastest.
Arguments:
- queries: bfloat16 [4, 4, 4, 8, 16, 2048], P('segment', 'grp', None, 'sp'), may hold values from -140 to 140
- key_states: bfloat16 [4, 4, 4, 8, 16, 2048], P('segment', 'grp', None, 'sp'), may hold values from -6 to 6
- value_states: bfloat16 [4, 4, 4, 8, 16, 2048], P('segment', 'grp', None, 'sp'), may hold values from -6 to 6
- kept_tiles: int32 [16, 2, 2], replicated, may hold values from 0 to 1, as said below
- kept_counts: int32 [16, 2], replicated, may hold values from 1 to 2
- patch_weight: bfloat16 [2048, 64], replicated, may hold values from -1.5 to 1.5
- decode_slot: int32 [4], replicated, may hold values from 0 to 3, each once
- first_kernel: bfloat16 [27, 16, 256], replicated, may hold values from -0.3125 to 0.3125
- second_kernel: bfloat16 [27, 256, 256], P(None, 'grp'), may hold values from -0.078125 to 0.078125
Outputs:
- decoded: bfloat16 [4, 4, 4, 16, 32, 256], P('segment', 'grp', None, 'sp')
The draws below stay inside these ranges and needn't reach their ends.
Inputs may be any that keep to these rules, and one draw needn't show every extreme that they name: `kept_tiles`: for each head and query tile the 2 entries name distinct tiles, the query tile itself among them in some slot.
All inputs are finite; a program needn't handle non-finite values.
Results may differ from the reference program's by a relative error of at most 0.018.
Values may be sent and summed in bfloat16 or wider, within the bound.
No kernel may reach another device: no remote copies, remote signals or barrier semaphores. Data moves between devices by JAX's collectives and lax.ppermute only.
A program may use at most 128 MiB of HBM per device.

```python
import jax
import jax.numpy as jnp
from jax import lax

HEADS = 16
HD = 128
LAT = 16
CH = 256
TT = 4
TH = 8
TW = 8
FT = 4
FW = 16
FH = 8
TILE = 256
SEQ = 512
NT = 2
KEEP = 2
MICRO = 4
CLIPS = 4


def grid_shape():
    return (MICRO, CLIPS, FT, FH, FW, HEADS * HD)


def shared_keys(key):
    return jax.random.truncated_normal(jax.random.fold_in(key, 7), -6.0, 6.0, grid_shape(), jnp.float32)


def draw_key_states(key, part):
    base = shared_keys(key)
    return base.astype(jnp.bfloat16)


def draw_queries(key, part):
    base = shared_keys(key)
    key = jax.random.fold_in(key, 5)
    result = jax.random.truncated_normal(jax.random.fold_in(key, 2), -6.0, 6.0, base.shape, jnp.float32)
    return result.astype(jnp.bfloat16)


def draw_kept_tiles(key, part):
    key = jax.random.fold_in(key, 11)
    noise = jax.random.randint(jax.random.fold_in(key, 1), (HEADS, NT, NT), 0, 1 << 20)
    column = jnp.arange(NT, dtype=jnp.int32)
    ranked = noise * NT + column[None, None, :]
    ranked = jnp.where(column[None, None, :] == column[None, :, None], -1, ranked)
    order = jnp.argsort(ranked, axis=-1, stable=True)[:, :, :KEEP]
    slot_noise = jax.random.randint(jax.random.fold_in(key, 2), (HEADS, NT, KEEP), 0, 1 << 20)
    slot_rank = slot_noise * KEEP + jnp.arange(KEEP, dtype=jnp.int32)[None, None, :]
    shuffle = jnp.argsort(slot_rank, axis=-1, stable=True)
    return jnp.take_along_axis(order, shuffle, axis=-1).astype(jnp.int32)


def draw_kept_counts(key, part):
    key = jax.random.fold_in(key, 13)
    level = jax.random.randint(jax.random.fold_in(key, 1), (HEADS, 1), 1, KEEP + 1)
    counts = jax.random.randint(jax.random.fold_in(key, 2), (HEADS, NT), 1, level + 1)
    chosen_spot = jax.random.randint(jax.random.fold_in(key, 3), (), 0, HEADS * NT)
    flat_counts = jnp.where(jnp.arange(HEADS * NT) == chosen_spot, KEEP, counts.reshape(-1))
    return flat_counts.reshape(HEADS, NT).astype(jnp.int32)


def shard_levels(stream_key, shape, cuts, low, largest):
    gain = 1.0
    for position, parts in cuts:
        draws = jax.random.uniform(jax.random.fold_in(jax.random.fold_in(stream_key, 6), position), (parts,), jnp.float32, low / len(cuts), largest / len(cuts))
        gain = gain * jnp.repeat(jnp.exp(draws), shape[position] // parts).reshape((-1,) + (1,) * (len(shape) - 1 - position))
    return gain


def centred(key, dims, spread, bound, split=(), kind=jnp.bfloat16):
    drawn = spread * jax.random.normal(key, dims, jnp.float32)
    if split:
        drawn = drawn * shard_levels(key, dims, split, -0.22, 0.18)
    return jnp.clip(drawn, -bound, bound).astype(kind)


def setup_inputs(seed: int = 0) -> dict:
    seeds = jax.random.split(jax.random.key(seed), 10)
    queries = draw_queries(jax.random.fold_in(seeds[9], 71), 0)
    key_states = draw_key_states(jax.random.fold_in(seeds[9], 71), 0)
    value_states = centred(seeds[2], (MICRO, CLIPS, FT, FH, FW, HEADS * HD), 1.0, 6.0, ((0, 4), (1, 4), (3, 2)))
    kept_tiles = draw_kept_tiles(jax.random.fold_in(seeds[9], 71), 0)
    kept_counts = draw_kept_counts(jax.random.fold_in(seeds[9], 71), 0)
    patch_weight = centred(seeds[5], (HEADS * HD, 4 * LAT), 16 ** -0.5, 1.5)
    decode_slot = jax.random.permutation(seeds[6], MICRO).astype(jnp.int32)
    first_kernel = centred(seeds[7], (27, LAT, CH), (27 * LAT) ** -0.5, 0.3125)
    second_kernel = centred(seeds[8], (27, CH, CH), (27 * CH) ** -0.5, 0.078125, ((1, 4),))
    return {"queries": queries, "key_states": key_states, "value_states": value_states, "kept_tiles": kept_tiles, "kept_counts": kept_counts, "patch_weight": patch_weight, "decode_slot": decode_slot, "first_kernel": first_kernel, "second_kernel": second_kernel}


VAE_SCALE = 1.0 / 0.476986


def head_attention(packed):
    query_tiles, key_tiles, value_tiles, tile_index, live_count = packed
    key_sel = key_tiles[tile_index].reshape(NT, KEEP * TILE, HD)
    value_sel = value_tiles[tile_index].reshape(NT, KEEP * TILE, HD)
    scores = jnp.einsum('nqd,nkd->nqk', query_tiles.astype(jnp.float32), key_sel.astype(jnp.float32)) * (HD ** -0.5)
    live = jnp.arange(KEEP, dtype=jnp.int32)[None, :] < live_count[:, None]
    live = jnp.repeat(live, TILE, axis=1)[:, None, :]
    scores = jnp.where(live, scores, -1e30)
    row_top = jnp.max(scores, axis=-1, keepdims=True)
    exponent = jnp.where(live, jnp.exp(scores - row_top), 0.0)
    weights = (exponent / jnp.sum(exponent, axis=-1, keepdims=True)).astype(jnp.bfloat16)
    result = jnp.einsum('nqk,nkd->nqd', weights.astype(jnp.float32), value_sel.astype(jnp.float32))
    return result.astype(jnp.bfloat16)


def to_tiles(grid):
    feature_width = grid.shape[-1]
    tiled = grid.reshape(FT // TT, TT, FH // TH, TH, FW // TW, TW, feature_width).transpose(0, 2, 4, 1, 3, 5, 6)
    return tiled.reshape(NT, TILE, feature_width)


def from_tiles(tiles):
    feature_width = tiles.shape[-1]
    grid = tiles.reshape(FT // TT, FH // TH, FW // TW, TT, TH, TW, feature_width).transpose(0, 3, 1, 4, 2, 5, 6)
    return grid.reshape(FT, FH, FW, feature_width)


def split_heads(tiles):
    return tiles.reshape(NT, TILE, HEADS, HD).transpose(2, 0, 1, 3)


def clip_latent(query_clip, key_clip, value_clip, kept_tiles, kept_counts, patch_weight):
    packed = (split_heads(to_tiles(query_clip)), split_heads(to_tiles(key_clip)), split_heads(to_tiles(value_clip)), kept_tiles, kept_counts)
    outputs = lax.map(head_attention, packed)
    attended = from_tiles(outputs.transpose(1, 2, 0, 3).reshape(NT, TILE, HEADS * HD))
    latent = jnp.dot(attended.reshape(SEQ, HEADS * HD), patch_weight, preferred_element_type=jnp.float32).astype(jnp.bfloat16)
    return latent.reshape(FT, FH, FW, 4 * LAT)


def to_cells(latent):
    grid = latent.reshape(FT, FH, FW, 2, 2, LAT).transpose(0, 1, 3, 2, 4, 5)
    return grid.reshape(FT, 2 * FH, 2 * FW, LAT)


def convolve(cells, kernel):
    row_count = cells.shape[1]
    col_count = cells.shape[2]
    padded = jnp.pad(cells, ((2, 0), (1, 1), (1, 1), (0, 0)), mode='edge')
    total = jnp.zeros((FT * row_count * col_count, kernel.shape[2]), jnp.float32)
    for offset_time in range(3):
        for offset_row in range(3):
            for offset_col in range(3):
                window = padded[offset_time:offset_time + FT, offset_row:offset_row + row_count, offset_col:offset_col + col_count]
                total = total + jnp.dot(window.reshape(-1, cells.shape[3]), kernel[(offset_time * 3 + offset_row) * 3 + offset_col], preferred_element_type=jnp.float32)
    return total.reshape(FT, row_count, col_count, kernel.shape[2])


def decode_clip(latent, first_kernel, second_kernel):
    cells = to_cells(latent)
    first = (convolve(cells, first_kernel) * VAE_SCALE).astype(jnp.bfloat16)
    act = jax.nn.silu(first.astype(jnp.float32)).astype(jnp.bfloat16)
    return (first.astype(jnp.float32) + convolve(act, second_kernel)).astype(jnp.bfloat16)


def reference(queries, key_states, value_states, kept_tiles, kept_counts, patch_weight, decode_slot, first_kernel, second_kernel):
    def flatten(block):
        return block.reshape(MICRO * CLIPS, FT, FH, FW, HEADS * HD)

    def one_clip(packed):
        return clip_latent(packed[0], packed[1], packed[2], kept_tiles, kept_counts, patch_weight)

    latents = lax.map(one_clip, (flatten(queries), flatten(key_states), flatten(value_states)))
    latents = latents.reshape(MICRO, CLIPS, FT, FH, FW, 4 * LAT)
    match = (decode_slot[:, None] == jnp.arange(MICRO, dtype=jnp.int32)[None, :]).astype(jnp.int32)
    source = jnp.sum(jnp.arange(MICRO, dtype=jnp.int32)[:, None] * match, axis=0).astype(jnp.int32)
    moved = latents[source].reshape(MICRO * CLIPS, FT, FH, FW, 4 * LAT)

    def one_decode(latent):
        return decode_clip(latent, first_kernel, second_kernel)

    decoded = lax.map(one_decode, moved)
    return decoded.reshape(MICRO, CLIPS, FT, 2 * FH, 2 * FW, CH)
```

```python
import functools

import jax
import jax.numpy as jnp
from jax import lax
from jax.experimental import pallas as pl
from jax.experimental.pallas import tpu as pltpu
from jax.sharding import PartitionSpec as P

HEADS = 16
HD = 128
LAT = 16
CH = 256
TT = 4
TH = 8
TW = 8

VAE_SCALE = 1.0 / 0.476986
SCORE_UNIT = HD**-0.5 * 1.4426950408889634
HEAD_BLOCK = 4
NARROW = 4 * LAT
MIB = 1 << 20


def partial_head(head, q, k, v, tiles_ref, counts_ref):
    keys, queries = k.shape[0], q.shape[0]
    tile_count = tiles_ref.shape[1]
    keep = tiles_ref.shape[2]
    scores = lax.dot_general(k, q, (((1,), (1,)), ((), ())), preferred_element_type=jnp.float32)
    lane = lax.broadcasted_iota(jnp.int32, (1, queries), 1)
    lane_tile = lax.rem(lax.div(lane, TW), tile_count)
    rows = []
    for key_tile in range(tile_count):
        row = jnp.zeros((1, queries), jnp.float32)
        for query_tile in range(tile_count):
            live = jnp.bool_(False)
            for slot in range(keep):
                here = jnp.logical_and(
                    tiles_ref[head, query_tile, slot] == key_tile, slot < counts_ref[head, query_tile]
                )
                live = jnp.logical_or(live, here)
            row = jnp.where(lane_tile == query_tile, jnp.where(live, 0.0, -1e30), row)
        rows.append(row[None])
    bias = jnp.concatenate(rows, axis=0)
    scores = scores.reshape(keys // (tile_count * TW), tile_count, TW, queries) + bias[None]
    scores = scores.reshape(keys, queries)
    top = jnp.max(scores, axis=0, keepdims=True)
    power = jnp.exp2((scores - top) * SCORE_UNIT)
    total = jnp.sum(power, axis=0, keepdims=True)
    out = lax.dot_general(
        v, power.astype(jnp.bfloat16), (((0,), (0,)), ((), ())), preferred_element_type=jnp.float32
    )
    return top * SCORE_UNIT, total, out


def own_kernel(tiles_ref, counts_ref, q_ref, k_ref, v_ref, w_ref, level_ref, mapped_ref):
    block = pl.program_id(0)
    for i in range(HEAD_BLOCK):
        cols = slice(i * HD, (i + 1) * HD)
        head = block * HEAD_BLOCK + i
        top, total, out = partial_head(
            head, q_ref[:, cols], k_ref[:, cols], v_ref[:, cols], tiles_ref, counts_ref
        )
        out = (out / total).astype(jnp.bfloat16)
        level_ref[pl.ds(head, 1), :] = top + jnp.log2(total)
        mapped_ref[i] = lax.dot_general(
            w_ref[cols, :], out, (((0,), (0,)), ((), ())), preferred_element_type=jnp.float32
        )


def other_kernel(tiles_ref, counts_ref, q_ref, k_ref, v_ref, w_ref, level_ref, sent_ref):
    block = pl.program_id(0)
    mapped = jnp.zeros((NARROW, q_ref.shape[0]), jnp.float32)
    for i in range(HEAD_BLOCK):
        cols = slice(i * HD, (i + 1) * HD)
        head = block * HEAD_BLOCK + i
        top, total, out = partial_head(
            head, q_ref[:, cols], k_ref[:, cols], v_ref[:, cols], tiles_ref, counts_ref
        )
        theirs = level_ref[pl.ds(head, 1), :]
        mine = top + jnp.log2(total)
        high = jnp.maximum(mine, theirs)
        level = high + jnp.log2(jnp.exp2(mine - high) + jnp.exp2(theirs - high))
        out = (out * jnp.exp2(top - level)).astype(jnp.bfloat16)
        sent_ref[pl.ds(NARROW + head, 1), :] = jnp.exp2(theirs - level)
        mapped = mapped + lax.dot_general(
            w_ref[cols, :], out, (((0,), (0,)), ((), ())), preferred_element_type=jnp.float32
        )

    @pl.when(block == 0)
    def _():
        sent_ref[0:NARROW, :] = mapped

    @pl.when(block > 0)
    def _():
        sent_ref[0:NARROW, :] = sent_ref[0:NARROW, :] + mapped


def merge_kernel(got_ref, mapped_ref, out_ref):
    total = got_ref[0:NARROW, :]
    for head in range(HEADS):
        total = total + mapped_ref[head] * got_ref[NARROW + head : NARROW + head + 1, :]
    twice = jnp.concatenate([total, total], axis=0)
    out_ref[...] = twice.T.astype(jnp.bfloat16)


def split_attention(flat_query, flat_key, flat_value, kept_tiles, kept_counts, patch_weight):
    tokens = flat_query.shape[0]
    other_query = lax.ppermute(flat_query, "sp", [(0, 1), (1, 0)])
    smem = pl.BlockSpec(memory_space=pltpu.SMEM)
    heads = pl.BlockSpec((tokens, HEAD_BLOCK * HD), lambda i: (0, i))
    weight = pl.BlockSpec((HEAD_BLOCK * HD, NARROW), lambda i: (i, 0))

    def whole(*shape):
        return pl.BlockSpec(shape, lambda i: (0,) * len(shape))

    params = pltpu.CompilerParams(
        dimension_semantics=("arbitrary",), vmem_limit_bytes=32 * MIB
    )
    cost = pl.CostEstimate(
        flops=4 * HEADS * tokens * tokens * HD,
        bytes_accessed=3 * tokens * HEADS * HD * 2,
        transcendentals=HEADS * tokens * tokens,
    )
    level, mapped = pl.pallas_call(
        own_kernel,
        grid=(HEADS // HEAD_BLOCK,),
        in_specs=[smem, smem, heads, heads, heads, weight],
        out_specs=[
            whole(HEADS, tokens),
            pl.BlockSpec((HEAD_BLOCK, NARROW, tokens), lambda i: (i, 0, 0)),
        ],
        out_shape=[
            jax.ShapeDtypeStruct((HEADS, tokens), jnp.float32),
            jax.ShapeDtypeStruct((HEADS, NARROW, tokens), jnp.float32),
        ],
        compiler_params=params,
        cost_estimate=cost,
        name="own_keys",
    )(kept_tiles, kept_counts, flat_query, flat_key, flat_value, patch_weight)
    other_level = lax.ppermute(level, "sp", [(0, 1), (1, 0)])
    sent = pl.pallas_call(
        other_kernel,
        grid=(HEADS // HEAD_BLOCK,),
        in_specs=[smem, smem, heads, heads, heads, weight, whole(HEADS, tokens)],
        out_specs=whole(NARROW + HEADS, tokens),
        out_shape=jax.ShapeDtypeStruct((NARROW + HEADS, tokens), jnp.float32),
        compiler_params=params,
        cost_estimate=cost,
        name="other_queries",
    )(kept_tiles, kept_counts, other_query, flat_key, flat_value, patch_weight, other_level)
    got = lax.ppermute(sent, "sp", [(0, 1), (1, 0)])
    return pl.pallas_call(
        merge_kernel,
        out_shape=jax.ShapeDtypeStruct((tokens, 2 * NARROW), jnp.bfloat16),
        name="merge",
    )(got, mapped)


def to_tiles(grid, tile_size):
    frame_count, row_count, col_count, feature_width = grid.shape
    tiled = grid.reshape(
        frame_count // TT, TT, row_count // TH, TH, col_count // TW, TW, feature_width
    ).transpose(0, 2, 4, 1, 3, 5, 6)
    return tiled.reshape(-1, tile_size, feature_width)


def from_tiles(tiles, frame_count, row_count, col_count):
    feature_width = tiles.shape[-1]
    grid = tiles.reshape(
        frame_count // TT, row_count // TH, col_count // TW, TT, TH, TW, feature_width
    ).transpose(0, 3, 1, 4, 2, 5, 6)
    return grid.reshape(frame_count, row_count, col_count, feature_width)


def attend_tiles(query_tiles, key_tiles, value_tiles, tile_index, live_count):
    head_count = query_tiles.shape[0]
    tile_size = query_tiles.shape[2]
    head_size = query_tiles.shape[3]
    keep_count = tile_index.shape[2]

    def one_tile(packed):
        query_block, index_block, count_block = packed
        key_sel = jax.vmap(lambda source, picks: source[picks])(key_tiles, index_block).reshape(
            head_count, keep_count * tile_size, head_size
        )
        value_sel = jax.vmap(lambda source, picks: source[picks])(value_tiles, index_block).reshape(
            head_count, keep_count * tile_size, head_size
        )
        scores = jnp.einsum(
            "hqd,hkd->hqk", query_block, key_sel, preferred_element_type=jnp.float32
        ) * head_size ** (-0.5)
        live = jnp.arange(keep_count, dtype=jnp.int32)[None, :] < count_block[:, None]
        live = jnp.repeat(live, tile_size, axis=1)[:, None, :]
        scores = jnp.where(live, scores, -1e30)
        row_top = jnp.max(scores, axis=-1, keepdims=True)
        exponent = jnp.where(live, jnp.exp(scores - row_top), 0.0)
        weights = (exponent / jnp.sum(exponent, axis=-1, keepdims=True)).astype(jnp.bfloat16)
        result = jnp.einsum("hqk,hkd->hqd", weights, value_sel, preferred_element_type=jnp.float32)
        return result.astype(jnp.bfloat16)

    return lax.map(
        one_tile,
        (
            query_tiles.transpose(1, 0, 2, 3),
            tile_index.transpose(1, 0, 2),
            live_count.transpose(1, 0),
        ),
    )


def exchanged_attention(queries, key_states, value_states, kept_tiles, kept_counts, patch_weight):
    frame_count, local_rows, token_cols, feature_count = queries.shape[2:]
    tokens = frame_count * local_rows * token_cols
    sp_count = lax.axis_size("sp")
    sp_rank = lax.axis_index("sp")
    local_heads = HEADS // sp_count
    clip_rows = local_rows * sp_count
    tile_size = TT * TH * TW
    mixed_query, mixed_key, mixed_value = (
        lax.all_to_all(part.reshape(tokens, feature_count), "sp", split_axis=1, concat_axis=0, tiled=True)
        for part in (queries, key_states, value_states)
    )
    own_width = mixed_query.shape[1]

    def head_tiles(mixed):
        grid = mixed.reshape(sp_count, frame_count, local_rows, token_cols, own_width).transpose(
            1, 0, 2, 3, 4
        )
        tiles = to_tiles(grid.reshape(frame_count, clip_rows, token_cols, own_width), tile_size)
        return tiles.reshape(tiles.shape[0], tile_size, local_heads, HD).transpose(2, 0, 1, 3)

    outputs = attend_tiles(
        head_tiles(mixed_query),
        head_tiles(mixed_key),
        head_tiles(mixed_value),
        lax.dynamic_slice_in_dim(kept_tiles, sp_rank * local_heads, local_heads, 0),
        lax.dynamic_slice_in_dim(kept_counts, sp_rank * local_heads, local_heads, 0),
    )
    tile_count = outputs.shape[0]
    attended = from_tiles(
        outputs.transpose(0, 2, 1, 3).reshape(tile_count, tile_size, own_width),
        frame_count,
        clip_rows,
        token_cols,
    )
    attended = attended.reshape(frame_count, sp_count, local_rows, token_cols, own_width).transpose(
        1, 0, 2, 3, 4
    )
    attended = attended.reshape(sp_count * tokens, own_width)
    restored = lax.all_to_all(attended, "sp", split_axis=0, concat_axis=1, tiled=True)
    latent = jnp.dot(restored, patch_weight, preferred_element_type=jnp.float32)
    latent = latent.astype(jnp.bfloat16)
    return jnp.concatenate([latent, latent], axis=1)


def first_weights(first_kernel):
    plain = first_kernel.reshape(3, 3, 3, LAT, CH)
    both_rows = jnp.stack(
        [jnp.pad(plain, ((0, 0), (r, 1 - r), (0, 0), (0, 0), (0, 0))) for r in range(2)], axis=4
    )
    matrices = []
    for c in range(2):
        wide = jnp.pad(both_rows, ((0, 0), (0, 0), (c, 1 - c), (0, 0), (0, 0), (0, 0)))
        wide = wide.reshape(3, 2, 2, 2, 2, LAT, 2, CH).transpose(0, 1, 3, 2, 4, 5, 6, 7)
        matrices.append(wide.reshape(3 * 2 * 2 * NARROW, 2 * CH))
    return matrices


def decode_kernel(
    frames,
    rows,
    cols,
    place_ref,
    latent_ref,
    left_ref,
    right_ref,
    mine_ref,
    theirs_ref,
    out_ref,
    token_ref,
    pair_ref,
    first_ref,
    act_ref,
    wide_ref,
    kernel_ref,
    sems,
):
    rank = place_ref[1]
    ranks = place_ref[2]
    half = place_ref[3]
    copies = [
        pltpu.make_async_copy(mine_ref, kernel_ref.at[half], sems.at[0]),
        pltpu.make_async_copy(theirs_ref, kernel_ref.at[1 - half], sems.at[1]),
    ]
    for copy in copies:
        copy.start()
    at_first = rank == 0
    at_last = rank == ranks - 1

    for f in range(frames):
        for r in range(rows):
            token_ref[f, 1 + r, 8 : 8 + cols, :] = latent_ref[0, rank, f, r].astype(jnp.float32)
        above = latent_ref[0, jnp.maximum(rank - 1, 0), f, rows - 1].astype(jnp.float32)
        edge = pltpu.roll(token_ref[f, 1, 8 : 8 + cols, :], 2 * LAT, 1)
        token_ref[f, 0, 8 : 8 + cols, :] = jnp.where(at_first, edge, above)
        below = latent_ref[0, jnp.minimum(rank + 1, ranks - 1), f, 0].astype(jnp.float32)
        edge = pltpu.roll(token_ref[f, rows, 8 : 8 + cols, :], 2 * NARROW - 2 * LAT, 1)
        token_ref[f, rows + 1, 8 : 8 + cols, :] = jnp.where(at_last, edge, below)
    for f in range(frames):
        for r in range(rows + 2):
            start = token_ref[f, r, 8:16, :]
            token_ref[f, r, 7:8, :] = pltpu.roll(start, LAT, 1)[0:1]
            end = token_ref[f, r, cols : 8 + cols, :]
            token_ref[f, r, 8 + cols : 9 + cols, :] = pltpu.roll(end, 2 * NARROW - LAT, 1)[7:8]

    lane = lax.broadcasted_iota(jnp.int32, (1, 1, cols, 2 * NARROW), 3)
    for side in range(2):
        pair = jnp.where(
            lane < NARROW,
            token_ref[:, :, 7 + side : 7 + side + cols, :],
            token_ref[:, :, 8 + side : 8 + side + cols, :],
        ).astype(jnp.bfloat16)
        pair_ref[side, 2:] = pair
        pair_ref[side, 0] = pair[0]
        pair_ref[side, 1] = pair[0]

    gaps = rows + 1
    for side, weight_ref in ((0, left_ref), (1, right_ref)):
        columns = jnp.concatenate(
            [
                pair_ref[side, dt : dt + frames, rr : rr + gaps].reshape(frames * gaps * cols, 2 * NARROW)
                for dt in range(3)
                for rr in range(2)
            ],
            axis=1,
        )
        first = jnp.dot(columns, weight_ref[...], preferred_element_type=jnp.float32) * VAE_SCALE
        first = first.astype(jnp.bfloat16).astype(jnp.float32)
        act = first / (1.0 + jnp.exp(-first))
        first = first.reshape(frames, gaps, cols, 2 * CH)
        act = act.reshape(frames, gaps, cols, 2 * CH)
        for f in range(frames):
            for g in range(gaps):
                for ro in range(2):
                    for part in range(CH // 128):
                        lanes = slice(ro * CH + part * 128, ro * CH + part * 128 + 128)
                        row = 2 * g + ro
                        into = pl.ds(8 + side, cols, stride=2)
                        first_ref[part, f, row, into, :] = first[f, g, :, lanes]
                        act_ref[part, f, row, into, :] = act[f, g, :, lanes]

    width = 2 * cols
    height = 2 * rows
    for part in range(CH // 128):
        for f in range(frames):
            act_ref[part, f, 0] = jnp.where(at_first, act_ref[part, f, 1], act_ref[part, f, 0])
            act_ref[part, f, height + 1] = jnp.where(
                at_last, act_ref[part, f, height], act_ref[part, f, height + 1]
            )
        act_ref[part, :, :, 7:8, :] = act_ref[part, :, :, 8:9, :]
        act_ref[part, :, :, 8 + width : 9 + width, :] = act_ref[part, :, :, 7 + width : 8 + width, :]
        for dz in range(3):
            lanes = slice(dz * CH + part * 128, dz * CH + part * 128 + 128)
            shifted = act_ref[part, :, :, 7 + dz : 7 + dz + width, :].astype(jnp.bfloat16)
            wide_ref[2:, :, :, lanes] = shifted
            wide_ref[0, :, :, lanes] = shifted[0]
            wide_ref[1, :, :, lanes] = shifted[0]

    for copy in copies:
        copy.wait()
    cells = frames * height * width
    total = None
    for dt in range(3):
        for dy in range(3):
            window = wide_ref[dt : dt + frames, dy : dy + height].reshape(cells, 3 * CH)
            weight = jnp.concatenate(
                [
                    jnp.concatenate(
                        [kernel_ref[side, :, (dt * 3 + dy) * 3 + dz].reshape(CH, CH // 2) for side in range(2)],
                        axis=1,
                    )
                    for dz in range(3)
                ],
                axis=0,
            )
            product = jnp.dot(window, weight, preferred_element_type=jnp.float32)
            total = product if total is None else total + product
    total = total.reshape(frames, height, width, CH)
    for part in range(CH // 128):
        lanes = slice(part * 128, part * 128 + 128)
        residual = first_ref[part, :, 1 : 1 + height, 8 : 8 + width, :]
        out_ref[:, :, :, lanes] = (total[:, :, :, lanes] + residual).astype(jnp.bfloat16)


def decode(place, gathered, left, right, mine, theirs):
    _, ranks, frames, rows, cols, _ = gathered.shape
    height, width = 2 * rows, 2 * cols

    def whole(shape):
        return pl.BlockSpec(shape, lambda i, place: (0,) * len(shape))

    grid_spec = pltpu.PrefetchScalarGridSpec(
        num_scalar_prefetch=1,
        grid=(1,),
        in_specs=[
            pl.BlockSpec((1,) + gathered.shape[1:], lambda i, place: (place[0], 0, 0, 0, 0, 0)),
            whole(left.shape),
            whole(right.shape),
            pl.BlockSpec(memory_space=pl.ANY),
            pl.BlockSpec(memory_space=pl.ANY),
        ],
        out_specs=whole((frames, height, width, CH)),
        scratch_shapes=[
            pltpu.VMEM((frames, rows + 2, cols + 16, 2 * NARROW), jnp.float32),
            pltpu.VMEM((2, frames + 2, rows + 2, cols, 2 * NARROW), jnp.bfloat16),
            pltpu.VMEM((CH // 128, frames, height + 2, width + 16, 128), jnp.float32),
            pltpu.VMEM((CH // 128, frames, height + 2, width + 16, 128), jnp.float32),
            pltpu.VMEM((frames + 2, height + 2, width, 3 * CH), jnp.bfloat16),
            pltpu.VMEM((2,) + mine.shape, jnp.bfloat16),
            pltpu.SemaphoreType.DMA((2,)),
        ],
    )
    return pl.pallas_call(
        functools.partial(decode_kernel, frames, rows, cols),
        grid_spec=grid_spec,
        out_shape=jax.ShapeDtypeStruct((frames, height, width, CH), jnp.bfloat16),
        compiler_params=pltpu.CompilerParams(vmem_limit_bytes=48 * MIB),
        cost_estimate=pl.CostEstimate(
            flops=2 * frames * height * width * 27 * CH * CH,
            bytes_accessed=27 * CH * CH * 2 + frames * height * width * CH * 2,
            transcendentals=frames * height * width * CH,
        ),
        name="decode_block",
    )(place, gathered, left, right, mine, theirs)


def local(
    queries,
    key_states,
    value_states,
    kept_tiles,
    kept_counts,
    patch_weight,
    decode_slot,
    first_kernel,
    second_kernel,
):
    frames, rows, cols, feature_count = queries.shape[2:]
    tokens = frames * rows * cols
    sp_count = lax.axis_size("sp")
    sp_rank = lax.axis_index("sp")
    segment_count = lax.axis_size("segment")
    segment_rank = lax.axis_index("segment")

    half = lax.rem(segment_rank, 2)
    share = lax.dynamic_slice_in_dim(second_kernel, half * (CH // 2), CH // 2, 2)
    mine = lax.all_gather(share, "grp", axis=0, tiled=False)
    theirs = lax.ppermute(mine, "segment", [(i, i ^ 1) for i in range(segment_count)])
    left, right = first_weights(first_kernel)[::-1]

    if sp_count == 2 and rows * sp_count == TH and frames == TT:
        latent = split_attention(
            queries.reshape(tokens, feature_count),
            key_states.reshape(tokens, feature_count),
            value_states.reshape(tokens, feature_count),
            kept_tiles,
            kept_counts,
            patch_weight,
        )
    else:
        latent = exchanged_attention(
            queries, key_states, value_states, kept_tiles, kept_counts, patch_weight
        )

    gathered = lax.all_gather(latent, ("segment", "sp"), axis=0, tiled=False)
    gathered = gathered.reshape(segment_count, sp_count, frames, rows, cols, 2 * NARROW)
    picks = (decode_slot == segment_rank).astype(jnp.int32)
    source = jnp.sum(jnp.arange(segment_count, dtype=jnp.int32) * picks)
    place = jnp.stack([source, sp_rank, jnp.int32(sp_count), half]).astype(jnp.int32)
    return decode(place, gathered, left, right, mine, theirs)[None, None]


def solution(mesh):
    return jax.shard_map(
        local,
        mesh=mesh,
        in_specs=(
            P("segment", "grp", None, "sp", None, None),
            P("segment", "grp", None, "sp", None, None),
            P("segment", "grp", None, "sp", None, None),
            P(),
            P(),
            P(),
            P(),
            P(),
            P(None, "grp", None),
        ),
        out_specs=P("segment", "grp", None, "sp", None, None),
        check_vma=False,
    )
```

```python
import functools

import jax
import jax.numpy as jnp
from jax import lax
from jax.experimental import pallas as pl
from jax.experimental.pallas import tpu as pltpu
from jax.sharding import PartitionSpec as P

HEADS = 16
HD = 128
LAT = 16
CH = 256
TT = 4
TH = 8
TW = 8

VAE_SCALE = 1.0 / 0.476986
SCORE_UNIT = HD**-0.5 * 1.4426950408889634
HEAD_BLOCK = 4
NARROW = 4 * LAT
MIB = 1 << 20


def partial_head(head, q, k, v, tiles_ref, counts_ref):
    keys, queries = k.shape[0], q.shape[0]
    tile_count, keep = tiles_ref.shape[:2]
    scores = lax.dot_general(k, q, (((1,), (1,)), ((), ())), preferred_element_type=jnp.float32)
    lane = lax.broadcasted_iota(jnp.int32, (1, queries), 1)
    lane_tile = lax.rem(lax.div(lane, TW), tile_count)
    rows = []
    for key_tile in range(tile_count):
        row = jnp.zeros((1, queries), jnp.float32)
        for query_tile in range(tile_count):
            live = jnp.bool_(False)
            for slot in range(keep):
                here = jnp.logical_and(
                    tiles_ref[query_tile, slot, head] == key_tile, slot < counts_ref[query_tile, head]
                )
                live = jnp.logical_or(live, here)
            row = jnp.where(lane_tile == query_tile, jnp.where(live, 0.0, -1e30), row)
        rows.append(row[None])
    bias = jnp.concatenate(rows, axis=0)
    scores = scores.reshape(keys // (tile_count * TW), tile_count, TW, queries) + bias[None]
    scores = scores.reshape(keys, queries)
    top = jnp.max(scores, axis=0, keepdims=True)
    power = jnp.exp2((scores - top) * SCORE_UNIT)
    total = jnp.sum(power, axis=0, keepdims=True)
    out = lax.dot_general(
        v, power.astype(jnp.bfloat16), (((0,), (0,)), ((), ())), preferred_element_type=jnp.float32
    )
    return top * SCORE_UNIT, total, out


def own_kernel(tiles_ref, counts_ref, q_ref, k_ref, v_ref, w_ref, level_ref, mapped_ref):
    block = pl.program_id(0)
    for i in range(HEAD_BLOCK):
        cols = slice(i * HD, (i + 1) * HD)
        head = block * HEAD_BLOCK + i
        top, total, out = partial_head(
            head, q_ref[:, cols], k_ref[:, cols], v_ref[:, cols], tiles_ref, counts_ref
        )
        out = (out / total).astype(jnp.bfloat16)
        level_ref[pl.ds(head, 1), :] = top + jnp.log2(total)
        mapped_ref[i] = lax.dot_general(
            w_ref[:, cols], out, (((1,), (0,)), ((), ())), preferred_element_type=jnp.float32
        )


def other_kernel(tiles_ref, counts_ref, q_ref, k_ref, v_ref, w_ref, level_ref, sent_ref):
    block = pl.program_id(0)
    mapped = jnp.zeros((NARROW, q_ref.shape[0]), jnp.float32)
    for i in range(HEAD_BLOCK):
        cols = slice(i * HD, (i + 1) * HD)
        head = block * HEAD_BLOCK + i
        top, total, out = partial_head(
            head, q_ref[:, cols], k_ref[:, cols], v_ref[:, cols], tiles_ref, counts_ref
        )
        theirs = level_ref[pl.ds(head, 1), :]
        mine = top + jnp.log2(total)
        high = jnp.maximum(mine, theirs)
        level = high + jnp.log2(jnp.exp2(mine - high) + jnp.exp2(theirs - high))
        out = (out * jnp.exp2(top - level)).astype(jnp.bfloat16)
        sent_ref[pl.ds(NARROW + head, 1), :] = jnp.exp2(theirs - level)
        mapped = mapped + lax.dot_general(
            w_ref[:, cols], out, (((1,), (0,)), ((), ())), preferred_element_type=jnp.float32
        )

    @pl.when(block == 0)
    def _():
        sent_ref[0:NARROW, :] = mapped

    @pl.when(block > 0)
    def _():
        sent_ref[0:NARROW, :] = sent_ref[0:NARROW, :] + mapped


def merge_kernel(frames, rows, cols, rank_ref, got_ref, mapped_ref, out_ref, rim_ref):
    total = got_ref[0:NARROW, :]
    for head in range(HEADS):
        total = total + mapped_ref[head] * got_ref[NARROW + head : NARROW + head + 1, :]
    half = total.shape[1] // 2
    packed = jnp.concatenate([total[:, :half], total[:, half:]], axis=0).T
    out_ref[...] = packed.astype(jnp.bfloat16)
    grid = packed.reshape(frames // 2, rows, cols, 2 * NARROW)
    rim = jnp.where(rank_ref[0] == 0, grid[:, rows - 1], grid[:, 0])
    rim_ref[...] = rim.reshape(-1, 2 * NARROW).astype(jnp.bfloat16)


def split_attention(queries, key_states, value_states, kept_tiles, kept_counts, patch_weight, ready):
    frames, rows, cols, feature_count = queries.shape[2:]
    tokens = frames * rows * cols
    flat_query = queries.reshape(tokens, feature_count)
    flat_key = key_states.reshape(tokens, feature_count)
    flat_value = value_states.reshape(tokens, feature_count)
    other_query = lax.ppermute(flat_query, "sp", [(0, 1), (1, 0)])
    kept_tiles = kept_tiles.transpose(1, 2, 0)
    kept_counts = kept_counts.T
    patch_weight = patch_weight.T
    smem = pl.BlockSpec(memory_space=pltpu.SMEM)
    heads = pl.BlockSpec((tokens, HEAD_BLOCK * HD), lambda i: (0, i))
    weight = pl.BlockSpec((NARROW, HEAD_BLOCK * HD), lambda i: (0, i))

    def whole(*shape):
        return pl.BlockSpec(shape, lambda i: (0,) * len(shape))

    params = pltpu.CompilerParams(
        dimension_semantics=("arbitrary",), vmem_limit_bytes=24 * MIB
    )
    cost = pl.CostEstimate(
        flops=4 * HEADS * tokens * tokens * HD,
        bytes_accessed=3 * tokens * HEADS * HD * 2,
        transcendentals=HEADS * tokens * tokens,
    )
    level, mapped = pl.pallas_call(
        own_kernel,
        grid=(HEADS // HEAD_BLOCK,),
        in_specs=[smem, smem, heads, heads, heads, weight],
        out_specs=[
            whole(HEADS, tokens),
            pl.BlockSpec((HEAD_BLOCK, NARROW, tokens), lambda i: (i, 0, 0)),
        ],
        out_shape=[
            jax.ShapeDtypeStruct((HEADS, tokens), jnp.float32),
            jax.ShapeDtypeStruct((HEADS, NARROW, tokens), jnp.float32),
        ],
        compiler_params=params,
        cost_estimate=cost,
        name="own_keys",
    )(kept_tiles, kept_counts, flat_query, flat_key, flat_value, patch_weight)
    level, ready = lax.optimization_barrier((level, ready))
    other_level = lax.ppermute(level, "sp", [(0, 1), (1, 0)])
    sent = pl.pallas_call(
        other_kernel,
        grid=(HEADS // HEAD_BLOCK,),
        in_specs=[smem, smem, heads, heads, heads, weight, whole(HEADS, tokens)],
        out_specs=whole(NARROW + HEADS, tokens),
        out_shape=jax.ShapeDtypeStruct((NARROW + HEADS, tokens), jnp.float32),
        compiler_params=params,
        cost_estimate=cost,
        name="other_queries",
    )(kept_tiles, kept_counts, other_query, flat_key, flat_value, patch_weight, other_level)
    got = lax.ppermute(sent, "sp", [(0, 1), (1, 0)])
    rank = lax.axis_index("sp").astype(jnp.int32).reshape(1)
    rim_tokens = frames // 2 * cols
    latent, rim = pl.pallas_call(
        functools.partial(merge_kernel, frames, rows, cols),
        grid=(1,),
        in_specs=[smem, whole(NARROW + HEADS, tokens), whole(HEADS, NARROW, tokens)],
        out_specs=[whole(tokens // 2, 2 * NARROW), whole(rim_tokens, 2 * NARROW)],
        out_shape=[
            jax.ShapeDtypeStruct((tokens // 2, 2 * NARROW), jnp.bfloat16),
            jax.ShapeDtypeStruct((rim_tokens, 2 * NARROW), jnp.bfloat16),
        ],
        compiler_params=params,
        name="merge",
    )(rank, got, mapped)
    return latent, rim, ready


def to_tiles(grid, tile_size):
    frame_count, row_count, col_count, feature_width = grid.shape
    tiled = grid.reshape(
        frame_count // TT, TT, row_count // TH, TH, col_count // TW, TW, feature_width
    ).transpose(0, 2, 4, 1, 3, 5, 6)
    return tiled.reshape(-1, tile_size, feature_width)


def from_tiles(tiles, frame_count, row_count, col_count):
    feature_width = tiles.shape[-1]
    grid = tiles.reshape(
        frame_count // TT, row_count // TH, col_count // TW, TT, TH, TW, feature_width
    ).transpose(0, 3, 1, 4, 2, 5, 6)
    return grid.reshape(frame_count, row_count, col_count, feature_width)


def attend_tiles(query_tiles, key_tiles, value_tiles, tile_index, live_count):
    head_count = query_tiles.shape[0]
    tile_size = query_tiles.shape[2]
    head_size = query_tiles.shape[3]
    keep_count = tile_index.shape[2]

    def one_tile(packed):
        query_block, index_block, count_block = packed
        key_sel = jax.vmap(lambda source, picks: source[picks])(key_tiles, index_block).reshape(
            head_count, keep_count * tile_size, head_size
        )
        value_sel = jax.vmap(lambda source, picks: source[picks])(value_tiles, index_block).reshape(
            head_count, keep_count * tile_size, head_size
        )
        scores = jnp.einsum(
            "hqd,hkd->hqk", query_block, key_sel, preferred_element_type=jnp.float32
        ) * head_size ** (-0.5)
        live = jnp.arange(keep_count, dtype=jnp.int32)[None, :] < count_block[:, None]
        live = jnp.repeat(live, tile_size, axis=1)[:, None, :]
        scores = jnp.where(live, scores, -1e30)
        row_top = jnp.max(scores, axis=-1, keepdims=True)
        exponent = jnp.where(live, jnp.exp(scores - row_top), 0.0)
        weights = (exponent / jnp.sum(exponent, axis=-1, keepdims=True)).astype(jnp.bfloat16)
        result = jnp.einsum("hqk,hkd->hqd", weights, value_sel, preferred_element_type=jnp.float32)
        return result.astype(jnp.bfloat16)

    return lax.map(
        one_tile,
        (
            query_tiles.transpose(1, 0, 2, 3),
            tile_index.transpose(1, 0, 2),
            live_count.transpose(1, 0),
        ),
    )


def exchanged_attention(queries, key_states, value_states, kept_tiles, kept_counts, patch_weight):
    frame_count, local_rows, token_cols, feature_count = queries.shape[2:]
    tokens = frame_count * local_rows * token_cols
    sp_count = lax.axis_size("sp")
    sp_rank = lax.axis_index("sp")
    local_heads = HEADS // sp_count
    clip_rows = local_rows * sp_count
    tile_size = TT * TH * TW
    mixed_query, mixed_key, mixed_value = (
        lax.all_to_all(part.reshape(tokens, feature_count), "sp", split_axis=1, concat_axis=0, tiled=True)
        for part in (queries, key_states, value_states)
    )
    own_width = mixed_query.shape[1]

    def head_tiles(mixed):
        grid = mixed.reshape(sp_count, frame_count, local_rows, token_cols, own_width).transpose(
            1, 0, 2, 3, 4
        )
        tiles = to_tiles(grid.reshape(frame_count, clip_rows, token_cols, own_width), tile_size)
        return tiles.reshape(tiles.shape[0], tile_size, local_heads, HD).transpose(2, 0, 1, 3)

    outputs = attend_tiles(
        head_tiles(mixed_query),
        head_tiles(mixed_key),
        head_tiles(mixed_value),
        lax.dynamic_slice_in_dim(kept_tiles, sp_rank * local_heads, local_heads, 0),
        lax.dynamic_slice_in_dim(kept_counts, sp_rank * local_heads, local_heads, 0),
    )
    tile_count = outputs.shape[0]
    attended = from_tiles(
        outputs.transpose(0, 2, 1, 3).reshape(tile_count, tile_size, own_width),
        frame_count,
        clip_rows,
        token_cols,
    )
    attended = attended.reshape(frame_count, sp_count, local_rows, token_cols, own_width).transpose(
        1, 0, 2, 3, 4
    )
    attended = attended.reshape(sp_count * tokens, own_width)
    restored = lax.all_to_all(attended, "sp", split_axis=0, concat_axis=1, tiled=True)
    latent = jnp.dot(restored, patch_weight, preferred_element_type=jnp.float32)
    latent = latent.astype(jnp.bfloat16)
    packed = jnp.concatenate([latent[: tokens // 2], latent[tokens // 2 :]], axis=1)
    grid = packed.reshape(frame_count // 2, local_rows, token_cols, 2 * NARROW)
    return packed, grid[:, 0].reshape(-1, 2 * NARROW), grid[:, -1].reshape(-1, 2 * NARROW)


def first_weights(first_kernel):
    plain = first_kernel.reshape(3, 3, 3, LAT, CH)
    both_rows = jnp.stack(
        [jnp.pad(plain, ((0, 0), (r, 1 - r), (0, 0), (0, 0), (0, 0))) for r in range(2)], axis=4
    )
    matrices = []
    for c in (1, 0):
        wide = jnp.pad(both_rows, ((0, 0), (0, 0), (c, 1 - c), (0, 0), (0, 0), (0, 0)))
        wide = wide.reshape(3, 2, 2, 2, 2, LAT, 2, CH).transpose(0, 1, 3, 2, 4, 5, 6, 7)
        matrices.append(wide.reshape(3 * 2 * 2 * NARROW, 2 * CH))
    return jnp.stack(matrices)


def decode_kernel(
    frames,
    rows,
    cols,
    place_ref,
    own_refs,
    above_refs,
    below_refs,
    weight_hbm,
    mine_ref,
    theirs_ref,
    out_ref,
    token_ref,
    pair_ref,
    first_ref,
    act_ref,
    wide_ref,
    weight_ref,
    kernel_ref,
    sems,
):
    step = place_ref[0]
    at_first = place_ref[1] == 0
    at_last = place_ref[1] == place_ref[2] - 1
    half = place_ref[3]
    copies = [
        pltpu.make_async_copy(weight_hbm, weight_ref, sems.at[0]),
        pltpu.make_async_copy(mine_ref, kernel_ref.at[half], sems.at[1]),
        pltpu.make_async_copy(theirs_ref, kernel_ref.at[1 - half], sems.at[2]),
    ]
    for copy in copies:
        copy.start()

    lane = lax.broadcasted_iota(jnp.int32, (1, 1, 1, 2 * NARROW), 3)

    def picked(refs, height):
        chosen = refs[0][...]
        for k in range(1, len(refs)):
            chosen = jnp.where(step == k, refs[k][...], chosen)
        chosen = chosen.astype(jnp.float32)
        turned = pltpu.roll(chosen, NARROW, 1)
        shape = (frames // 2, height, cols, 2 * NARROW)
        chosen, turned = chosen.reshape(shape), turned.reshape(shape)
        early = jnp.where(lane < NARROW, chosen, turned)
        late = jnp.where(lane < NARROW, turned, chosen)
        return jnp.concatenate([early, late], axis=0)

    token_ref[:, 1 : 1 + rows, 8 : 8 + cols, :] = picked(own_refs, rows)
    above = picked(above_refs, 1)
    below = above if below_refs is above_refs else picked(below_refs, 1)
    for f in range(frames):
        edge = pltpu.roll(token_ref[f, 1, 8 : 8 + cols, :], 2 * LAT, 1)
        token_ref[f, 0, 8 : 8 + cols, :] = jnp.where(at_first, edge, above[f, 0])
        edge = pltpu.roll(token_ref[f, rows, 8 : 8 + cols, :], 2 * NARROW - 2 * LAT, 1)
        token_ref[f, rows + 1, 8 : 8 + cols, :] = jnp.where(at_last, edge, below[f, 0])
    for f in range(frames):
        for r in range(rows + 2):
            start = token_ref[f, r, 8:16, :]
            token_ref[f, r, 7:8, :] = pltpu.roll(start, LAT, 1)[0:1]
            end = token_ref[f, r, cols : 8 + cols, :]
            token_ref[f, r, 8 + cols : 9 + cols, :] = pltpu.roll(end, 2 * NARROW - LAT, 1)[7:8]

    for side in range(2):
        pair = jnp.where(
            lane < NARROW,
            token_ref[:, :, 7 + side : 7 + side + cols, :],
            token_ref[:, :, 8 + side : 8 + side + cols, :],
        ).astype(jnp.bfloat16)
        pair_ref[side, 2:] = pair
        pair_ref[side, 0] = pair[0]
        pair_ref[side, 1] = pair[0]

    copies[0].wait()
    gaps = rows + 1
    for side in range(2):
        columns = jnp.concatenate(
            [
                pair_ref[side, dt : dt + frames, rr : rr + gaps].reshape(frames * gaps * cols, 2 * NARROW)
                for dt in range(3)
                for rr in range(2)
            ],
            axis=1,
        )
        first = jnp.dot(columns, weight_ref[side], preferred_element_type=jnp.float32) * VAE_SCALE
        first = first.astype(jnp.bfloat16).astype(jnp.float32)
        act = first / (1.0 + jnp.exp(-first))
        first = first.reshape(frames, gaps, cols, 2 * CH)
        act = act.reshape(frames, gaps, cols, 2 * CH)
        for f in range(frames):
            for g in range(gaps):
                for ro in range(2):
                    for part in range(CH // 128):
                        lanes = slice(ro * CH + part * 128, ro * CH + part * 128 + 128)
                        row = 2 * g + ro
                        into = pl.ds(8 + side, cols, stride=2)
                        first_ref[part, f, row, into, :] = first[f, g, :, lanes]
                        act_ref[part, f, row, into, :] = act[f, g, :, lanes]

    width = 2 * cols
    height = 2 * rows
    for part in range(CH // 128):
        for f in range(frames):
            act_ref[part, f, 0] = jnp.where(at_first, act_ref[part, f, 1], act_ref[part, f, 0])
            act_ref[part, f, height + 1] = jnp.where(
                at_last, act_ref[part, f, height], act_ref[part, f, height + 1]
            )
        act_ref[part, :, :, 7:8, :] = act_ref[part, :, :, 8:9, :]
        act_ref[part, :, :, 8 + width : 9 + width, :] = act_ref[part, :, :, 7 + width : 8 + width, :]
        for dz in range(3):
            lanes = slice(dz * CH + part * 128, dz * CH + part * 128 + 128)
            shifted = act_ref[part, :, :, 7 + dz : 7 + dz + width, :].astype(jnp.bfloat16)
            wide_ref[2:, :, :, lanes] = shifted
            wide_ref[0, :, :, lanes] = shifted[0]
            wide_ref[1, :, :, lanes] = shifted[0]

    for copy in copies[1:]:
        copy.wait()
    cells = frames * height * width
    total = None
    for dt in range(3):
        for dy in range(3):
            window = wide_ref[dt : dt + frames, dy : dy + height].reshape(cells, 3 * CH)
            weight = jnp.concatenate(
                [
                    jnp.concatenate(
                        [kernel_ref[side, :, (dt * 3 + dy) * 3 + dz].reshape(CH, CH // 2) for side in range(2)],
                        axis=1,
                    )
                    for dz in range(3)
                ],
                axis=0,
            )
            product = jnp.dot(window, weight, preferred_element_type=jnp.float32)
            total = product if total is None else total + product
    total = total.reshape(frames, height, width, CH)
    for part in range(CH // 128):
        lanes = slice(part * 128, part * 128 + 128)
        residual = first_ref[part, :, 1 : 1 + height, 8 : 8 + width, :]
        out_ref[:, :, :, lanes] = (total[:, :, :, lanes] + residual).astype(jnp.bfloat16)


def decode(frames, rows, cols, place, own, above, below, weights, mine, theirs):
    height, width = 2 * rows, 2 * cols
    steps = len(own)
    rims = [above] if below is above else [above, below]
    small = own + [part for rim in rims for part in rim]

    def whole(shape):
        return pl.BlockSpec(shape, lambda i, place: (0,) * len(shape))

    def body(place_ref, *refs):
        own_refs, above_refs = refs[:steps], refs[steps : 2 * steps]
        below_refs = above_refs if len(rims) == 1 else refs[2 * steps : 3 * steps]
        decode_kernel(
            frames, rows, cols, place_ref, own_refs, above_refs, below_refs, *refs[len(small) :]
        )

    grid_spec = pltpu.PrefetchScalarGridSpec(
        num_scalar_prefetch=1,
        grid=(1,),
        in_specs=[whole(part.shape) for part in small]
        + [pl.BlockSpec(memory_space=space) for space in (pl.ANY, pltpu.HBM, pl.ANY)],
        out_specs=whole((frames, height, width, CH)),
        scratch_shapes=[
            pltpu.VMEM((frames, rows + 2, cols + 16, 2 * NARROW), jnp.float32),
            pltpu.VMEM((2, frames + 2, rows + 2, cols, 2 * NARROW), jnp.bfloat16),
            pltpu.VMEM((CH // 128, frames, height + 2, width + 16, 128), jnp.float32),
            pltpu.VMEM((CH // 128, frames, height + 2, width + 16, 128), jnp.float32),
            pltpu.VMEM((frames + 2, height + 2, width, 3 * CH), jnp.bfloat16),
            pltpu.VMEM(weights.shape, jnp.bfloat16),
            pltpu.VMEM((2,) + mine.shape, jnp.bfloat16),
            pltpu.SemaphoreType.DMA((3,)),
        ],
    )
    return pl.pallas_call(
        body,
        grid_spec=grid_spec,
        out_shape=jax.ShapeDtypeStruct((frames, height, width, CH), jnp.bfloat16),
        compiler_params=pltpu.CompilerParams(vmem_limit_bytes=32 * MIB),
        cost_estimate=pl.CostEstimate(
            flops=2 * frames * height * width * 27 * CH * CH,
            bytes_accessed=27 * CH * CH * 2 + frames * height * width * CH * 2,
            transcendentals=frames * height * width * CH,
        ),
        name="decode_block",
    )(place, *small, weights, mine, theirs)


def local(
    queries,
    key_states,
    value_states,
    kept_tiles,
    kept_counts,
    patch_weight,
    decode_slot,
    first_kernel,
    second_kernel,
):
    frames, rows, cols = queries.shape[2:5]
    sp_count = lax.axis_size("sp")
    sp_rank = lax.axis_index("sp")
    segment_count = lax.axis_size("segment")
    segment_rank = lax.axis_index("segment")

    half = lax.rem(segment_rank, 2)
    share = lax.dynamic_slice_in_dim(second_kernel, half * (CH // 2), CH // 2, 2)
    mine = lax.all_gather(share, "grp", axis=0, tiled=False)

    weights = first_weights(first_kernel)
    picks = (decode_slot == segment_rank).astype(jnp.int32)
    source = jnp.sum(jnp.arange(segment_count, dtype=jnp.int32) * picks)
    step = lax.rem(segment_rank - source + segment_count, segment_count)
    place = jnp.stack([step, sp_rank, jnp.int32(sp_count), half]).astype(jnp.int32)

    arguments = (queries, key_states, value_states, kept_tiles, kept_counts, patch_weight)
    if sp_count == 2 and rows * sp_count == TH and frames == TT:
        latent, rim, (weights, place) = split_attention(*arguments, (weights, place))
        rims = [(rim, [(0, 1), (1, 0)])]
    else:
        latent, top, bottom = exchanged_attention(*arguments)
        rims = [
            (bottom, [(i, i + 1) for i in range(sp_count - 1)]),
            (top, [(i + 1, i) for i in range(sp_count - 1)]),
        ]
    mine, _ = lax.optimization_barrier((mine, latent))
    theirs = lax.ppermute(mine, "segment", [(i, i ^ 1) for i in range(segment_count)])

    def along_segment(part, step, moves):
        pairs = [
            (i * sp_count + a, (i + step) % segment_count * sp_count + b)
            for i in range(segment_count)
            for a, b in moves
        ]
        return lax.ppermute(part, ("segment", "sp"), pairs)

    stay = [(i, i) for i in range(sp_count)]
    own = [latent] + [along_segment(latent, step, stay) for step in range(1, segment_count)]
    beside = [[along_segment(rim, step, moves) for step in range(segment_count)] for rim, moves in rims]
    decoded = decode(frames, rows, cols, place, own, beside[0], beside[-1], weights, mine, theirs)
    return decoded[None, None]


def solution(mesh):
    return jax.shard_map(
        local,
        mesh=mesh,
        in_specs=(
            P("segment", "grp", None, "sp", None, None),
            P("segment", "grp", None, "sp", None, None),
            P("segment", "grp", None, "sp", None, None),
            P(),
            P(),
            P(),
            P(),
            P(),
            P(None, "grp", None),
        ),
        out_specs=P("segment", "grp", None, "sp", None, None),
        check_vma=False,
    )
```

```python
import functools
import itertools

import jax
import jax.numpy as jnp
from jax import lax
from jax.experimental import pallas as pl
from jax.experimental.pallas import tpu as pltpu
from jax.sharding import PartitionSpec as P

HEADS = 16
HD = 128
LAT = 16
CH = 256
TT = 4
TH = 8
TW = 8

VAE_SCALE = 1.0 / 0.476986
SCORE_UNIT = HD**-0.5 * 1.4426950408889634
HEAD_BLOCK = 4
HEAD_PARTS = (12, 4)
NARROW = 4 * LAT
MIB = 1 << 20


def partial_head(head, q, k, v, tiles_ref, counts_ref):
    keys, queries = k.shape[0], q.shape[0]
    tile_count, keep = tiles_ref.shape[:2]
    scores = lax.dot_general(k, q, (((1,), (1,)), ((), ())), preferred_element_type=jnp.float32)
    lane = lax.broadcasted_iota(jnp.int32, (1, queries), 1)
    lane_tile = lax.rem(lax.div(lane, TW), tile_count)
    rows = []
    for key_tile in range(tile_count):
        row = jnp.zeros((1, queries), jnp.float32)
        for query_tile in range(tile_count):
            live = jnp.bool_(False)
            for slot in range(keep):
                here = jnp.logical_and(
                    tiles_ref[query_tile, slot, head] == key_tile, slot < counts_ref[query_tile, head]
                )
                live = jnp.logical_or(live, here)
            row = jnp.where(lane_tile == query_tile, jnp.where(live, 0.0, -1e30), row)
        rows.append(row[None])
    bias = jnp.concatenate(rows, axis=0)
    scores = scores.reshape(keys // (tile_count * TW), tile_count, TW, queries) + bias[None]
    scores = scores.reshape(keys, queries)
    top = jnp.max(scores, axis=0, keepdims=True)
    power = jnp.exp2((scores - top) * SCORE_UNIT)
    total = jnp.sum(power, axis=0, keepdims=True)
    out = lax.dot_general(
        v, power.astype(jnp.bfloat16), (((0,), (0,)), ((), ())), preferred_element_type=jnp.float32
    )
    return top * SCORE_UNIT, total, out


def attend_kernel(offset, tiles_ref, counts_ref, q_ref, k_ref, v_ref, w_ref, level_ref, mapped_ref):
    block = pl.program_id(0)
    for i in range(HEAD_BLOCK):
        cols = slice(i * HD, (i + 1) * HD)
        row = block * HEAD_BLOCK + i
        top, total, out = partial_head(
            offset + row, q_ref[:, cols], k_ref[:, cols], v_ref[:, cols], tiles_ref, counts_ref
        )
        out = (out / total).astype(jnp.bfloat16)
        level_ref[pl.ds(row, 1), :] = top + jnp.log2(total)
        mapped_ref[i] = lax.dot_general(
            w_ref[:, cols], out, (((1,), (0,)), ((), ())), preferred_element_type=jnp.float32
        )


def combine_kernel(parts, theirs_ref, *refs):
    level_refs, mapped_refs, sent_ref = refs[:parts], refs[parts : 2 * parts], refs[-1]
    theirs = theirs_ref[...]
    mine = jnp.concatenate([ref[...] for ref in level_refs], axis=0)
    high = jnp.maximum(mine, theirs)
    level = high + jnp.log2(jnp.exp2(mine - high) + jnp.exp2(theirs - high))
    mine = jnp.exp2(mine - level)
    total = None
    head = 0
    for ref in mapped_refs:
        for i in range(ref.shape[0]):
            term = ref[i] * mine[head : head + 1]
            total = term if total is None else total + term
            head += 1
    sent_ref[0:NARROW, :] = total
    sent_ref[NARROW:, :] = jnp.exp2(theirs - level)


def merge_kernel(frames, rows, cols, rank_ref, got_ref, mapped_ref, out_ref, rim_ref):
    total = got_ref[0:NARROW, :]
    for head in range(HEADS):
        total = total + mapped_ref[head] * got_ref[NARROW + head : NARROW + head + 1, :]
    half = total.shape[1] // 2
    packed = jnp.concatenate([total[:, :half], total[:, half:]], axis=0).T
    out_ref[...] = packed.astype(jnp.bfloat16)
    grid = packed.reshape(frames // 2, rows, cols, 2 * NARROW)
    rim = jnp.where(rank_ref[0] == 0, grid[:, rows - 1], grid[:, 0])
    rim_ref[...] = rim.reshape(-1, 2 * NARROW).astype(jnp.bfloat16)


def split_attention(queries, key_states, value_states, kept_tiles, kept_counts, patch_weight, ready):
    frames, rows, cols, feature_count = queries.shape[2:]
    tokens = frames * rows * cols
    flat_query = queries.reshape(tokens, feature_count)
    flat_key = key_states.reshape(tokens, feature_count)
    flat_value = value_states.reshape(tokens, feature_count)
    swap = [(0, 1), (1, 0)]
    ends = list(itertools.accumulate(HEAD_PARTS))
    starts = [0] + ends[:-1]
    other_queries = [
        lax.ppermute(flat_query[:, start * HD : end * HD], "sp", swap) for start, end in zip(starts, ends)
    ]
    kept_tiles = kept_tiles.transpose(1, 2, 0)
    kept_counts = kept_counts.T
    patch_weight = patch_weight.T
    smem = pl.BlockSpec(memory_space=pltpu.SMEM)
    params = pltpu.CompilerParams(
        dimension_semantics=("arbitrary",), vmem_limit_bytes=24 * MIB
    )

    def whole(*shape):
        return pl.BlockSpec(shape, lambda i: (0,) * len(shape))

    def attend(part, start, name):
        count = part.shape[1] // HD
        first_block = start // HEAD_BLOCK
        heads = pl.BlockSpec((tokens, HEAD_BLOCK * HD), lambda i: (0, first_block + i))
        return pl.pallas_call(
            functools.partial(attend_kernel, start),
            grid=(count // HEAD_BLOCK,),
            in_specs=[
                smem,
                smem,
                pl.BlockSpec((tokens, HEAD_BLOCK * HD), lambda i: (0, i)),
                heads,
                heads,
                pl.BlockSpec((NARROW, HEAD_BLOCK * HD), lambda i: (0, first_block + i)),
            ],
            out_specs=[
                whole(count, tokens),
                pl.BlockSpec((HEAD_BLOCK, NARROW, tokens), lambda i: (i, 0, 0)),
            ],
            out_shape=[
                jax.ShapeDtypeStruct((count, tokens), jnp.float32),
                jax.ShapeDtypeStruct((count, NARROW, tokens), jnp.float32),
            ],
            compiler_params=params,
            cost_estimate=pl.CostEstimate(
                flops=4 * count * tokens * tokens * HD,
                bytes_accessed=3 * tokens * count * HD * 2,
                transcendentals=count * tokens * tokens,
            ),
            name=name,
        )(kept_tiles, kept_counts, part, flat_key, flat_value, patch_weight)

    level, mapped = attend(flat_query, 0, "own_queries")
    level, ready = lax.optimization_barrier((level, ready))
    other_level = lax.ppermute(level, "sp", swap)
    levels, shares = [], []
    for part, start in zip(other_queries, starts):
        if levels:
            part, _ = lax.optimization_barrier((part, levels[-1]))
        part_level, share = attend(part, start, "other_queries")
        levels.append(part_level)
        shares.append(share)
    sent = pl.pallas_call(
        functools.partial(combine_kernel, len(levels)),
        grid=(1,),
        in_specs=[whole(*part.shape) for part in (other_level, *levels, *shares)],
        out_specs=whole(NARROW + HEADS, tokens),
        out_shape=jax.ShapeDtypeStruct((NARROW + HEADS, tokens), jnp.float32),
        compiler_params=params,
        name="combine",
    )(other_level, *levels, *shares)
    got = lax.ppermute(sent, "sp", swap)
    rank = lax.axis_index("sp").astype(jnp.int32).reshape(1)
    rim_tokens = frames // 2 * cols
    latent, rim = pl.pallas_call(
        functools.partial(merge_kernel, frames, rows, cols),
        grid=(1,),
        in_specs=[smem, whole(NARROW + HEADS, tokens), whole(HEADS, NARROW, tokens)],
        out_specs=[whole(tokens // 2, 2 * NARROW), whole(rim_tokens, 2 * NARROW)],
        out_shape=[
            jax.ShapeDtypeStruct((tokens // 2, 2 * NARROW), jnp.bfloat16),
            jax.ShapeDtypeStruct((rim_tokens, 2 * NARROW), jnp.bfloat16),
        ],
        compiler_params=params,
        name="merge",
    )(rank, got, mapped)
    return latent, rim, ready


def to_tiles(grid, tile_size):
    frame_count, row_count, col_count, feature_width = grid.shape
    tiled = grid.reshape(
        frame_count // TT, TT, row_count // TH, TH, col_count // TW, TW, feature_width
    ).transpose(0, 2, 4, 1, 3, 5, 6)
    return tiled.reshape(-1, tile_size, feature_width)


def from_tiles(tiles, frame_count, row_count, col_count):
    feature_width = tiles.shape[-1]
    grid = tiles.reshape(
        frame_count // TT, row_count // TH, col_count // TW, TT, TH, TW, feature_width
    ).transpose(0, 3, 1, 4, 2, 5, 6)
    return grid.reshape(frame_count, row_count, col_count, feature_width)


def attend_tiles(query_tiles, key_tiles, value_tiles, tile_index, live_count):
    head_count = query_tiles.shape[0]
    tile_size = query_tiles.shape[2]
    head_size = query_tiles.shape[3]
    keep_count = tile_index.shape[2]

    def one_tile(packed):
        query_block, index_block, count_block = packed
        key_sel = jax.vmap(lambda source, picks: source[picks])(key_tiles, index_block).reshape(
            head_count, keep_count * tile_size, head_size
        )
        value_sel = jax.vmap(lambda source, picks: source[picks])(value_tiles, index_block).reshape(
            head_count, keep_count * tile_size, head_size
        )
        scores = jnp.einsum(
            "hqd,hkd->hqk", query_block, key_sel, preferred_element_type=jnp.float32
        ) * head_size ** (-0.5)
        live = jnp.arange(keep_count, dtype=jnp.int32)[None, :] < count_block[:, None]
        live = jnp.repeat(live, tile_size, axis=1)[:, None, :]
        scores = jnp.where(live, scores, -1e30)
        row_top = jnp.max(scores, axis=-1, keepdims=True)
        exponent = jnp.where(live, jnp.exp(scores - row_top), 0.0)
        weights = (exponent / jnp.sum(exponent, axis=-1, keepdims=True)).astype(jnp.bfloat16)
        result = jnp.einsum("hqk,hkd->hqd", weights, value_sel, preferred_element_type=jnp.float32)
        return result.astype(jnp.bfloat16)

    return lax.map(
        one_tile,
        (
            query_tiles.transpose(1, 0, 2, 3),
            tile_index.transpose(1, 0, 2),
            live_count.transpose(1, 0),
        ),
    )


def exchanged_attention(queries, key_states, value_states, kept_tiles, kept_counts, patch_weight):
    frame_count, local_rows, token_cols, feature_count = queries.shape[2:]
    tokens = frame_count * local_rows * token_cols
    sp_count = lax.axis_size("sp")
    sp_rank = lax.axis_index("sp")
    local_heads = HEADS // sp_count
    clip_rows = local_rows * sp_count
    tile_size = TT * TH * TW
    mixed_query, mixed_key, mixed_value = (
        lax.all_to_all(part.reshape(tokens, feature_count), "sp", split_axis=1, concat_axis=0, tiled=True)
        for part in (queries, key_states, value_states)
    )
    own_width = mixed_query.shape[1]

    def head_tiles(mixed):
        grid = mixed.reshape(sp_count, frame_count, local_rows, token_cols, own_width).transpose(
            1, 0, 2, 3, 4
        )
        tiles = to_tiles(grid.reshape(frame_count, clip_rows, token_cols, own_width), tile_size)
        return tiles.reshape(tiles.shape[0], tile_size, local_heads, HD).transpose(2, 0, 1, 3)

    outputs = attend_tiles(
        head_tiles(mixed_query),
        head_tiles(mixed_key),
        head_tiles(mixed_value),
        lax.dynamic_slice_in_dim(kept_tiles, sp_rank * local_heads, local_heads, 0),
        lax.dynamic_slice_in_dim(kept_counts, sp_rank * local_heads, local_heads, 0),
    )
    tile_count = outputs.shape[0]
    attended = from_tiles(
        outputs.transpose(0, 2, 1, 3).reshape(tile_count, tile_size, own_width),
        frame_count,
        clip_rows,
        token_cols,
    )
    attended = attended.reshape(frame_count, sp_count, local_rows, token_cols, own_width).transpose(
        1, 0, 2, 3, 4
    )
    attended = attended.reshape(sp_count * tokens, own_width)
    restored = lax.all_to_all(attended, "sp", split_axis=0, concat_axis=1, tiled=True)
    latent = jnp.dot(restored, patch_weight, preferred_element_type=jnp.float32)
    latent = latent.astype(jnp.bfloat16)
    packed = jnp.concatenate([latent[: tokens // 2], latent[tokens // 2 :]], axis=1)
    grid = packed.reshape(frame_count // 2, local_rows, token_cols, 2 * NARROW)
    return packed, grid[:, 0].reshape(-1, 2 * NARROW), grid[:, -1].reshape(-1, 2 * NARROW)


def spread_kernel(plain_ref, out_ref):
    empty = jnp.zeros((LAT, CH), jnp.bfloat16)
    for side in range(2):
        blocks = itertools.product(range(3), range(2), range(2), range(2), range(2))
        for position, (dt, rr, cc, u, w) in enumerate(blocks):
            dz = 2 * cc + w - (1 - side)
            for ro in range(2):
                dy = 2 * rr + u - ro
                inside = 0 <= dy < 3 and 0 <= dz < 3
                block = plain_ref[(dt * 3 + dy) * 3 + dz] if inside else empty
                out_ref[side, position * LAT : (position + 1) * LAT, ro * CH : (ro + 1) * CH] = block


def first_weights(first_kernel):
    return pl.pallas_call(
        spread_kernel,
        grid=(1,),
        in_specs=[pl.BlockSpec(first_kernel.shape, lambda i: (0, 0, 0))],
        out_specs=pl.BlockSpec((2, 12 * NARROW, 2 * CH), lambda i: (0, 0, 0)),
        out_shape=jax.ShapeDtypeStruct((2, 12 * NARROW, 2 * CH), jnp.bfloat16),
        name="spread_first_kernel",
    )(first_kernel)


def decode_kernel(
    frames,
    rows,
    cols,
    place_ref,
    own_ref,
    above_ref,
    below_ref,
    weight_hbm,
    kernel_hbm,
    out_ref,
    token_ref,
    pair_ref,
    first_ref,
    act_ref,
    wide_ref,
    weight_ref,
    kernel_ref,
    sems,
):
    at_first = place_ref[0] == 0
    at_last = place_ref[0] == place_ref[1] - 1
    copies = [
        pltpu.make_async_copy(weight_hbm, weight_ref, sems.at[0]),
        pltpu.make_async_copy(kernel_hbm, kernel_ref, sems.at[1]),
    ]
    for copy in copies:
        copy.start()

    lane = lax.broadcasted_iota(jnp.int32, (1, 1, 1, 2 * NARROW), 3)

    def unpacked(ref, height):
        plain = ref[...].astype(jnp.float32)
        turned = pltpu.roll(plain, NARROW, 1)
        shape = (frames // 2, height, cols, 2 * NARROW)
        plain, turned = plain.reshape(shape), turned.reshape(shape)
        early = jnp.where(lane < NARROW, plain, turned)
        late = jnp.where(lane < NARROW, turned, plain)
        return jnp.concatenate([early, late], axis=0)

    token_ref[:, 1 : 1 + rows, 8 : 8 + cols, :] = unpacked(own_ref, rows)
    above = unpacked(above_ref, 1)
    below = above if below_ref is above_ref else unpacked(below_ref, 1)
    for f in range(frames):
        edge = pltpu.roll(token_ref[f, 1, 8 : 8 + cols, :], 2 * LAT, 1)
        token_ref[f, 0, 8 : 8 + cols, :] = jnp.where(at_first, edge, above[f, 0])
        edge = pltpu.roll(token_ref[f, rows, 8 : 8 + cols, :], 2 * NARROW - 2 * LAT, 1)
        token_ref[f, rows + 1, 8 : 8 + cols, :] = jnp.where(at_last, edge, below[f, 0])
    for f in range(frames):
        for r in range(rows + 2):
            start = token_ref[f, r, 8:16, :]
            token_ref[f, r, 7:8, :] = pltpu.roll(start, LAT, 1)[0:1]
            end = token_ref[f, r, cols : 8 + cols, :]
            token_ref[f, r, 8 + cols : 9 + cols, :] = pltpu.roll(end, 2 * NARROW - LAT, 1)[7:8]

    for side in range(2):
        pair = jnp.where(
            lane < NARROW,
            token_ref[:, :, 7 + side : 7 + side + cols, :],
            token_ref[:, :, 8 + side : 8 + side + cols, :],
        ).astype(jnp.bfloat16)
        pair_ref[side, 2:] = pair
        pair_ref[side, 0] = pair[0]
        pair_ref[side, 1] = pair[0]

    copies[0].wait()
    gaps = rows + 1
    for side in range(2):
        columns = jnp.concatenate(
            [
                pair_ref[side, dt : dt + frames, rr : rr + gaps].reshape(frames * gaps * cols, 2 * NARROW)
                for dt in range(3)
                for rr in range(2)
            ],
            axis=1,
        )
        first = jnp.dot(columns, weight_ref[side], preferred_element_type=jnp.float32) * VAE_SCALE
        first = first.astype(jnp.bfloat16).astype(jnp.float32)
        act = first / (1.0 + jnp.exp(-first))
        first = first.reshape(frames, gaps, cols, 2 * CH)
        act = act.reshape(frames, gaps, cols, 2 * CH)
        for f in range(frames):
            for g in range(gaps):
                for ro in range(2):
                    for part in range(CH // 128):
                        lanes = slice(ro * CH + part * 128, ro * CH + part * 128 + 128)
                        row = 2 * g + ro
                        into = pl.ds(8 + side, cols, stride=2)
                        first_ref[part, f, row, into, :] = first[f, g, :, lanes]
                        act_ref[part, f, row, into, :] = act[f, g, :, lanes]

    width = 2 * cols
    height = 2 * rows
    for part in range(CH // 128):
        for f in range(frames):
            act_ref[part, f, 0] = jnp.where(at_first, act_ref[part, f, 1], act_ref[part, f, 0])
            act_ref[part, f, height + 1] = jnp.where(
                at_last, act_ref[part, f, height], act_ref[part, f, height + 1]
            )
        act_ref[part, :, :, 7:8, :] = act_ref[part, :, :, 8:9, :]
        act_ref[part, :, :, 8 + width : 9 + width, :] = act_ref[part, :, :, 7 + width : 8 + width, :]
        for dz in range(3):
            lanes = slice(dz * CH + part * 128, dz * CH + part * 128 + 128)
            shifted = act_ref[part, :, :, 7 + dz : 7 + dz + width, :].astype(jnp.bfloat16)
            wide_ref[2:, :, :, lanes] = shifted
            wide_ref[0, :, :, lanes] = shifted[0]
            wide_ref[1, :, :, lanes] = shifted[0]

    for copy in copies[1:]:
        copy.wait()
    cells = frames * height * width
    total = None
    for dt in range(3):
        for dy in range(3):
            window = wide_ref[dt : dt + frames, dy : dy + height].reshape(cells, 3 * CH)
            weight = jnp.concatenate(
                [kernel_ref[:, (dt * 3 + dy) * 3 + dz].reshape(CH, CH) for dz in range(3)], axis=0
            )
            product = jnp.dot(window, weight, preferred_element_type=jnp.float32)
            total = product if total is None else total + product
    total = total.reshape(frames, height, width, CH)
    for part in range(CH // 128):
        lanes = slice(part * 128, part * 128 + 128)
        residual = first_ref[part, :, 1 : 1 + height, 8 : 8 + width, :]
        out_ref[:, :, :, lanes] = (total[:, :, :, lanes] + residual).astype(jnp.bfloat16)


def decode(frames, rows, cols, place, own, rims, weights, kernel):
    height, width = 2 * rows, 2 * cols
    small = [own, *rims]

    def whole(shape):
        return pl.BlockSpec(shape, lambda i, place: (0,) * len(shape))

    def body(place_ref, own_ref, *refs):
        above_ref, below_ref = refs[0], refs[len(rims) - 1]
        decode_kernel(
            frames, rows, cols, place_ref, own_ref, above_ref, below_ref, *refs[len(rims) :]
        )

    grid_spec = pltpu.PrefetchScalarGridSpec(
        num_scalar_prefetch=1,
        grid=(1,),
        in_specs=[whole(part.shape) for part in small]
        + [pl.BlockSpec(memory_space=pl.ANY)] * 2,
        out_specs=whole((frames, height, width, CH)),
        scratch_shapes=[
            pltpu.VMEM((frames, rows + 2, cols + 16, 2 * NARROW), jnp.float32),
            pltpu.VMEM((2, frames + 2, rows + 2, cols, 2 * NARROW), jnp.bfloat16),
            pltpu.VMEM((CH // 128, frames, height + 2, width + 16, 128), jnp.float32),
            pltpu.VMEM((CH // 128, frames, height + 2, width + 16, 128), jnp.float32),
            pltpu.VMEM((frames + 2, height + 2, width, 3 * CH), jnp.bfloat16),
            pltpu.VMEM(weights.shape, jnp.bfloat16),
            pltpu.VMEM(kernel.shape, jnp.bfloat16),
            pltpu.SemaphoreType.DMA((2,)),
        ],
    )
    return pl.pallas_call(
        body,
        grid_spec=grid_spec,
        out_shape=jax.ShapeDtypeStruct((frames, height, width, CH), jnp.bfloat16),
        compiler_params=pltpu.CompilerParams(vmem_limit_bytes=56 * MIB),
        cost_estimate=pl.CostEstimate(
            flops=2 * frames * height * width * 27 * CH * CH,
            bytes_accessed=27 * CH * CH * 2 + frames * height * width * CH * 2,
            transcendentals=frames * height * width * CH,
        ),
        name="decode_block",
    )(place, *small, weights, kernel)


def local(
    queries,
    key_states,
    value_states,
    kept_tiles,
    kept_counts,
    patch_weight,
    decode_slot,
    first_kernel,
    second_kernel,
):
    frames, rows, cols = queries.shape[2:5]
    sp_count = lax.axis_size("sp")
    sp_rank = lax.axis_index("sp")
    segment_count = lax.axis_size("segment")
    segment_rank = lax.axis_index("segment")

    taps, own_channels, channels = second_kernel.shape
    share = taps * own_channels // segment_count
    flat = second_kernel.reshape(taps * own_channels, channels)
    flat = lax.dynamic_slice_in_dim(flat, segment_rank * share, share, 0)
    kernel = lax.all_gather(flat, ("grp", "segment"), axis=0, tiled=True)
    kernel = kernel.reshape(-1, taps, own_channels, channels)
    weights = first_weights(first_kernel)
    place = jnp.stack([sp_rank, jnp.int32(sp_count)]).astype(jnp.int32)
    orders = list(itertools.permutations(range(segment_count)))
    same = jnp.all(decode_slot[None, :] == jnp.array(orders, jnp.int32), axis=1)
    order = jnp.sum(jnp.where(same, jnp.arange(len(orders), dtype=jnp.int32), 0)).astype(jnp.int32)

    arguments = (queries, key_states, value_states, kept_tiles, kept_counts, patch_weight)
    if sp_count == 2 and rows * sp_count == TH and frames == TT:
        latent, rim, (weights, place, order) = split_attention(*arguments, (weights, place, order))
        moves = [(rim, [(0, 1), (1, 0)])]
    else:
        latent, top, bottom = exchanged_attention(*arguments)
        moves = [
            (bottom, [(i, i + 1) for i in range(sp_count - 1)]),
            (top, [(i + 1, i) for i in range(sp_count - 1)]),
        ]
    moves = [(latent, [(i, i) for i in range(sp_count)])] + moves

    def ordered(slots):
        def send(*parts):
            return tuple(
                lax.ppermute(
                    part,
                    ("segment", "sp"),
                    [(i * sp_count + a, slots[i] * sp_count + b) for i in range(segment_count) for a, b in pairs],
                )
                for part, (_, pairs) in zip(parts, moves)
            )

        return send

    own, *rims = lax.switch(order, [ordered(slots) for slots in orders], *[part for part, _ in moves])
    return decode(frames, rows, cols, place, own, rims, weights, kernel)[None, None]


def solution(mesh):
    return jax.shard_map(
        local,
        mesh=mesh,
        in_specs=(
            P("segment", "grp", None, "sp", None, None),
            P("segment", "grp", None, "sp", None, None),
            P("segment", "grp", None, "sp", None, None),
            P(),
            P(),
            P(),
            P(),
            P(),
            P(None, "grp", None),
        ),
        out_specs=P("segment", "grp", None, "sp", None, None),
        check_vma=False,
    )
```

```python
import functools
import itertools

import jax
import jax.numpy as jnp
from jax import lax
from jax.experimental import pallas as pl
from jax.experimental.pallas import tpu as pltpu
from jax.sharding import PartitionSpec as P

HEADS = 16
HD = 128
LAT = 16
CH = 256
TT = 4
TH = 8
TW = 8

VAE_SCALE = 1.0 / 0.476986
SCORE_UNIT = HD**-0.5 * 1.4426950408889634
HEAD_BLOCK = 4
HEAD_PARTS = (4, 8, 4)
TAP_PARTS = (15, 12)
NARROW = 4 * LAT
MIB = 1 << 20


def partial_head(head, q, k, v, tiles_ref, counts_ref):
    keys, queries = k.shape[0], q.shape[0]
    tile_count, keep = tiles_ref.shape[:2]
    scores = lax.dot_general(k, q, (((1,), (1,)), ((), ())), preferred_element_type=jnp.float32)
    lane = lax.broadcasted_iota(jnp.int32, (1, queries), 1)
    lane_tile = lax.rem(lax.div(lane, TW), tile_count)
    rows = []
    for key_tile in range(tile_count):
        row = jnp.zeros((1, queries), jnp.float32)
        for query_tile in range(tile_count):
            live = jnp.bool_(False)
            for slot in range(keep):
                here = jnp.logical_and(
                    tiles_ref[query_tile, slot, head] == key_tile, slot < counts_ref[query_tile, head]
                )
                live = jnp.logical_or(live, here)
            row = jnp.where(lane_tile == query_tile, jnp.where(live, 0.0, -1e30), row)
        rows.append(row[None])
    bias = jnp.concatenate(rows, axis=0)
    scores = scores.reshape(keys // (tile_count * TW), tile_count, TW, queries) + bias[None]
    scores = scores.reshape(keys, queries)
    top = jnp.max(scores, axis=0, keepdims=True)
    power = jnp.exp2((scores - top) * SCORE_UNIT)
    total = jnp.sum(power, axis=0, keepdims=True)
    out = lax.dot_general(
        v, power.astype(jnp.bfloat16), (((0,), (0,)), ((), ())), preferred_element_type=jnp.float32
    )
    return top * SCORE_UNIT, total, out


def row_choice(frames, rows, cols, row, lanes, start):
    token = lax.broadcasted_iota(jnp.int32, (frames * rows * cols, lanes), 0)
    lane = lax.broadcasted_iota(jnp.int32, (frames * rows * cols, lanes), 1) - start
    wanted = lax.div(lane, cols) * (rows * cols) + row * cols + lax.rem(lane, cols)
    inside = jnp.logical_and(lane >= 0, lane < frames * cols)
    return jnp.where(jnp.logical_and(inside, token == wanted), 1.0, 0.0)


def attend_kernel(
    offset, grid, rank_ref, tiles_ref, counts_ref, q_ref, k_ref, v_ref, w_ref, level_ref, mapped_ref, *rim_refs
):
    block = pl.program_id(0)
    if rim_refs:
        frames, rows, cols = grid
        near = jnp.where(rank_ref[0] == 0, rows - 1, 0)
        choices = [
            row_choice(frames, rows, cols, near, 2 * NARROW, start).astype(jnp.bfloat16)
            for start in (0, NARROW)
        ]
    for i in range(HEAD_BLOCK):
        cols = slice(i * HD, (i + 1) * HD)
        row = block * HEAD_BLOCK + i
        top, total, out = partial_head(
            offset + row, q_ref[:, cols], k_ref[:, cols], v_ref[:, cols], tiles_ref, counts_ref
        )
        out = (out / total).astype(jnp.bfloat16)
        level_ref[pl.ds(row, 1), :] = top + jnp.log2(total)
        mapped = jnp.dot(w_ref[:, cols], out, preferred_element_type=jnp.float32)
        mapped_ref[i] = mapped
        if rim_refs:
            rim = jnp.dot(mapped.astype(jnp.bfloat16), choices[i % 2], preferred_element_type=jnp.float32)
            if i % 2 == 0:
                even = rim
            else:
                rim_refs[0][i // 2] = (even + rim).astype(jnp.bfloat16)


def combine_kernel(parts, grid, rank_ref, theirs_ref, rim_ref, *refs):
    level_refs, mapped_refs = refs[:parts], refs[parts : 2 * parts]
    sent_ref, beside_ref = refs[2 * parts :]
    theirs = theirs_ref[...]
    mine = jnp.concatenate([ref[...] for ref in level_refs], axis=0)
    high = jnp.maximum(mine, theirs)
    level = high + jnp.log2(jnp.exp2(mine - high) + jnp.exp2(theirs - high))
    mine = jnp.exp2(mine - level)
    total = None
    head = 0
    for ref in mapped_refs:
        for i in range(ref.shape[0]):
            term = ref[i] * mine[head : head + 1]
            total = term if total is None else total + term
            head += 1
    theirs = jnp.exp2(theirs - level)
    sent_ref[0:NARROW, :] = total
    sent_ref[NARROW:, :] = theirs
    frames, rows, cols = grid
    near = jnp.where(rank_ref[0] == 0, 0, rows - 1)
    choice = row_choice(frames, rows, cols, near, frames * cols, 0)
    near_row = jnp.dot(
        jnp.concatenate([total, theirs], axis=0),
        choice,
        preferred_element_type=jnp.float32,
        precision=lax.Precision.HIGHEST,
    )
    beside = near_row[:NARROW]
    for head in range(HEADS):
        side = head % 2 * NARROW
        mapped = rim_ref[head // 2][:, side : side + NARROW].astype(jnp.float32)
        beside = beside + mapped * near_row[NARROW + head : NARROW + head + 1]
    beside_ref[...] = packed_latents(beside)


def packed_latents(latents):
    half = latents.shape[1] // 2
    packed = jnp.concatenate([latents[:, :half], latents[:, half:]], axis=0)
    return packed.T.astype(jnp.bfloat16)


def merge_kernel(got_ref, mapped_ref, beside_ref, out_ref):
    total = got_ref[0:NARROW, :]
    for head in range(HEADS):
        total = total + mapped_ref[head] * got_ref[NARROW + head : NARROW + head + 1, :]
    own = total.shape[1] // 2
    out_ref[0:own, :] = packed_latents(total)
    out_ref[own:, :] = beside_ref[...]


def split_attention(queries, key_states, value_states, kept_tiles, kept_counts, patch_weight, ready):
    frames, rows, cols, feature_count = queries.shape[2:]
    tokens = frames * rows * cols
    flat_query = queries.reshape(tokens, feature_count)
    flat_key = key_states.reshape(tokens, feature_count)
    flat_value = value_states.reshape(tokens, feature_count)
    swap = [(0, 1), (1, 0)]
    ends = list(itertools.accumulate(HEAD_PARTS))
    starts = [0] + ends[:-1]
    other_queries = [
        lax.ppermute(flat_query[:, start * HD : end * HD], "sp", swap) for start, end in zip(starts, ends)
    ]
    kept_tiles = kept_tiles.transpose(1, 2, 0)
    kept_counts = kept_counts.T
    patch_weight = patch_weight.T
    smem = pl.BlockSpec(memory_space=pltpu.SMEM)
    params = pltpu.CompilerParams(
        dimension_semantics=("arbitrary",), vmem_limit_bytes=24 * MIB
    )

    def whole(*shape):
        return pl.BlockSpec(shape, lambda i: (0,) * len(shape))

    grid = (frames, rows, cols)
    rank = lax.axis_index("sp").astype(jnp.int32).reshape(1)
    rim_tokens = frames * cols

    def attend(part, start, name, with_rim=False):
        count = part.shape[1] // HD
        first_block = start // HEAD_BLOCK
        heads = pl.BlockSpec((tokens, HEAD_BLOCK * HD), lambda i: (0, first_block + i))
        return pl.pallas_call(
            functools.partial(attend_kernel, start, grid),
            grid=(count // HEAD_BLOCK,),
            in_specs=[
                smem,
                smem,
                smem,
                pl.BlockSpec((tokens, HEAD_BLOCK * HD), lambda i: (0, i)),
                heads,
                heads,
                pl.BlockSpec((NARROW, HEAD_BLOCK * HD), lambda i: (0, first_block + i)),
            ],
            out_specs=[
                whole(count, tokens),
                pl.BlockSpec((HEAD_BLOCK, NARROW, tokens), lambda i: (i, 0, 0)),
                pl.BlockSpec((HEAD_BLOCK // 2, NARROW, 2 * rim_tokens), lambda i: (i, 0, 0)),
            ][: 3 if with_rim else 2],
            out_shape=[
                jax.ShapeDtypeStruct((count, tokens), jnp.float32),
                jax.ShapeDtypeStruct((count, NARROW, tokens), jnp.float32),
                jax.ShapeDtypeStruct((count // 2, NARROW, 2 * rim_tokens), jnp.bfloat16),
            ][: 3 if with_rim else 2],
            compiler_params=params,
            cost_estimate=pl.CostEstimate(
                flops=4 * count * tokens * tokens * HD,
                bytes_accessed=3 * tokens * count * HD * 2,
                transcendentals=count * tokens * tokens,
            ),
            name=name,
        )(rank, kept_tiles, kept_counts, part, flat_key, flat_value, patch_weight)

    level, mapped, rim = attend(flat_query, 0, "own_queries", with_rim=True)
    level, ready = lax.optimization_barrier((level, ready))
    other_level = lax.ppermute(level, "sp", swap)
    other_rim = lax.ppermute(rim, "sp", swap)
    levels, shares = [], []
    for part, start in zip(other_queries, starts):
        if levels:
            part, _ = lax.optimization_barrier((part, levels[-1]))
        part_level, share = attend(part, start, "other_queries")
        levels.append(part_level)
        shares.append(share)
    operands = (other_level, other_rim, *levels, *shares)
    sent, beside = pl.pallas_call(
        functools.partial(combine_kernel, len(levels), grid),
        grid=(1,),
        in_specs=[smem] + [whole(*part.shape) for part in operands],
        out_specs=[whole(NARROW + HEADS, tokens), whole(rim_tokens // 2, 2 * NARROW)],
        out_shape=[
            jax.ShapeDtypeStruct((NARROW + HEADS, tokens), jnp.float32),
            jax.ShapeDtypeStruct((rim_tokens // 2, 2 * NARROW), jnp.bfloat16),
        ],
        compiler_params=params,
        name="combine",
    )(rank, *operands)
    got = lax.ppermute(sent, "sp", swap)
    message = pl.pallas_call(
        merge_kernel,
        grid=(1,),
        in_specs=[whole(*part.shape) for part in (got, mapped, beside)],
        out_specs=whole((tokens + rim_tokens) // 2, 2 * NARROW),
        out_shape=jax.ShapeDtypeStruct(((tokens + rim_tokens) // 2, 2 * NARROW), jnp.bfloat16),
        compiler_params=params,
        name="merge",
    )(got, mapped, beside)
    return message, ready


def to_tiles(grid, tile_size):
    frame_count, row_count, col_count, feature_width = grid.shape
    tiled = grid.reshape(
        frame_count // TT, TT, row_count // TH, TH, col_count // TW, TW, feature_width
    ).transpose(0, 2, 4, 1, 3, 5, 6)
    return tiled.reshape(-1, tile_size, feature_width)


def from_tiles(tiles, frame_count, row_count, col_count):
    feature_width = tiles.shape[-1]
    grid = tiles.reshape(
        frame_count // TT, row_count // TH, col_count // TW, TT, TH, TW, feature_width
    ).transpose(0, 3, 1, 4, 2, 5, 6)
    return grid.reshape(frame_count, row_count, col_count, feature_width)


def attend_tiles(query_tiles, key_tiles, value_tiles, tile_index, live_count):
    head_count = query_tiles.shape[0]
    tile_size = query_tiles.shape[2]
    head_size = query_tiles.shape[3]
    keep_count = tile_index.shape[2]

    def one_tile(packed):
        query_block, index_block, count_block = packed
        key_sel = jax.vmap(lambda source, picks: source[picks])(key_tiles, index_block).reshape(
            head_count, keep_count * tile_size, head_size
        )
        value_sel = jax.vmap(lambda source, picks: source[picks])(value_tiles, index_block).reshape(
            head_count, keep_count * tile_size, head_size
        )
        scores = jnp.einsum(
            "hqd,hkd->hqk", query_block, key_sel, preferred_element_type=jnp.float32
        ) * head_size ** (-0.5)
        live = jnp.arange(keep_count, dtype=jnp.int32)[None, :] < count_block[:, None]
        live = jnp.repeat(live, tile_size, axis=1)[:, None, :]
        scores = jnp.where(live, scores, -1e30)
        row_top = jnp.max(scores, axis=-1, keepdims=True)
        exponent = jnp.where(live, jnp.exp(scores - row_top), 0.0)
        weights = (exponent / jnp.sum(exponent, axis=-1, keepdims=True)).astype(jnp.bfloat16)
        result = jnp.einsum("hqk,hkd->hqd", weights, value_sel, preferred_element_type=jnp.float32)
        return result.astype(jnp.bfloat16)

    return lax.map(
        one_tile,
        (
            query_tiles.transpose(1, 0, 2, 3),
            tile_index.transpose(1, 0, 2),
            live_count.transpose(1, 0),
        ),
    )


def exchanged_attention(queries, key_states, value_states, kept_tiles, kept_counts, patch_weight):
    frame_count, local_rows, token_cols, feature_count = queries.shape[2:]
    tokens = frame_count * local_rows * token_cols
    sp_count = lax.axis_size("sp")
    sp_rank = lax.axis_index("sp")
    local_heads = HEADS // sp_count
    clip_rows = local_rows * sp_count
    tile_size = TT * TH * TW
    mixed_query, mixed_key, mixed_value = (
        lax.all_to_all(part.reshape(tokens, feature_count), "sp", split_axis=1, concat_axis=0, tiled=True)
        for part in (queries, key_states, value_states)
    )
    own_width = mixed_query.shape[1]

    def head_tiles(mixed):
        grid = mixed.reshape(sp_count, frame_count, local_rows, token_cols, own_width).transpose(
            1, 0, 2, 3, 4
        )
        tiles = to_tiles(grid.reshape(frame_count, clip_rows, token_cols, own_width), tile_size)
        return tiles.reshape(tiles.shape[0], tile_size, local_heads, HD).transpose(2, 0, 1, 3)

    outputs = attend_tiles(
        head_tiles(mixed_query),
        head_tiles(mixed_key),
        head_tiles(mixed_value),
        lax.dynamic_slice_in_dim(kept_tiles, sp_rank * local_heads, local_heads, 0),
        lax.dynamic_slice_in_dim(kept_counts, sp_rank * local_heads, local_heads, 0),
    )
    tile_count = outputs.shape[0]
    attended = from_tiles(
        outputs.transpose(0, 2, 1, 3).reshape(tile_count, tile_size, own_width),
        frame_count,
        clip_rows,
        token_cols,
    )
    attended = attended.reshape(frame_count, sp_count, local_rows, token_cols, own_width).transpose(
        1, 0, 2, 3, 4
    )
    attended = attended.reshape(sp_count * tokens, own_width)
    restored = lax.all_to_all(attended, "sp", split_axis=0, concat_axis=1, tiled=True)
    latent = jnp.dot(restored, patch_weight, preferred_element_type=jnp.float32)
    latent = latent.astype(jnp.bfloat16)
    packed = jnp.concatenate([latent[: tokens // 2], latent[tokens // 2 :]], axis=1)
    grid = packed.reshape(frame_count // 2, local_rows, token_cols, 2 * NARROW)
    above = lax.ppermute(grid[:, -1], "sp", [(i, i + 1) for i in range(sp_count - 1)])
    below = lax.ppermute(grid[:, 0], "sp", [(i + 1, i) for i in range(sp_count - 1)])
    rims = [rim.reshape(-1, 2 * NARROW) for rim in (above, below)]
    return jnp.concatenate([packed, *rims], axis=0)


def spread_kernel(plain_ref, out_ref):
    empty = jnp.zeros((LAT, CH), jnp.bfloat16)
    for side in range(2):
        blocks = itertools.product(range(3), range(2), range(2), range(2), range(2))
        for position, (dt, rr, cc, u, w) in enumerate(blocks):
            dz = 2 * cc + w - (1 - side)
            for ro in range(2):
                dy = 2 * rr + u - ro
                inside = 0 <= dy < 3 and 0 <= dz < 3
                block = plain_ref[(dt * 3 + dy) * 3 + dz] if inside else empty
                out_ref[side, position * LAT : (position + 1) * LAT, ro * CH : (ro + 1) * CH] = block


def first_weights(first_kernel):
    return pl.pallas_call(
        spread_kernel,
        grid=(1,),
        in_specs=[pl.BlockSpec(first_kernel.shape, lambda i: (0, 0, 0))],
        out_specs=pl.BlockSpec((2, 12 * NARROW, 2 * CH), lambda i: (0, 0, 0)),
        out_shape=jax.ShapeDtypeStruct((2, 12 * NARROW, 2 * CH), jnp.bfloat16),
        name="spread_first_kernel",
    )(first_kernel)


def decode_kernel(
    frames,
    rows,
    cols,
    place_ref,
    message_refs,
    weight_hbm,
    mine_refs,
    theirs_refs,
    out_ref,
    token_ref,
    pair_ref,
    first_ref,
    act_ref,
    wide_ref,
    weight_ref,
    kernel_ref,
    sems,
):
    at_first = place_ref[0] == 0
    at_last = place_ref[0] == place_ref[1] - 1
    step = place_ref[2]
    half = place_ref[3]
    copies = [pltpu.make_async_copy(weight_hbm, weight_ref, sems.at[0])]
    tap = 0
    for mine_ref, theirs_ref in zip(mine_refs, theirs_refs):
        taps = pl.ds(tap, mine_ref.shape[1])
        for part_ref, side in ((mine_ref, half), (theirs_ref, 1 - half)):
            copies.append(
                pltpu.make_async_copy(part_ref, kernel_ref.at[side, :, taps], sems.at[len(copies)])
            )
        tap += mine_ref.shape[1]
    for copy in copies:
        copy.start()

    lane = lax.broadcasted_iota(jnp.int32, (1, 1, 1, 2 * NARROW), 3)

    message = message_refs[0][...]
    for k in range(1, len(message_refs)):
        message = jnp.where(step == k, message_refs[k][...], message)
    own_count = frames // 2 * rows * cols
    rim_count = frames // 2 * cols

    def unpacked(packed, height):
        plain = packed.astype(jnp.float32)
        turned = pltpu.roll(plain, NARROW, 1)
        shape = (frames // 2, height, cols, 2 * NARROW)
        plain, turned = plain.reshape(shape), turned.reshape(shape)
        early = jnp.where(lane < NARROW, plain, turned)
        late = jnp.where(lane < NARROW, turned, plain)
        return jnp.concatenate([early, late], axis=0)

    token_ref[:, 1 : 1 + rows, 8 : 8 + cols, :] = unpacked(message[:own_count], rows)
    above = unpacked(message[own_count : own_count + rim_count], 1)
    below = unpacked(message[-rim_count:], 1)
    for f in range(frames):
        edge = pltpu.roll(token_ref[f, 1, 8 : 8 + cols, :], 2 * LAT, 1)
        token_ref[f, 0, 8 : 8 + cols, :] = jnp.where(at_first, edge, above[f, 0])
        edge = pltpu.roll(token_ref[f, rows, 8 : 8 + cols, :], 2 * NARROW - 2 * LAT, 1)
        token_ref[f, rows + 1, 8 : 8 + cols, :] = jnp.where(at_last, edge, below[f, 0])
    for f in range(frames):
        for r in range(rows + 2):
            start = token_ref[f, r, 8:16, :]
            token_ref[f, r, 7:8, :] = pltpu.roll(start, LAT, 1)[0:1]
            end = token_ref[f, r, cols : 8 + cols, :]
            token_ref[f, r, 8 + cols : 9 + cols, :] = pltpu.roll(end, 2 * NARROW - LAT, 1)[7:8]

    for side in range(2):
        pair = jnp.where(
            lane < NARROW,
            token_ref[:, :, 7 + side : 7 + side + cols, :],
            token_ref[:, :, 8 + side : 8 + side + cols, :],
        ).astype(jnp.bfloat16)
        pair_ref[side, 2:] = pair
        pair_ref[side, 0] = pair[0]
        pair_ref[side, 1] = pair[0]

    copies[0].wait()
    gaps = rows + 1
    for side in range(2):
        columns = jnp.concatenate(
            [
                pair_ref[side, dt : dt + frames, rr : rr + gaps].reshape(frames * gaps * cols, 2 * NARROW)
                for dt in range(3)
                for rr in range(2)
            ],
            axis=1,
        )
        first = jnp.dot(columns, weight_ref[side], preferred_element_type=jnp.float32) * VAE_SCALE
        first = first.astype(jnp.bfloat16).astype(jnp.float32)
        act = first / (1.0 + jnp.exp(-first))
        first = first.reshape(frames, gaps, cols, 2 * CH)
        act = act.reshape(frames, gaps, cols, 2 * CH)
        for f in range(frames):
            for g in range(gaps):
                for ro in range(2):
                    for part in range(CH // 128):
                        lanes = slice(ro * CH + part * 128, ro * CH + part * 128 + 128)
                        row = 2 * g + ro
                        into = pl.ds(8 + side, cols, stride=2)
                        first_ref[part, f, row, into, :] = first[f, g, :, lanes]
                        act_ref[part, f, row, into, :] = act[f, g, :, lanes]

    width = 2 * cols
    height = 2 * rows
    for part in range(CH // 128):
        for f in range(frames):
            act_ref[part, f, 0] = jnp.where(at_first, act_ref[part, f, 1], act_ref[part, f, 0])
            act_ref[part, f, height + 1] = jnp.where(
                at_last, act_ref[part, f, height], act_ref[part, f, height + 1]
            )
        act_ref[part, :, :, 7:8, :] = act_ref[part, :, :, 8:9, :]
        act_ref[part, :, :, 8 + width : 9 + width, :] = act_ref[part, :, :, 7 + width : 8 + width, :]
        for dz in range(3):
            lanes = slice(dz * CH + part * 128, dz * CH + part * 128 + 128)
            shifted = act_ref[part, :, :, 7 + dz : 7 + dz + width, :].astype(jnp.bfloat16)
            wide_ref[2:, :, :, lanes] = shifted
            wide_ref[0, :, :, lanes] = shifted[0]
            wide_ref[1, :, :, lanes] = shifted[0]

    for copy in copies[1:]:
        copy.wait()
    cells = frames * height * width
    total = None
    for dt in range(3):
        for dy in range(3):
            window = wide_ref[dt : dt + frames, dy : dy + height].reshape(cells, 3 * CH)
            weight = jnp.concatenate(
                [
                    jnp.concatenate(
                        [kernel_ref[side, :, (dt * 3 + dy) * 3 + dz].reshape(CH, CH // 2) for side in range(2)],
                        axis=1,
                    )
                    for dz in range(3)
                ],
                axis=0,
            )
            product = jnp.dot(window, weight, preferred_element_type=jnp.float32)
            total = product if total is None else total + product
    total = total.reshape(frames, height, width, CH)
    for part in range(CH // 128):
        lanes = slice(part * 128, part * 128 + 128)
        residual = first_ref[part, :, 1 : 1 + height, 8 : 8 + width, :]
        out_ref[:, :, :, lanes] = (total[:, :, :, lanes] + residual).astype(jnp.bfloat16)


def decode(frames, rows, cols, place, messages, weights, mine, theirs):
    height, width = 2 * rows, 2 * cols
    count, parts = len(messages), len(mine)
    groups, _, depth, _ = mine[0].shape

    def whole(shape):
        return pl.BlockSpec(shape, lambda i, place: (0,) * len(shape))

    def body(place_ref, *refs):
        message_refs, refs = refs[:count], refs[count:]
        weight_hbm, mine_refs, theirs_refs = refs[0], refs[1 : 1 + parts], refs[1 + parts : 1 + 2 * parts]
        decode_kernel(
            frames, rows, cols, place_ref, message_refs, weight_hbm, mine_refs, theirs_refs,
            *refs[1 + 2 * parts :],
        )

    grid_spec = pltpu.PrefetchScalarGridSpec(
        num_scalar_prefetch=1,
        grid=(1,),
        in_specs=[whole(part.shape) for part in messages]
        + [pl.BlockSpec(memory_space=pl.ANY)] * (1 + 2 * parts),
        out_specs=whole((frames, height, width, CH)),
        scratch_shapes=[
            pltpu.VMEM((frames, rows + 2, cols + 16, 2 * NARROW), jnp.float32),
            pltpu.VMEM((2, frames + 2, rows + 2, cols, 2 * NARROW), jnp.bfloat16),
            pltpu.VMEM((CH // 128, frames, height + 2, width + 16, 128), jnp.float32),
            pltpu.VMEM((CH // 128, frames, height + 2, width + 16, 128), jnp.float32),
            pltpu.VMEM((frames + 2, height + 2, width, 3 * CH), jnp.bfloat16),
            pltpu.VMEM(weights.shape, jnp.bfloat16),
            pltpu.VMEM((2, groups, 27, depth, CH // 2), jnp.bfloat16),
            pltpu.SemaphoreType.DMA((1 + 2 * parts,)),
        ],
    )
    return pl.pallas_call(
        body,
        grid_spec=grid_spec,
        out_shape=jax.ShapeDtypeStruct((frames, height, width, CH), jnp.bfloat16),
        compiler_params=pltpu.CompilerParams(vmem_limit_bytes=32 * MIB),
        cost_estimate=pl.CostEstimate(
            flops=2 * frames * height * width * 27 * CH * CH,
            bytes_accessed=27 * CH * CH * 2 + frames * height * width * CH * 2,
            transcendentals=frames * height * width * CH,
        ),
        name="decode_block",
    )(place, *messages, weights, *mine, *theirs)


def local(
    queries,
    key_states,
    value_states,
    kept_tiles,
    kept_counts,
    patch_weight,
    decode_slot,
    first_kernel,
    second_kernel,
):
    frames, rows, cols = queries.shape[2:5]
    sp_count = lax.axis_size("sp")
    sp_rank = lax.axis_index("sp")
    segment_count = lax.axis_size("segment")
    segment_rank = lax.axis_index("segment")

    half = lax.rem(segment_rank, 2)
    share = lax.dynamic_slice_in_dim(second_kernel, half * (CH // 2), CH // 2, 2)
    ends = list(itertools.accumulate(TAP_PARTS))
    mine = [
        lax.all_gather(share[end - count : end], "grp", axis=0, tiled=False)
        for end, count in zip(ends, TAP_PARTS)
    ]
    weights = first_weights(first_kernel)
    picks = (decode_slot == segment_rank).astype(jnp.int32)
    source = jnp.sum(jnp.arange(segment_count, dtype=jnp.int32) * picks)
    step = lax.rem(segment_rank - source + segment_count, segment_count)
    place = jnp.stack([sp_rank, jnp.int32(sp_count), step, half]).astype(jnp.int32)

    arguments = (queries, key_states, value_states, kept_tiles, kept_counts, patch_weight)
    if sp_count == 2 and rows * sp_count == TH and frames == TT:
        message, (weights, place) = split_attention(*arguments, (weights, place))
    else:
        message = exchanged_attention(*arguments)
    messages = [message] + [
        lax.ppermute(message, "segment", [(i, (i + step) % segment_count) for i in range(segment_count)])
        for step in range(1, segment_count)
    ]
    *mine, _ = lax.optimization_barrier((*mine, messages[-1]))
    theirs = [
        lax.ppermute(part, "segment", [(i, i ^ 1) for i in range(segment_count)]) for part in mine
    ]
    return decode(frames, rows, cols, place, messages, weights, mine, theirs)[None, None]


def solution(mesh):
    return jax.shard_map(
        local,
        mesh=mesh,
        in_specs=(
            P("segment", "grp", None, "sp", None, None),
            P("segment", "grp", None, "sp", None, None),
            P("segment", "grp", None, "sp", None, None),
            P(),
            P(),
            P(),
            P(),
            P(),
            P(None, "grp", None),
        ),
        out_specs=P("segment", "grp", None, "sp", None, None),
        check_vma=False,
    )
```

```python
import functools
import itertools

import jax
import jax.numpy as jnp
from jax import lax
from jax.experimental import pallas as pl
from jax.experimental.pallas import tpu as pltpu
from jax.sharding import PartitionSpec as P

HEADS = 16
HD = 128
LAT = 16
CH = 256
TT = 4
TH = 8
TW = 8

VAE_SCALE = 1.0 / 0.476986
SCORE_UNIT = HD**-0.5 * 1.4426950408889634
HEAD_BLOCK = 4
HEAD_PARTS = (4, 8, 4)
NARROW = 4 * LAT
MIB = 1 << 20


def partial_head(head, q, k, v, tiles_ref, counts_ref):
    keys, queries = k.shape[0], q.shape[0]
    tile_count, keep = tiles_ref.shape[:2]
    scores = lax.dot_general(k, q, (((1,), (1,)), ((), ())), preferred_element_type=jnp.float32)
    lane = lax.broadcasted_iota(jnp.int32, (1, queries), 1)
    lane_tile = lax.rem(lax.div(lane, TW), tile_count)
    rows = []
    for key_tile in range(tile_count):
        row = jnp.zeros((1, queries), jnp.float32)
        for query_tile in range(tile_count):
            live = jnp.bool_(False)
            for slot in range(keep):
                here = jnp.logical_and(
                    tiles_ref[query_tile, slot, head] == key_tile, slot < counts_ref[query_tile, head]
                )
                live = jnp.logical_or(live, here)
            row = jnp.where(lane_tile == query_tile, jnp.where(live, 0.0, -1e30), row)
        rows.append(row[None])
    bias = jnp.concatenate(rows, axis=0)
    scores = scores.reshape(keys // (tile_count * TW), tile_count, TW, queries) + bias[None]
    scores = scores.reshape(keys, queries)
    top = jnp.max(scores, axis=0, keepdims=True)
    power = jnp.exp2((scores - top) * SCORE_UNIT)
    total = jnp.sum(power, axis=0, keepdims=True)
    out = lax.dot_general(
        v, power.astype(jnp.bfloat16), (((0,), (0,)), ((), ())), preferred_element_type=jnp.float32
    )
    return top * SCORE_UNIT, total, out


def row_choice(frames, rows, cols, row, lanes, start):
    token = lax.broadcasted_iota(jnp.int32, (frames * rows * cols, lanes), 0)
    lane = lax.broadcasted_iota(jnp.int32, (frames * rows * cols, lanes), 1) - start
    wanted = lax.div(lane, cols) * (rows * cols) + row * cols + lax.rem(lane, cols)
    inside = jnp.logical_and(lane >= 0, lane < frames * cols)
    return jnp.where(jnp.logical_and(inside, token == wanted), 1.0, 0.0)


def attend_kernel(
    offset, grid, rank_ref, tiles_ref, counts_ref, q_ref, k_ref, v_ref, w_ref, level_ref, mapped_ref, *note_refs
):
    block = pl.program_id(0)
    if note_refs:
        note_ref = note_refs[0]
        frames, rows, cols = grid
        near = jnp.where(rank_ref[0] == 0, rows - 1, 0)
        choices = [
            row_choice(frames, rows, cols, near, 2 * NARROW, start).astype(jnp.bfloat16)
            for start in (0, NARROW)
        ]
    for i in range(HEAD_BLOCK):
        cols = slice(i * HD, (i + 1) * HD)
        row = block * HEAD_BLOCK + i
        top, total, out = partial_head(
            offset + row, q_ref[:, cols], k_ref[:, cols], v_ref[:, cols], tiles_ref, counts_ref
        )
        out = (out / total).astype(jnp.bfloat16)
        level_ref[pl.ds(row, 1), :] = top + jnp.log2(total)
        mapped = jnp.dot(w_ref[:, cols], out, preferred_element_type=jnp.float32)
        mapped_ref[i] = mapped
        if note_refs:
            rim = jnp.dot(mapped.astype(jnp.bfloat16), choices[i % 2], preferred_element_type=jnp.float32)
            if i % 2 == 0:
                even = rim
            else:
                pair = pl.multiple_of((row // 2) * NARROW, NARROW)
                note_ref[pl.ds(pair, NARROW), :] = (even + rim).astype(jnp.bfloat16)
    if note_refs:

        @pl.when(block == pl.num_programs(0) - 1)
        def _():
            rest = level_ref[...]
            rest = jnp.concatenate([rest[:, :128], rest[:, 128:]], axis=0)
            start = HEADS // 2 * NARROW
            for _ in range(3):
                part = rest.astype(jnp.bfloat16)
                note_ref[start : start + 2 * HEADS, :] = part
                rest = rest - part.astype(jnp.float32)
                start += 2 * HEADS


def combine_kernel(parts, note_ref, *refs):
    level_refs, mapped_refs, sent_ref = refs[:parts], refs[parts : 2 * parts], refs[-1]
    start = HEADS // 2 * NARROW
    theirs = [note_ref[start + k * 2 * HEADS : start + (k + 1) * 2 * HEADS, :] for k in range(3)]
    theirs = theirs[0].astype(jnp.float32) + theirs[1].astype(jnp.float32) + theirs[2].astype(jnp.float32)
    theirs = jnp.concatenate([theirs[:HEADS], theirs[HEADS:]], axis=1)
    mine = jnp.concatenate([ref[...] for ref in level_refs], axis=0)
    high = jnp.maximum(mine, theirs)
    level = high + jnp.log2(jnp.exp2(mine - high) + jnp.exp2(theirs - high))
    mine = jnp.exp2(mine - level)
    total = None
    head = 0
    for ref in mapped_refs:
        for i in range(ref.shape[0]):
            term = ref[i] * mine[head : head + 1]
            total = term if total is None else total + term
            head += 1
    sent_ref[0:NARROW, :] = total
    sent_ref[NARROW:, :] = jnp.exp2(theirs - level)


def beside_kernel(grid, rank_ref, sent_ref, note_ref, beside_ref):
    frames, rows, cols = grid
    near = jnp.where(rank_ref[0] == 0, 0, rows - 1)
    choice = row_choice(frames, rows, cols, near, frames * cols, 0)
    near_row = jnp.dot(
        sent_ref[...],
        choice,
        preferred_element_type=jnp.float32,
        precision=lax.Precision.HIGHEST,
    )
    beside = near_row[:NARROW]
    for head in range(HEADS):
        side = head % 2 * NARROW
        pair = head // 2 * NARROW
        mapped = note_ref[pair : pair + NARROW, side : side + NARROW].astype(jnp.float32)
        beside = beside + mapped * near_row[NARROW + head : NARROW + head + 1]
    beside_ref[...] = packed_latents(beside)


def packed_latents(latents):
    half = latents.shape[1] // 2
    packed = jnp.concatenate([latents[:, :half], latents[:, half:]], axis=0)
    return packed.T.astype(jnp.bfloat16)


def merge_kernel(got_ref, mapped_ref, beside_ref, out_ref):
    total = got_ref[0:NARROW, :]
    for head in range(HEADS):
        total = total + mapped_ref[head] * got_ref[NARROW + head : NARROW + head + 1, :]
    own = total.shape[1] // 2
    out_ref[0:own, :] = packed_latents(total)
    out_ref[own:, :] = beside_ref[...]


def split_attention(queries, key_states, value_states, kept_tiles, kept_counts, patch_weight, ready):
    frames, rows, cols, feature_count = queries.shape[2:]
    tokens = frames * rows * cols
    flat_query = queries.reshape(tokens, feature_count)
    flat_key = key_states.reshape(tokens, feature_count)
    flat_value = value_states.reshape(tokens, feature_count)
    swap = [(0, 1), (1, 0)]
    ends = list(itertools.accumulate(HEAD_PARTS))
    starts = [0] + ends[:-1]
    parts = []
    source = flat_query
    for start, end in zip(starts, ends):
        parts.append(source[:, start * HD : end * HD])
        if start == 0:
            source, _ = lax.optimization_barrier((source, parts[0]))
    other_queries = [lax.ppermute(part, "sp", swap) for part in parts]
    kept_tiles = kept_tiles.transpose(1, 2, 0)
    kept_counts = kept_counts.T
    patch_weight = patch_weight.T
    smem = pl.BlockSpec(memory_space=pltpu.SMEM)
    params = pltpu.CompilerParams(
        dimension_semantics=("arbitrary",), vmem_limit_bytes=24 * MIB
    )

    def whole(*shape):
        return pl.BlockSpec(shape, lambda i: (0,) * len(shape))

    grid = (frames, rows, cols)
    rank = lax.axis_index("sp").astype(jnp.int32).reshape(1)
    rim_tokens = frames * cols

    note_rows = HEADS // 2 * NARROW + 6 * HEADS

    def attend(part, start, name, with_note=False):
        count = part.shape[1] // HD
        first_block = start // HEAD_BLOCK
        heads = pl.BlockSpec((tokens, HEAD_BLOCK * HD), lambda i: (0, first_block + i))
        return pl.pallas_call(
            functools.partial(attend_kernel, start, grid),
            grid=(count // HEAD_BLOCK,),
            in_specs=[
                smem,
                smem,
                smem,
                pl.BlockSpec((tokens, HEAD_BLOCK * HD), lambda i: (0, i)),
                heads,
                heads,
                pl.BlockSpec((NARROW, HEAD_BLOCK * HD), lambda i: (0, first_block + i)),
            ],
            out_specs=[
                whole(count, tokens),
                pl.BlockSpec((HEAD_BLOCK, NARROW, tokens), lambda i: (i, 0, 0)),
                whole(note_rows, 2 * NARROW),
            ][: 3 if with_note else 2],
            out_shape=[
                jax.ShapeDtypeStruct((count, tokens), jnp.float32),
                jax.ShapeDtypeStruct((count, NARROW, tokens), jnp.float32),
                jax.ShapeDtypeStruct((note_rows, 2 * NARROW), jnp.bfloat16),
            ][: 3 if with_note else 2],
            compiler_params=params,
            cost_estimate=pl.CostEstimate(
                flops=count * tokens, bytes_accessed=count * tokens, transcendentals=0
            ),
            name=name,
        )(rank, kept_tiles, kept_counts, part, flat_key, flat_value, patch_weight)

    flat_query, *_ = lax.optimization_barrier((flat_query, *parts))
    _, mapped, note = attend(flat_query, 0, "own_queries", with_note=True)
    note, ready = lax.optimization_barrier((note, ready))
    other_note = lax.ppermute(note, "sp", swap)
    levels, shares = [], []
    for part, start in zip(other_queries, starts):
        part, _ = lax.optimization_barrier((part, levels[-1] if levels else note))
        part_level, share = attend(part, start, "other_queries")
        levels.append(part_level)
        shares.append(share)
    operands = (other_note, *levels, *shares)
    sent = pl.pallas_call(
        functools.partial(combine_kernel, len(levels)),
        grid=(1,),
        in_specs=[whole(*part.shape) for part in operands],
        out_specs=whole(NARROW + HEADS, tokens),
        out_shape=jax.ShapeDtypeStruct((NARROW + HEADS, tokens), jnp.float32),
        compiler_params=params,
        name="combine",
    )(*operands)
    got = lax.ppermute(sent, "sp", swap)
    beside = pl.pallas_call(
        functools.partial(beside_kernel, grid),
        grid=(1,),
        in_specs=[smem, whole(*sent.shape), whole(*other_note.shape)],
        out_specs=whole(rim_tokens // 2, 2 * NARROW),
        out_shape=jax.ShapeDtypeStruct((rim_tokens // 2, 2 * NARROW), jnp.bfloat16),
        compiler_params=params,
        name="beside",
    )(rank, sent, other_note)
    message = pl.pallas_call(
        merge_kernel,
        grid=(1,),
        in_specs=[whole(*part.shape) for part in (got, mapped, beside)],
        out_specs=whole((tokens + rim_tokens) // 2, 2 * NARROW),
        out_shape=jax.ShapeDtypeStruct(((tokens + rim_tokens) // 2, 2 * NARROW), jnp.bfloat16),
        compiler_params=params,
        name="merge",
    )(got, mapped, beside)
    return message, got, ready


def to_tiles(grid, tile_size):
    frame_count, row_count, col_count, feature_width = grid.shape
    tiled = grid.reshape(
        frame_count // TT, TT, row_count // TH, TH, col_count // TW, TW, feature_width
    ).transpose(0, 2, 4, 1, 3, 5, 6)
    return tiled.reshape(-1, tile_size, feature_width)


def from_tiles(tiles, frame_count, row_count, col_count):
    feature_width = tiles.shape[-1]
    grid = tiles.reshape(
        frame_count // TT, row_count // TH, col_count // TW, TT, TH, TW, feature_width
    ).transpose(0, 3, 1, 4, 2, 5, 6)
    return grid.reshape(frame_count, row_count, col_count, feature_width)


def attend_tiles(query_tiles, key_tiles, value_tiles, tile_index, live_count):
    head_count = query_tiles.shape[0]
    tile_size = query_tiles.shape[2]
    head_size = query_tiles.shape[3]
    keep_count = tile_index.shape[2]

    def one_tile(packed):
        query_block, index_block, count_block = packed
        key_sel = jax.vmap(lambda source, picks: source[picks])(key_tiles, index_block).reshape(
            head_count, keep_count * tile_size, head_size
        )
        value_sel = jax.vmap(lambda source, picks: source[picks])(value_tiles, index_block).reshape(
            head_count, keep_count * tile_size, head_size
        )
        scores = jnp.einsum(
            "hqd,hkd->hqk", query_block, key_sel, preferred_element_type=jnp.float32
        ) * head_size ** (-0.5)
        live = jnp.arange(keep_count, dtype=jnp.int32)[None, :] < count_block[:, None]
        live = jnp.repeat(live, tile_size, axis=1)[:, None, :]
        scores = jnp.where(live, scores, -1e30)
        row_top = jnp.max(scores, axis=-1, keepdims=True)
        exponent = jnp.where(live, jnp.exp(scores - row_top), 0.0)
        weights = (exponent / jnp.sum(exponent, axis=-1, keepdims=True)).astype(jnp.bfloat16)
        result = jnp.einsum("hqk,hkd->hqd", weights, value_sel, preferred_element_type=jnp.float32)
        return result.astype(jnp.bfloat16)

    return lax.map(
        one_tile,
        (
            query_tiles.transpose(1, 0, 2, 3),
            tile_index.transpose(1, 0, 2),
            live_count.transpose(1, 0),
        ),
    )


def exchanged_attention(queries, key_states, value_states, kept_tiles, kept_counts, patch_weight):
    frame_count, local_rows, token_cols, feature_count = queries.shape[2:]
    tokens = frame_count * local_rows * token_cols
    sp_count = lax.axis_size("sp")
    sp_rank = lax.axis_index("sp")
    local_heads = HEADS // sp_count
    clip_rows = local_rows * sp_count
    tile_size = TT * TH * TW
    mixed_query, mixed_key, mixed_value = (
        lax.all_to_all(part.reshape(tokens, feature_count), "sp", split_axis=1, concat_axis=0, tiled=True)
        for part in (queries, key_states, value_states)
    )
    own_width = mixed_query.shape[1]

    def head_tiles(mixed):
        grid = mixed.reshape(sp_count, frame_count, local_rows, token_cols, own_width).transpose(
            1, 0, 2, 3, 4
        )
        tiles = to_tiles(grid.reshape(frame_count, clip_rows, token_cols, own_width), tile_size)
        return tiles.reshape(tiles.shape[0], tile_size, local_heads, HD).transpose(2, 0, 1, 3)

    outputs = attend_tiles(
        head_tiles(mixed_query),
        head_tiles(mixed_key),
        head_tiles(mixed_value),
        lax.dynamic_slice_in_dim(kept_tiles, sp_rank * local_heads, local_heads, 0),
        lax.dynamic_slice_in_dim(kept_counts, sp_rank * local_heads, local_heads, 0),
    )
    tile_count = outputs.shape[0]
    attended = from_tiles(
        outputs.transpose(0, 2, 1, 3).reshape(tile_count, tile_size, own_width),
        frame_count,
        clip_rows,
        token_cols,
    )
    attended = attended.reshape(frame_count, sp_count, local_rows, token_cols, own_width).transpose(
        1, 0, 2, 3, 4
    )
    attended = attended.reshape(sp_count * tokens, own_width)
    restored = lax.all_to_all(attended, "sp", split_axis=0, concat_axis=1, tiled=True)
    latent = jnp.dot(restored, patch_weight, preferred_element_type=jnp.float32)
    latent = latent.astype(jnp.bfloat16)
    packed = jnp.concatenate([latent[: tokens // 2], latent[tokens // 2 :]], axis=1)
    grid = packed.reshape(frame_count // 2, local_rows, token_cols, 2 * NARROW)
    above = lax.ppermute(grid[:, -1], "sp", [(i, i + 1) for i in range(sp_count - 1)])
    below = lax.ppermute(grid[:, 0], "sp", [(i + 1, i) for i in range(sp_count - 1)])
    rims = [rim.reshape(-1, 2 * NARROW) for rim in (above, below)]
    return jnp.concatenate([packed, *rims], axis=0)


def spread_kernel(plain_ref, out_ref):
    empty = jnp.zeros((LAT, CH), jnp.bfloat16)
    for side in range(2):
        blocks = itertools.product(range(3), range(2), range(2), range(2), range(2))
        for position, (dt, rr, cc, u, w) in enumerate(blocks):
            dz = 2 * cc + w - (1 - side)
            for ro in range(2):
                dy = 2 * rr + u - ro
                inside = 0 <= dy < 3 and 0 <= dz < 3
                block = plain_ref[(dt * 3 + dy) * 3 + dz] if inside else empty
                out_ref[side, position * LAT : (position + 1) * LAT, ro * CH : (ro + 1) * CH] = block


def first_weights(first_kernel):
    return pl.pallas_call(
        spread_kernel,
        grid=(1,),
        in_specs=[pl.BlockSpec(first_kernel.shape, lambda i: (0, 0, 0))],
        out_specs=pl.BlockSpec((2, 12 * NARROW, 2 * CH), lambda i: (0, 0, 0)),
        out_shape=jax.ShapeDtypeStruct((2, 12 * NARROW, 2 * CH), jnp.bfloat16),
        name="spread_first_kernel",
    )(first_kernel)


def decode_kernel(
    frames,
    rows,
    cols,
    place_ref,
    message_refs,
    weight_hbm,
    shard_refs,
    out_ref,
    token_ref,
    pair_ref,
    first_ref,
    act_ref,
    wide_ref,
    weight_ref,
    kernel_ref,
    sems,
):
    at_first = place_ref[0] == 0
    at_last = place_ref[0] == place_ref[1] - 1
    step = place_ref[2]
    weight_copy = pltpu.make_async_copy(weight_hbm, weight_ref, sems.at[0])
    weight_copy.start()
    if len(shard_refs) == 1:
        shard_copies = [pltpu.make_async_copy(shard_refs[0], kernel_ref, sems.at[1])]
    else:
        shard_copies = [
            pltpu.make_async_copy(ref, kernel_ref.at[place_ref[3 + k]], sems.at[1 + k])
            for k, ref in enumerate(shard_refs)
        ]
    direct = place_ref[3 + len(shard_refs)]

    def each_shard(act):
        for k, copy in enumerate(shard_copies):
            if len(shard_copies) - k > 2 or len(shard_copies) == 1:
                act(copy)
            else:
                pl.when(direct == len(shard_copies) - 1 - k)(functools.partial(act, copy))

    each_shard(lambda copy: copy.start())

    lane = lax.broadcasted_iota(jnp.int32, (1, 1, 1, 2 * NARROW), 3)

    message = message_refs[0][...]
    for k in range(1, len(message_refs)):
        message = jnp.where(step == k, message_refs[k][...], message)
    own_count = frames // 2 * rows * cols
    rim_count = frames // 2 * cols

    def unpacked(packed, height):
        plain = packed.astype(jnp.float32)
        turned = pltpu.roll(plain, NARROW, 1)
        shape = (frames // 2, height, cols, 2 * NARROW)
        plain, turned = plain.reshape(shape), turned.reshape(shape)
        early = jnp.where(lane < NARROW, plain, turned)
        late = jnp.where(lane < NARROW, turned, plain)
        return jnp.concatenate([early, late], axis=0)

    token_ref[:, 1 : 1 + rows, 8 : 8 + cols, :] = unpacked(message[:own_count], rows)
    above = unpacked(message[own_count : own_count + rim_count], 1)
    below = unpacked(message[-rim_count:], 1)
    for f in range(frames):
        edge = pltpu.roll(token_ref[f, 1, 8 : 8 + cols, :], 2 * LAT, 1)
        token_ref[f, 0, 8 : 8 + cols, :] = jnp.where(at_first, edge, above[f, 0])
        edge = pltpu.roll(token_ref[f, rows, 8 : 8 + cols, :], 2 * NARROW - 2 * LAT, 1)
        token_ref[f, rows + 1, 8 : 8 + cols, :] = jnp.where(at_last, edge, below[f, 0])
    for f in range(frames):
        for r in range(rows + 2):
            start = token_ref[f, r, 8:16, :]
            token_ref[f, r, 7:8, :] = pltpu.roll(start, LAT, 1)[0:1]
            end = token_ref[f, r, cols : 8 + cols, :]
            token_ref[f, r, 8 + cols : 9 + cols, :] = pltpu.roll(end, 2 * NARROW - LAT, 1)[7:8]

    for side in range(2):
        pair = jnp.where(
            lane < NARROW,
            token_ref[:, :, 7 + side : 7 + side + cols, :],
            token_ref[:, :, 8 + side : 8 + side + cols, :],
        ).astype(jnp.bfloat16)
        pair_ref[side, 2:] = pair
        pair_ref[side, 0] = pair[0]
        pair_ref[side, 1] = pair[0]

    weight_copy.wait()
    gaps = rows + 1
    for side in range(2):
        columns = jnp.concatenate(
            [
                pair_ref[side, dt : dt + frames, rr : rr + gaps].reshape(frames * gaps * cols, 2 * NARROW)
                for dt in range(3)
                for rr in range(2)
            ],
            axis=1,
        )
        first = jnp.dot(columns, weight_ref[side], preferred_element_type=jnp.float32) * VAE_SCALE
        first = first.astype(jnp.bfloat16).astype(jnp.float32)
        act = first / (1.0 + jnp.exp(-first))
        first = first.reshape(frames, gaps, cols, 2 * CH)
        act = act.reshape(frames, gaps, cols, 2 * CH)
        for f in range(frames):
            for g in range(gaps):
                for ro in range(2):
                    for part in range(CH // 128):
                        lanes = slice(ro * CH + part * 128, ro * CH + part * 128 + 128)
                        row = 2 * g + ro
                        into = pl.ds(8 + side, cols, stride=2)
                        first_ref[part, f, row, into, :] = first[f, g, :, lanes]
                        act_ref[part, f, row, into, :] = act[f, g, :, lanes]

    width = 2 * cols
    height = 2 * rows
    for part in range(CH // 128):
        for f in range(frames):
            act_ref[part, f, 0] = jnp.where(at_first, act_ref[part, f, 1], act_ref[part, f, 0])
            act_ref[part, f, height + 1] = jnp.where(
                at_last, act_ref[part, f, height], act_ref[part, f, height + 1]
            )
        act_ref[part, :, :, 7:8, :] = act_ref[part, :, :, 8:9, :]
        act_ref[part, :, :, 8 + width : 9 + width, :] = act_ref[part, :, :, 7 + width : 8 + width, :]
        for dz in range(3):
            lanes = slice(dz * CH + part * 128, dz * CH + part * 128 + 128)
            shifted = act_ref[part, :, :, 7 + dz : 7 + dz + width, :].astype(jnp.bfloat16)
            wide_ref[2:, :, :, lanes] = shifted
            wide_ref[0, :, :, lanes] = shifted[0]
            wide_ref[1, :, :, lanes] = shifted[0]

    each_shard(lambda copy: copy.wait())
    cells = frames * height * width
    total = None
    for dt in range(3):
        for dy in range(3):
            window = wide_ref[dt : dt + frames, dy : dy + height].reshape(cells, 3 * CH)
            weight = jnp.concatenate(
                [kernel_ref[:, (dt * 3 + dy) * 3 + dz].reshape(CH, CH) for dz in range(3)], axis=0
            )
            product = jnp.dot(window, weight, preferred_element_type=jnp.float32)
            total = product if total is None else total + product
    total = total.reshape(frames, height, width, CH)
    for part in range(CH // 128):
        lanes = slice(part * 128, part * 128 + 128)
        residual = first_ref[part, :, 1 : 1 + height, 8 : 8 + width, :]
        out_ref[:, :, :, lanes] = (total[:, :, :, lanes] + residual).astype(jnp.bfloat16)


def decode(frames, rows, cols, place, messages, weights, groups, shards):
    height, width = 2 * rows, 2 * cols
    count = len(messages)
    taps, depth = shards[0].shape[-3:-1]

    def whole(shape):
        return pl.BlockSpec(shape, lambda i, place: (0,) * len(shape))

    def body(place_ref, *refs):
        message_refs, refs = refs[:count], refs[count:]
        weight_hbm, shard_refs = refs[0], refs[1 : 1 + len(shards)]
        decode_kernel(
            frames, rows, cols, place_ref, message_refs, weight_hbm, shard_refs, *refs[1 + len(shards) :]
        )

    grid_spec = pltpu.PrefetchScalarGridSpec(
        num_scalar_prefetch=1,
        grid=(1,),
        in_specs=[whole(part.shape) for part in messages]
        + [pl.BlockSpec(memory_space=pl.ANY)] * (1 + len(shards)),
        out_specs=whole((frames, height, width, CH)),
        scratch_shapes=[
            pltpu.VMEM((frames, rows + 2, cols + 16, 2 * NARROW), jnp.float32),
            pltpu.VMEM((2, frames + 2, rows + 2, cols, 2 * NARROW), jnp.bfloat16),
            pltpu.VMEM((CH // 128, frames, height + 2, width + 16, 128), jnp.float32),
            pltpu.VMEM((CH // 128, frames, height + 2, width + 16, 128), jnp.float32),
            pltpu.VMEM((frames + 2, height + 2, width, 3 * CH), jnp.bfloat16),
            pltpu.VMEM(weights.shape, jnp.bfloat16),
            pltpu.VMEM((groups, taps, depth, CH), jnp.bfloat16),
            pltpu.SemaphoreType.DMA((1 + len(shards),)),
        ],
    )
    return pl.pallas_call(
        body,
        grid_spec=grid_spec,
        out_shape=jax.ShapeDtypeStruct((frames, height, width, CH), jnp.bfloat16),
        compiler_params=pltpu.CompilerParams(vmem_limit_bytes=32 * MIB),
        cost_estimate=pl.CostEstimate(
            flops=2 * frames * height * width * 27 * CH * CH,
            bytes_accessed=27 * CH * CH * 2 + frames * height * width * CH * 2,
            transcendentals=frames * height * width * CH,
        ),
        name="decode_block",
    )(place, *messages, weights, *shards)


def trade_shards(shard, segment_count):
    segments = range(segment_count)
    near = [(s * 4 + g, s * 4 + (g ^ (1 + s % 2))) for s in segments for g in range(4)]
    far = [(s * 4 + g, s * 4 + (g ^ 3)) for s in segments for g in ((1, 2), (0, 3))[s % 2]]
    return [lax.ppermute(shard, ("segment", "grp"), pairs) for pairs in (near, far)]


def swap_shards(near, far, ready, segment_count):
    near, far, _ = lax.optimization_barrier((near, far, ready))
    segments = range(segment_count)
    pairs = [(s * 4 + g, (s ^ 1) * 4 + g) for s in segments for g in ((1, 2), (0, 3))[s % 2]]
    return (
        near,
        lax.ppermute(near, "segment", [(s, s ^ 1) for s in segments]),
        far,
        lax.ppermute(far, ("segment", "grp"), pairs),
    )


def local(
    queries,
    key_states,
    value_states,
    kept_tiles,
    kept_counts,
    patch_weight,
    decode_slot,
    first_kernel,
    second_kernel,
):
    frames, rows, cols = queries.shape[2:5]
    sp_count = lax.axis_size("sp")
    sp_rank = lax.axis_index("sp")
    segment_count = lax.axis_size("segment")
    segment_rank = lax.axis_index("segment")

    weights = first_weights(first_kernel)
    picks = (decode_slot == segment_rank).astype(jnp.int32)
    source = jnp.sum(jnp.arange(segment_count, dtype=jnp.int32) * picks)
    step = lax.rem(segment_rank - source + segment_count, segment_count)
    group_count = lax.axis_size("grp")
    group = lax.axis_index("grp")
    core = lax.rem(segment_rank, 2)
    line = group_count == 4 and segment_count % 2 == 0
    places = [sp_rank, jnp.int32(sp_count), step]
    if line:
        inner = jnp.logical_or(group == 1, group == 2)
        places += [group, group ^ (1 + core), group ^ (2 - core), group ^ 3, group ^ 3]
        places.append((inner == (core == 0)).astype(jnp.int32))
        traded = trade_shards(second_kernel, segment_count)
    else:
        places += [jnp.int32(0)] * 2
    place = jnp.stack(places).astype(jnp.int32)

    arguments = (queries, key_states, value_states, kept_tiles, kept_counts, patch_weight)
    if sp_count == 2 and rows * sp_count == TH and frames == TT:
        message, got, (weights, place) = split_attention(*arguments, (weights, place))
    else:
        message = got = exchanged_attention(*arguments)
    if line:
        shards = [second_kernel, *swap_shards(*traded, got, segment_count)]
    else:
        shards = [lax.all_gather(second_kernel, "grp", axis=0, tiled=False)]
    messages = [message] + [
        lax.ppermute(message, "segment", [(i, (i + step) % segment_count) for i in range(segment_count)])
        for step in range(1, segment_count)
    ]
    return decode(frames, rows, cols, place, messages, weights, group_count, shards)[None, None]


def solution(mesh):
    return jax.shard_map(
        local,
        mesh=mesh,
        in_specs=(
            P("segment", "grp", None, "sp", None, None),
            P("segment", "grp", None, "sp", None, None),
            P("segment", "grp", None, "sp", None, None),
            P(),
            P(),
            P(),
            P(),
            P(),
            P(None, "grp", None),
        ),
        out_specs=P("segment", "grp", None, "sp", None, None),
        check_vma=False,
    )
```

```python
import functools
import itertools

import jax
import jax.numpy as jnp
from jax import lax
from jax.experimental import pallas as pl
from jax.experimental.pallas import tpu as pltpu
from jax.sharding import PartitionSpec as P

HEADS = 16
HD = 128
LAT = 16
CH = 256
TT = 4
TH = 8
TW = 8

VAE_SCALE = 1.0 / 0.476986
SCORE_UNIT = HD**-0.5 * 1.4426950408889634
HEAD_BLOCK = 4
HEAD_PARTS = (16,)
NARROW = 4 * LAT
MIB = 1 << 20


def partial_head(head, q, k, v, tiles_ref, counts_ref):
    keys, queries = k.shape[0], q.shape[0]
    tile_count, keep = tiles_ref.shape[:2]
    scores = lax.dot_general(k, q, (((1,), (1,)), ((), ())), preferred_element_type=jnp.float32)
    lane = lax.broadcasted_iota(jnp.int32, (1, queries), 1)
    lane_tile = lax.rem(lax.div(lane, TW), tile_count)
    rows = []
    for key_tile in range(tile_count):
        row = jnp.zeros((1, queries), jnp.float32)
        for query_tile in range(tile_count):
            live = jnp.bool_(False)
            for slot in range(keep):
                here = jnp.logical_and(
                    tiles_ref[query_tile, slot, head] == key_tile, slot < counts_ref[query_tile, head]
                )
                live = jnp.logical_or(live, here)
            row = jnp.where(lane_tile == query_tile, jnp.where(live, 0.0, -1e30), row)
        rows.append(row[None])
    bias = jnp.concatenate(rows, axis=0)
    scores = scores.reshape(keys // (tile_count * TW), tile_count, TW, queries) + bias[None]
    scores = scores.reshape(keys, queries)
    top = jnp.max(scores, axis=0, keepdims=True)
    power = jnp.exp2((scores - top) * SCORE_UNIT)
    total = jnp.sum(power, axis=0, keepdims=True)
    out = lax.dot_general(
        v, power.astype(jnp.bfloat16), (((0,), (0,)), ((), ())), preferred_element_type=jnp.float32
    )
    return top * SCORE_UNIT, total, out


def row_choice(frames, rows, cols, row, lanes, start):
    token = lax.broadcasted_iota(jnp.int32, (frames * rows * cols, lanes), 0)
    lane = lax.broadcasted_iota(jnp.int32, (frames * rows * cols, lanes), 1) - start
    wanted = lax.div(lane, cols) * (rows * cols) + row * cols + lax.rem(lane, cols)
    inside = jnp.logical_and(lane >= 0, lane < frames * cols)
    return jnp.where(jnp.logical_and(inside, token == wanted), 1.0, 0.0)


def attend_kernel(
    offset, grid, rank_ref, tiles_ref, counts_ref, q_ref, k_ref, v_ref, w_ref, level_ref, mapped_ref, *note_refs
):
    block = pl.program_id(0)
    if note_refs:
        note_ref = note_refs[0]
        frames, rows, cols = grid
        near = jnp.where(rank_ref[0] == 0, rows - 1, 0)
        choices = [
            row_choice(frames, rows, cols, near, 2 * NARROW, start).astype(jnp.bfloat16)
            for start in (0, NARROW)
        ]
    for i in range(HEAD_BLOCK):
        cols = slice(i * HD, (i + 1) * HD)
        row = block * HEAD_BLOCK + i
        top, total, out = partial_head(
            offset + row, q_ref[:, cols], k_ref[:, cols], v_ref[:, cols], tiles_ref, counts_ref
        )
        out = (out / total).astype(jnp.bfloat16)
        level_ref[pl.ds(row, 1), :] = top + jnp.log2(total)
        mapped = jnp.dot(w_ref[:, cols], out, preferred_element_type=jnp.float32)
        mapped_ref[i] = mapped
        if note_refs:
            rim = jnp.dot(mapped.astype(jnp.bfloat16), choices[i % 2], preferred_element_type=jnp.float32)
            if i % 2 == 0:
                even = rim
            else:
                pair = pl.multiple_of((row // 2) * NARROW, NARROW)
                note_ref[pl.ds(pair, NARROW), :] = (even + rim).astype(jnp.bfloat16)
    if note_refs:

        @pl.when(block == pl.num_programs(0) - 1)
        def _():
            rest = level_ref[...]
            rest = jnp.concatenate([rest[:, :128], rest[:, 128:]], axis=0)
            start = HEADS // 2 * NARROW
            for _ in range(3):
                part = rest.astype(jnp.bfloat16)
                note_ref[start : start + 2 * HEADS, :] = part
                rest = rest - part.astype(jnp.float32)
                start += 2 * HEADS


def combine_kernel(parts, note_ref, *refs):
    level_refs, mapped_refs, sent_ref = refs[:parts], refs[parts : 2 * parts], refs[-1]
    start = HEADS // 2 * NARROW
    theirs = [note_ref[start + k * 2 * HEADS : start + (k + 1) * 2 * HEADS, :] for k in range(3)]
    theirs = theirs[0].astype(jnp.float32) + theirs[1].astype(jnp.float32) + theirs[2].astype(jnp.float32)
    theirs = jnp.concatenate([theirs[:HEADS], theirs[HEADS:]], axis=1)
    mine = jnp.concatenate([ref[...] for ref in level_refs], axis=0)
    high = jnp.maximum(mine, theirs)
    level = high + jnp.log2(jnp.exp2(mine - high) + jnp.exp2(theirs - high))
    mine = jnp.exp2(mine - level)
    total = None
    head = 0
    for ref in mapped_refs:
        for i in range(ref.shape[0]):
            term = ref[i] * mine[head : head + 1]
            total = term if total is None else total + term
            head += 1
    theirs = jnp.exp2(theirs - level)
    high = theirs.astype(jnp.bfloat16)
    sent_ref[0:NARROW, :] = total.astype(jnp.bfloat16)
    sent_ref[NARROW : NARROW + HEADS, :] = high
    sent_ref[NARROW + HEADS :, :] = (theirs - high.astype(jnp.float32)).astype(jnp.bfloat16)


def unpacked_share(sent_ref):
    sent = sent_ref[...].astype(jnp.float32)
    return sent[:NARROW], sent[NARROW : NARROW + HEADS] + sent[NARROW + HEADS :]


def beside_kernel(grid, rank_ref, sent_ref, note_ref, beside_ref):
    frames, rows, cols = grid
    near = jnp.where(rank_ref[0] == 0, 0, rows - 1)
    choice = row_choice(frames, rows, cols, near, frames * cols, 0)
    near_row = jnp.dot(
        sent_ref[...], choice.astype(jnp.bfloat16), preferred_element_type=jnp.float32
    )
    beside = near_row[:NARROW]
    weights = near_row[NARROW : NARROW + HEADS] + near_row[NARROW + HEADS :]
    for head in range(HEADS):
        side = head % 2 * NARROW
        pair = head // 2 * NARROW
        mapped = note_ref[pair : pair + NARROW, side : side + NARROW].astype(jnp.float32)
        beside = beside + mapped * weights[head : head + 1]
    beside_ref[...] = packed_latents(beside)


def packed_latents(latents):
    half = latents.shape[1] // 2
    packed = jnp.concatenate([latents[:, :half], latents[:, half:]], axis=0)
    return packed.T.astype(jnp.bfloat16)


def merge_kernel(got_ref, mapped_ref, beside_ref, out_ref):
    total, weights = unpacked_share(got_ref)
    for head in range(HEADS):
        total = total + mapped_ref[head] * weights[head : head + 1]
    own = total.shape[1] // 2
    out_ref[0:own, :] = packed_latents(total)
    out_ref[own:, :] = beside_ref[...]


def split_attention(queries, key_states, value_states, kept_tiles, kept_counts, patch_weight, ready):
    frames, rows, cols, feature_count = queries.shape[2:]
    tokens = frames * rows * cols
    flat_query = queries.reshape(tokens, feature_count)
    flat_key = key_states.reshape(tokens, feature_count)
    flat_value = value_states.reshape(tokens, feature_count)
    swap = [(0, 1), (1, 0)]
    ends = list(itertools.accumulate(HEAD_PARTS))
    starts = [0] + ends[:-1]
    parts = []
    source = flat_query
    for start, end in zip(starts, ends):
        parts.append(source[:, start * HD : end * HD])
        if start == 0:
            source, _ = lax.optimization_barrier((source, parts[0]))
    other_queries = [lax.ppermute(part, "sp", swap) for part in parts]
    kept_tiles = kept_tiles.transpose(1, 2, 0)
    kept_counts = kept_counts.T
    patch_weight = patch_weight.T
    smem = pl.BlockSpec(memory_space=pltpu.SMEM)
    params = pltpu.CompilerParams(
        dimension_semantics=("arbitrary",), vmem_limit_bytes=24 * MIB
    )

    def whole(*shape):
        return pl.BlockSpec(shape, lambda i: (0,) * len(shape))

    grid = (frames, rows, cols)
    rank = lax.axis_index("sp").astype(jnp.int32).reshape(1)
    rim_tokens = frames * cols

    note_rows = HEADS // 2 * NARROW + 6 * HEADS

    def attend(part, start, name, with_note=False):
        count = part.shape[1] // HD
        first_block = start // HEAD_BLOCK
        heads = pl.BlockSpec((tokens, HEAD_BLOCK * HD), lambda i: (0, first_block + i))
        return pl.pallas_call(
            functools.partial(attend_kernel, start, grid),
            grid=(count // HEAD_BLOCK,),
            in_specs=[
                smem,
                smem,
                smem,
                pl.BlockSpec((tokens, HEAD_BLOCK * HD), lambda i: (0, i)),
                heads,
                heads,
                pl.BlockSpec((NARROW, HEAD_BLOCK * HD), lambda i: (0, first_block + i)),
            ],
            out_specs=[
                whole(count, tokens),
                pl.BlockSpec((HEAD_BLOCK, NARROW, tokens), lambda i: (i, 0, 0)),
                whole(note_rows, 2 * NARROW),
            ][: 3 if with_note else 2],
            out_shape=[
                jax.ShapeDtypeStruct((count, tokens), jnp.float32),
                jax.ShapeDtypeStruct((count, NARROW, tokens), jnp.float32),
                jax.ShapeDtypeStruct((note_rows, 2 * NARROW), jnp.bfloat16),
            ][: 3 if with_note else 2],
            compiler_params=params,
            cost_estimate=pl.CostEstimate(
                flops=count * tokens, bytes_accessed=count * tokens, transcendentals=0
            ),
            name=name,
        )(rank, kept_tiles, kept_counts, part, flat_key, flat_value, patch_weight)

    flat_query, *_ = lax.optimization_barrier((flat_query, *parts))
    _, mapped, note = attend(flat_query, 0, "own_queries", with_note=True)
    note, ready = lax.optimization_barrier((note, ready))
    other_note = lax.ppermute(note, "sp", swap)
    levels, shares = [], []
    for part, start in zip(other_queries, starts):
        part, _ = lax.optimization_barrier((part, levels[-1] if levels else note))
        part_level, share = attend(part, start, "other_queries")
        levels.append(part_level)
        shares.append(share)
    operands = (other_note, *levels, *shares)
    sent = pl.pallas_call(
        functools.partial(combine_kernel, len(levels)),
        grid=(1,),
        in_specs=[whole(*part.shape) for part in operands],
        out_specs=whole(NARROW + 2 * HEADS, tokens),
        out_shape=jax.ShapeDtypeStruct((NARROW + 2 * HEADS, tokens), jnp.bfloat16),
        compiler_params=params,
        name="combine",
    )(*operands)
    got = lax.ppermute(sent, "sp", swap)
    beside = pl.pallas_call(
        functools.partial(beside_kernel, grid),
        grid=(1,),
        in_specs=[smem, whole(*sent.shape), whole(*other_note.shape)],
        out_specs=whole(rim_tokens // 2, 2 * NARROW),
        out_shape=jax.ShapeDtypeStruct((rim_tokens // 2, 2 * NARROW), jnp.bfloat16),
        compiler_params=params,
        name="beside",
    )(rank, sent, other_note)
    message = pl.pallas_call(
        merge_kernel,
        grid=(1,),
        in_specs=[whole(*part.shape) for part in (got, mapped, beside)],
        out_specs=whole((tokens + rim_tokens) // 2, 2 * NARROW),
        out_shape=jax.ShapeDtypeStruct(((tokens + rim_tokens) // 2, 2 * NARROW), jnp.bfloat16),
        compiler_params=params,
        name="merge",
    )(got, mapped, beside)
    return message, ready


def to_tiles(grid, tile_size):
    frame_count, row_count, col_count, feature_width = grid.shape
    tiled = grid.reshape(
        frame_count // TT, TT, row_count // TH, TH, col_count // TW, TW, feature_width
    ).transpose(0, 2, 4, 1, 3, 5, 6)
    return tiled.reshape(-1, tile_size, feature_width)


def from_tiles(tiles, frame_count, row_count, col_count):
    feature_width = tiles.shape[-1]
    grid = tiles.reshape(
        frame_count // TT, row_count // TH, col_count // TW, TT, TH, TW, feature_width
    ).transpose(0, 3, 1, 4, 2, 5, 6)
    return grid.reshape(frame_count, row_count, col_count, feature_width)


def attend_tiles(query_tiles, key_tiles, value_tiles, tile_index, live_count):
    head_count = query_tiles.shape[0]
    tile_size = query_tiles.shape[2]
    head_size = query_tiles.shape[3]
    keep_count = tile_index.shape[2]

    def one_tile(packed):
        query_block, index_block, count_block = packed
        key_sel = jax.vmap(lambda source, picks: source[picks])(key_tiles, index_block).reshape(
            head_count, keep_count * tile_size, head_size
        )
        value_sel = jax.vmap(lambda source, picks: source[picks])(value_tiles, index_block).reshape(
            head_count, keep_count * tile_size, head_size
        )
        scores = jnp.einsum(
            "hqd,hkd->hqk", query_block, key_sel, preferred_element_type=jnp.float32
        ) * head_size ** (-0.5)
        live = jnp.arange(keep_count, dtype=jnp.int32)[None, :] < count_block[:, None]
        live = jnp.repeat(live, tile_size, axis=1)[:, None, :]
        scores = jnp.where(live, scores, -1e30)
        row_top = jnp.max(scores, axis=-1, keepdims=True)
        exponent = jnp.where(live, jnp.exp(scores - row_top), 0.0)
        weights = (exponent / jnp.sum(exponent, axis=-1, keepdims=True)).astype(jnp.bfloat16)
        result = jnp.einsum("hqk,hkd->hqd", weights, value_sel, preferred_element_type=jnp.float32)
        return result.astype(jnp.bfloat16)

    return lax.map(
        one_tile,
        (
            query_tiles.transpose(1, 0, 2, 3),
            tile_index.transpose(1, 0, 2),
            live_count.transpose(1, 0),
        ),
    )


def exchanged_attention(queries, key_states, value_states, kept_tiles, kept_counts, patch_weight):
    frame_count, local_rows, token_cols, feature_count = queries.shape[2:]
    tokens = frame_count * local_rows * token_cols
    sp_count = lax.axis_size("sp")
    sp_rank = lax.axis_index("sp")
    local_heads = HEADS // sp_count
    clip_rows = local_rows * sp_count
    tile_size = TT * TH * TW
    mixed_query, mixed_key, mixed_value = (
        lax.all_to_all(part.reshape(tokens, feature_count), "sp", split_axis=1, concat_axis=0, tiled=True)
        for part in (queries, key_states, value_states)
    )
    own_width = mixed_query.shape[1]

    def head_tiles(mixed):
        grid = mixed.reshape(sp_count, frame_count, local_rows, token_cols, own_width).transpose(
            1, 0, 2, 3, 4
        )
        tiles = to_tiles(grid.reshape(frame_count, clip_rows, token_cols, own_width), tile_size)
        return tiles.reshape(tiles.shape[0], tile_size, local_heads, HD).transpose(2, 0, 1, 3)

    outputs = attend_tiles(
        head_tiles(mixed_query),
        head_tiles(mixed_key),
        head_tiles(mixed_value),
        lax.dynamic_slice_in_dim(kept_tiles, sp_rank * local_heads, local_heads, 0),
        lax.dynamic_slice_in_dim(kept_counts, sp_rank * local_heads, local_heads, 0),
    )
    tile_count = outputs.shape[0]
    attended = from_tiles(
        outputs.transpose(0, 2, 1, 3).reshape(tile_count, tile_size, own_width),
        frame_count,
        clip_rows,
        token_cols,
    )
    attended = attended.reshape(frame_count, sp_count, local_rows, token_cols, own_width).transpose(
        1, 0, 2, 3, 4
    )
    attended = attended.reshape(sp_count * tokens, own_width)
    restored = lax.all_to_all(attended, "sp", split_axis=0, concat_axis=1, tiled=True)
    latent = jnp.dot(restored, patch_weight, preferred_element_type=jnp.float32)
    latent = latent.astype(jnp.bfloat16)
    packed = jnp.concatenate([latent[: tokens // 2], latent[tokens // 2 :]], axis=1)
    grid = packed.reshape(frame_count // 2, local_rows, token_cols, 2 * NARROW)
    above = lax.ppermute(grid[:, -1], "sp", [(i, i + 1) for i in range(sp_count - 1)])
    below = lax.ppermute(grid[:, 0], "sp", [(i + 1, i) for i in range(sp_count - 1)])
    rims = [rim.reshape(-1, 2 * NARROW) for rim in (above, below)]
    return jnp.concatenate([packed, *rims], axis=0)


def spread_kernel(plain_ref, out_ref):
    empty = jnp.zeros((LAT, CH), jnp.bfloat16)
    for side in range(2):
        blocks = itertools.product(range(3), range(2), range(2), range(2), range(2))
        for position, (dt, rr, cc, u, w) in enumerate(blocks):
            dz = 2 * cc + w - (1 - side)
            for ro in range(2):
                dy = 2 * rr + u - ro
                inside = 0 <= dy < 3 and 0 <= dz < 3
                block = plain_ref[(dt * 3 + dy) * 3 + dz] if inside else empty
                out_ref[side, position * LAT : (position + 1) * LAT, ro * CH : (ro + 1) * CH] = block


def first_weights(first_kernel):
    return pl.pallas_call(
        spread_kernel,
        grid=(1,),
        in_specs=[pl.BlockSpec(first_kernel.shape, lambda i: (0, 0, 0))],
        out_specs=pl.BlockSpec((2, 12 * NARROW, 2 * CH), lambda i: (0, 0, 0)),
        out_shape=jax.ShapeDtypeStruct((2, 12 * NARROW, 2 * CH), jnp.bfloat16),
        name="spread_first_kernel",
    )(first_kernel)


def decode_kernel(
    frames,
    rows,
    cols,
    place_ref,
    message_refs,
    weight_hbm,
    shard_refs,
    out_ref,
    token_ref,
    pair_ref,
    first_ref,
    act_ref,
    wide_ref,
    weight_ref,
    kernel_ref,
    sems,
):
    at_first = place_ref[0] == 0
    at_last = place_ref[0] == place_ref[1] - 1
    step = place_ref[2]
    weight_copy = pltpu.make_async_copy(weight_hbm, weight_ref, sems.at[0])
    weight_copy.start()
    if len(shard_refs) == 1:
        shard_copies = [pltpu.make_async_copy(shard_refs[0], kernel_ref, sems.at[1])]
    else:
        shard_copies = [
            pltpu.make_async_copy(ref, kernel_ref.at[place_ref[3 + k]], sems.at[1 + k])
            for k, ref in enumerate(shard_refs)
        ]
    direct = place_ref[3 + len(shard_refs)]

    def each_shard(act):
        for k, copy in enumerate(shard_copies):
            if len(shard_copies) - k > 2 or len(shard_copies) == 1:
                act(copy)
            else:
                pl.when(direct == len(shard_copies) - 1 - k)(functools.partial(act, copy))

    each_shard(lambda copy: copy.start())

    lane = lax.broadcasted_iota(jnp.int32, (1, 1, 1, 2 * NARROW), 3)

    message = message_refs[0][...]
    for k in range(1, len(message_refs)):
        message = jnp.where(step == k, message_refs[k][...], message)
    own_count = frames // 2 * rows * cols
    rim_count = frames // 2 * cols

    def unpacked(packed, height):
        plain = packed.astype(jnp.float32)
        turned = pltpu.roll(plain, NARROW, 1)
        shape = (frames // 2, height, cols, 2 * NARROW)
        plain, turned = plain.reshape(shape), turned.reshape(shape)
        early = jnp.where(lane < NARROW, plain, turned)
        late = jnp.where(lane < NARROW, turned, plain)
        return jnp.concatenate([early, late], axis=0)

    token_ref[:, 1 : 1 + rows, 8 : 8 + cols, :] = unpacked(message[:own_count], rows)
    above = unpacked(message[own_count : own_count + rim_count], 1)
    below = unpacked(message[-rim_count:], 1)
    for f in range(frames):
        edge = pltpu.roll(token_ref[f, 1, 8 : 8 + cols, :], 2 * LAT, 1)
        token_ref[f, 0, 8 : 8 + cols, :] = jnp.where(at_first, edge, above[f, 0])
        edge = pltpu.roll(token_ref[f, rows, 8 : 8 + cols, :], 2 * NARROW - 2 * LAT, 1)
        token_ref[f, rows + 1, 8 : 8 + cols, :] = jnp.where(at_last, edge, below[f, 0])
    for f in range(frames):
        for r in range(rows + 2):
            start = token_ref[f, r, 8:16, :]
            token_ref[f, r, 7:8, :] = pltpu.roll(start, LAT, 1)[0:1]
            end = token_ref[f, r, cols : 8 + cols, :]
            token_ref[f, r, 8 + cols : 9 + cols, :] = pltpu.roll(end, 2 * NARROW - LAT, 1)[7:8]

    for side in range(2):
        pair = jnp.where(
            lane < NARROW,
            token_ref[:, :, 7 + side : 7 + side + cols, :],
            token_ref[:, :, 8 + side : 8 + side + cols, :],
        ).astype(jnp.bfloat16)
        pair_ref[side, 2:] = pair
        pair_ref[side, 0] = pair[0]
        pair_ref[side, 1] = pair[0]

    weight_copy.wait()
    gaps = rows + 1
    for side in range(2):
        columns = jnp.concatenate(
            [
                pair_ref[side, dt : dt + frames, rr : rr + gaps].reshape(frames * gaps * cols, 2 * NARROW)
                for dt in range(3)
                for rr in range(2)
            ],
            axis=1,
        )
        first = jnp.dot(columns, weight_ref[side], preferred_element_type=jnp.float32) * VAE_SCALE
        first = first.astype(jnp.bfloat16).astype(jnp.float32)
        act = first / (1.0 + jnp.exp(-first))
        first = first.reshape(frames, gaps, cols, 2 * CH)
        act = act.reshape(frames, gaps, cols, 2 * CH)
        for f in range(frames):
            for g in range(gaps):
                for ro in range(2):
                    for part in range(CH // 128):
                        lanes = slice(ro * CH + part * 128, ro * CH + part * 128 + 128)
                        row = 2 * g + ro
                        into = pl.ds(8 + side, cols, stride=2)
                        first_ref[part, f, row, into, :] = first[f, g, :, lanes]
                        act_ref[part, f, row, into, :] = act[f, g, :, lanes]

    width = 2 * cols
    height = 2 * rows
    for part in range(CH // 128):
        for f in range(frames):
            act_ref[part, f, 0] = jnp.where(at_first, act_ref[part, f, 1], act_ref[part, f, 0])
            act_ref[part, f, height + 1] = jnp.where(
                at_last, act_ref[part, f, height], act_ref[part, f, height + 1]
            )
        act_ref[part, :, :, 7:8, :] = act_ref[part, :, :, 8:9, :]
        act_ref[part, :, :, 8 + width : 9 + width, :] = act_ref[part, :, :, 7 + width : 8 + width, :]
        for dz in range(3):
            lanes = slice(dz * CH + part * 128, dz * CH + part * 128 + 128)
            shifted = act_ref[part, :, :, 7 + dz : 7 + dz + width, :].astype(jnp.bfloat16)
            wide_ref[2:, :, :, lanes] = shifted
            wide_ref[0, :, :, lanes] = shifted[0]
            wide_ref[1, :, :, lanes] = shifted[0]

    each_shard(lambda copy: copy.wait())
    cells = frames * height * width
    total = None
    for dt in range(3):
        for dy in range(3):
            window = wide_ref[dt : dt + frames, dy : dy + height].reshape(cells, 3 * CH)
            weight = jnp.concatenate(
                [kernel_ref[:, (dt * 3 + dy) * 3 + dz].reshape(CH, CH) for dz in range(3)], axis=0
            )
            product = jnp.dot(window, weight, preferred_element_type=jnp.float32)
            total = product if total is None else total + product
    total = total.reshape(frames, height, width, CH)
    for part in range(CH // 128):
        lanes = slice(part * 128, part * 128 + 128)
        residual = first_ref[part, :, 1 : 1 + height, 8 : 8 + width, :]
        out_ref[:, :, :, lanes] = (total[:, :, :, lanes] + residual).astype(jnp.bfloat16)


def decode(frames, rows, cols, place, messages, weights, groups, shards):
    height, width = 2 * rows, 2 * cols
    count = len(messages)
    taps, depth = shards[0].shape[-3:-1]

    def whole(shape):
        return pl.BlockSpec(shape, lambda i, place: (0,) * len(shape))

    def body(place_ref, *refs):
        message_refs, refs = refs[:count], refs[count:]
        weight_hbm, shard_refs = refs[0], refs[1 : 1 + len(shards)]
        decode_kernel(
            frames, rows, cols, place_ref, message_refs, weight_hbm, shard_refs, *refs[1 + len(shards) :]
        )

    grid_spec = pltpu.PrefetchScalarGridSpec(
        num_scalar_prefetch=1,
        grid=(1,),
        in_specs=[whole(part.shape) for part in messages]
        + [pl.BlockSpec(memory_space=pl.ANY)] * (1 + len(shards)),
        out_specs=whole((frames, height, width, CH)),
        scratch_shapes=[
            pltpu.VMEM((frames, rows + 2, cols + 16, 2 * NARROW), jnp.float32),
            pltpu.VMEM((2, frames + 2, rows + 2, cols, 2 * NARROW), jnp.bfloat16),
            pltpu.VMEM((CH // 128, frames, height + 2, width + 16, 128), jnp.float32),
            pltpu.VMEM((CH // 128, frames, height + 2, width + 16, 128), jnp.float32),
            pltpu.VMEM((frames + 2, height + 2, width, 3 * CH), jnp.bfloat16),
            pltpu.VMEM(weights.shape, jnp.bfloat16),
            pltpu.VMEM((groups, taps, depth, CH), jnp.bfloat16),
            pltpu.SemaphoreType.DMA((1 + len(shards),)),
        ],
    )
    return pl.pallas_call(
        body,
        grid_spec=grid_spec,
        out_shape=jax.ShapeDtypeStruct((frames, height, width, CH), jnp.bfloat16),
        compiler_params=pltpu.CompilerParams(vmem_limit_bytes=32 * MIB),
        cost_estimate=pl.CostEstimate(
            flops=2 * frames * height * width * 27 * CH * CH,
            bytes_accessed=27 * CH * CH * 2 + frames * height * width * CH * 2,
            transcendentals=frames * height * width * CH,
        ),
        name="decode_block",
    )(place, *messages, weights, *shards)


def trade_shards(shard, segment_count):
    segments = range(segment_count)
    near = [(s * 4 + g, s * 4 + (g ^ (1 + s % 2))) for s in segments for g in range(4)]
    far = [(s * 4 + g, s * 4 + (g ^ 3)) for s in segments for g in ((1, 2), (0, 3))[s % 2]]
    return [lax.ppermute(shard, ("segment", "grp"), pairs) for pairs in (near, far)]


def swap_shards(near, far, ready, segment_count):
    near, far, _ = lax.optimization_barrier((near, far, ready))
    segments = range(segment_count)
    pairs = [(s * 4 + g, (s ^ 1) * 4 + g) for s in segments for g in ((1, 2), (0, 3))[s % 2]]
    return (
        near,
        lax.ppermute(near, "segment", [(s, s ^ 1) for s in segments]),
        far,
        lax.ppermute(far, ("segment", "grp"), pairs),
    )


def local(
    queries,
    key_states,
    value_states,
    kept_tiles,
    kept_counts,
    patch_weight,
    decode_slot,
    first_kernel,
    second_kernel,
):
    frames, rows, cols = queries.shape[2:5]
    sp_count = lax.axis_size("sp")
    sp_rank = lax.axis_index("sp")
    segment_count = lax.axis_size("segment")
    segment_rank = lax.axis_index("segment")

    weights = first_weights(first_kernel)
    picks = (decode_slot == segment_rank).astype(jnp.int32)
    source = jnp.sum(jnp.arange(segment_count, dtype=jnp.int32) * picks)
    step = lax.rem(segment_rank - source + segment_count, segment_count)
    group_count = lax.axis_size("grp")
    group = lax.axis_index("grp")
    core = lax.rem(segment_rank, 2)
    line = group_count == 4 and segment_count % 2 == 0
    places = [sp_rank, jnp.int32(sp_count), step]
    if line:
        inner = jnp.logical_or(group == 1, group == 2)
        places += [group, group ^ (1 + core), group ^ (2 - core), group ^ 3, group ^ 3]
        places.append((inner == (core == 0)).astype(jnp.int32))
        traded = trade_shards(second_kernel, segment_count)
    else:
        places += [jnp.int32(0)] * 2
    place = jnp.stack(places).astype(jnp.int32)

    arguments = (queries, key_states, value_states, kept_tiles, kept_counts, patch_weight)
    if sp_count == 2 and rows * sp_count == TH and frames == TT:
        message, (weights, place) = split_attention(*arguments, (weights, place))
    else:
        message = exchanged_attention(*arguments)
    if line:
        shards = [second_kernel, *swap_shards(*traded, message, segment_count)]
    else:
        shards = [lax.all_gather(second_kernel, "grp", axis=0, tiled=False)]
    messages = [message] + [
        lax.ppermute(message, "segment", [(i, (i + step) % segment_count) for i in range(segment_count)])
        for step in range(1, segment_count)
    ]
    return decode(frames, rows, cols, place, messages, weights, group_count, shards)[None, None]


def solution(mesh):
    return jax.shard_map(
        local,
        mesh=mesh,
        in_specs=(
            P("segment", "grp", None, "sp", None, None),
            P("segment", "grp", None, "sp", None, None),
            P("segment", "grp", None, "sp", None, None),
            P(),
            P(),
            P(),
            P(),
            P(),
            P(None, "grp", None),
        ),
        out_specs=P("segment", "grp", None, "sp", None, None),
        check_vma=False,
    )
```

```python
import functools
import itertools

import jax
import jax.numpy as jnp
from jax import lax
from jax.experimental import pallas as pl
from jax.experimental.pallas import tpu as pltpu
from jax.sharding import PartitionSpec as P

HEADS = 16
HD = 128
LAT = 16
CH = 256
TT = 4
TH = 8
TW = 8

VAE_SCALE = 1.0 / 0.476986
SCORE_UNIT = HD**-0.5 * 1.4426950408889634
HEAD_BLOCK = 4
HEAD_PARTS = (16,)
NARROW = 4 * LAT
MIB = 1 << 20


def partial_head(head, q, k, v, tiles_ref, counts_ref):
    keys, queries = k.shape[0], q.shape[0]
    tile_count, keep = tiles_ref.shape[:2]
    scores = lax.dot_general(k, q, (((1,), (1,)), ((), ())), preferred_element_type=jnp.float32)
    lane = lax.broadcasted_iota(jnp.int32, (1, queries), 1)
    lane_tile = lax.rem(lax.div(lane, TW), tile_count)
    rows = []
    for key_tile in range(tile_count):
        row = jnp.zeros((1, queries), jnp.float32)
        for query_tile in range(tile_count):
            live = jnp.bool_(False)
            for slot in range(keep):
                here = jnp.logical_and(
                    tiles_ref[query_tile, slot, head] == key_tile, slot < counts_ref[query_tile, head]
                )
                live = jnp.logical_or(live, here)
            row = jnp.where(lane_tile == query_tile, jnp.where(live, 0.0, -1e30), row)
        rows.append(row[None])
    bias = jnp.concatenate(rows, axis=0)
    scores = scores.reshape(keys // (tile_count * TW), tile_count, TW, queries) + bias[None]
    scores = scores.reshape(keys, queries)
    top = jnp.max(scores, axis=0, keepdims=True)
    power = jnp.exp2((scores - top) * SCORE_UNIT)
    total = jnp.sum(power, axis=0, keepdims=True)
    out = lax.dot_general(
        v, power.astype(jnp.bfloat16), (((0,), (0,)), ((), ())), preferred_element_type=jnp.float32
    )
    return top * SCORE_UNIT, total, out


def row_choice(frames, rows, cols, row, lanes, start):
    token = lax.broadcasted_iota(jnp.int32, (frames * rows * cols, lanes), 0)
    lane = lax.broadcasted_iota(jnp.int32, (frames * rows * cols, lanes), 1) - start
    wanted = lax.div(lane, cols) * (rows * cols) + row * cols + lax.rem(lane, cols)
    inside = jnp.logical_and(lane >= 0, lane < frames * cols)
    return jnp.where(jnp.logical_and(inside, token == wanted), 1.0, 0.0)


def attend_kernel(
    offset, grid, rank_ref, tiles_ref, counts_ref, q_ref, k_ref, v_ref, w_ref, level_ref, mapped_ref, *note_refs
):
    block = pl.program_id(0)
    if note_refs:
        note_ref = note_refs[0]
        frames, rows, cols = grid
        near = jnp.where(rank_ref[0] == 0, rows - 1, 0)
        choices = [
            row_choice(frames, rows, cols, near, 2 * NARROW, start).astype(jnp.bfloat16)
            for start in (0, NARROW)
        ]
    for i in range(HEAD_BLOCK):
        cols = slice(i * HD, (i + 1) * HD)
        row = block * HEAD_BLOCK + i
        top, total, out = partial_head(
            offset + row, q_ref[:, cols], k_ref[:, cols], v_ref[:, cols], tiles_ref, counts_ref
        )
        out = (out / total).astype(jnp.bfloat16)
        level_ref[pl.ds(row, 1), :] = top + jnp.log2(total)
        mapped = jnp.dot(w_ref[:, cols], out, preferred_element_type=jnp.float32)
        mapped_ref[i] = mapped
        if note_refs:
            rim = jnp.dot(mapped.astype(jnp.bfloat16), choices[i % 2], preferred_element_type=jnp.float32)
            if i % 2 == 0:
                even = rim
            else:
                pair = pl.multiple_of((row // 2) * NARROW, NARROW)
                note_ref[pl.ds(pair, NARROW), :] = (even + rim).astype(jnp.bfloat16)
    if note_refs:

        @pl.when(block == pl.num_programs(0) - 1)
        def _():
            rest = level_ref[...]
            rest = jnp.concatenate([rest[:, :128], rest[:, 128:]], axis=0)
            start = HEADS // 2 * NARROW
            for _ in range(3):
                part = rest.astype(jnp.bfloat16)
                note_ref[start : start + 2 * HEADS, :] = part
                rest = rest - part.astype(jnp.float32)
                start += 2 * HEADS


def combine_kernel(parts, note_ref, *refs):
    level_refs, mapped_refs, sent_ref = refs[:parts], refs[parts : 2 * parts], refs[-1]
    start = HEADS // 2 * NARROW
    theirs = [note_ref[start + k * 2 * HEADS : start + (k + 1) * 2 * HEADS, :] for k in range(3)]
    theirs = theirs[0].astype(jnp.float32) + theirs[1].astype(jnp.float32) + theirs[2].astype(jnp.float32)
    theirs = jnp.concatenate([theirs[:HEADS], theirs[HEADS:]], axis=1)
    mine = jnp.concatenate([ref[...] for ref in level_refs], axis=0)
    high = jnp.maximum(mine, theirs)
    level = high + jnp.log2(jnp.exp2(mine - high) + jnp.exp2(theirs - high))
    mine = jnp.exp2(mine - level)
    total = None
    head = 0
    for ref in mapped_refs:
        for i in range(ref.shape[0]):
            term = ref[i] * mine[head : head + 1]
            total = term if total is None else total + term
            head += 1
    theirs = jnp.exp2(theirs - level)
    high = theirs.astype(jnp.bfloat16)
    sent_ref[0:NARROW, :] = total.astype(jnp.bfloat16)
    sent_ref[NARROW : NARROW + HEADS, :] = high
    sent_ref[NARROW + HEADS :, :] = (theirs - high.astype(jnp.float32)).astype(jnp.bfloat16)


def unpacked_share(sent_ref):
    sent = sent_ref[...].astype(jnp.float32)
    return sent[:NARROW], sent[NARROW : NARROW + HEADS] + sent[NARROW + HEADS :]


def beside_kernel(grid, rank_ref, sent_ref, note_ref, beside_ref):
    frames, rows, cols = grid
    near = jnp.where(rank_ref[0] == 0, 0, rows - 1)
    choice = row_choice(frames, rows, cols, near, frames * cols, 0)
    near_row = jnp.dot(
        sent_ref[...], choice.astype(jnp.bfloat16), preferred_element_type=jnp.float32
    )
    beside = near_row[:NARROW]
    weights = near_row[NARROW : NARROW + HEADS] + near_row[NARROW + HEADS :]
    for head in range(HEADS):
        side = head % 2 * NARROW
        pair = head // 2 * NARROW
        mapped = note_ref[pair : pair + NARROW, side : side + NARROW].astype(jnp.float32)
        beside = beside + mapped * weights[head : head + 1]
    beside_ref[...] = packed_latents(beside)


def packed_latents(latents):
    half = latents.shape[1] // 2
    packed = jnp.concatenate([latents[:, :half], latents[:, half:]], axis=0)
    return packed.T.astype(jnp.bfloat16)


def merge_kernel(got_ref, mapped_ref, beside_ref, out_ref):
    total, weights = unpacked_share(got_ref)
    for head in range(HEADS):
        total = total + mapped_ref[head] * weights[head : head + 1]
    own = total.shape[1] // 2
    out_ref[0:own, :] = packed_latents(total)
    out_ref[own:, :] = beside_ref[...]


def split_attention(queries, key_states, value_states, kept_tiles, kept_counts, patch_weight, ready, forward):
    frames, rows, cols, feature_count = queries.shape[2:]
    tokens = frames * rows * cols
    flat_query = queries.reshape(tokens, feature_count)
    flat_key = key_states.reshape(tokens, feature_count)
    flat_value = value_states.reshape(tokens, feature_count)
    swap = [(0, 1), (1, 0)]
    ends = list(itertools.accumulate(HEAD_PARTS))
    starts = [0] + ends[:-1]
    parts = []
    source = flat_query
    for start, end in zip(starts, ends):
        parts.append(source[:, start * HD : end * HD])
        if start == 0:
            source, _ = lax.optimization_barrier((source, parts[0]))
    other_queries = [lax.ppermute(part, "sp", swap) for part in parts]
    kept_tiles = kept_tiles.transpose(1, 2, 0)
    kept_counts = kept_counts.T
    patch_weight = patch_weight.T
    smem = pl.BlockSpec(memory_space=pltpu.SMEM)
    params = pltpu.CompilerParams(
        dimension_semantics=("arbitrary",), vmem_limit_bytes=24 * MIB
    )

    def whole(*shape):
        return pl.BlockSpec(shape, lambda i: (0,) * len(shape))

    grid = (frames, rows, cols)
    rank = lax.axis_index("sp").astype(jnp.int32).reshape(1)
    rim_tokens = frames * cols

    note_rows = HEADS // 2 * NARROW + 6 * HEADS

    def attend(part, start, name, with_note=False):
        count = part.shape[1] // HD
        first_block = start // HEAD_BLOCK
        heads = pl.BlockSpec((tokens, HEAD_BLOCK * HD), lambda i: (0, first_block + i))
        return pl.pallas_call(
            functools.partial(attend_kernel, start, grid),
            grid=(count // HEAD_BLOCK,),
            in_specs=[
                smem,
                smem,
                smem,
                pl.BlockSpec((tokens, HEAD_BLOCK * HD), lambda i: (0, i)),
                heads,
                heads,
                pl.BlockSpec((NARROW, HEAD_BLOCK * HD), lambda i: (0, first_block + i)),
            ],
            out_specs=[
                whole(count, tokens),
                pl.BlockSpec((HEAD_BLOCK, NARROW, tokens), lambda i: (i, 0, 0)),
                whole(note_rows, 2 * NARROW),
            ][: 3 if with_note else 2],
            out_shape=[
                jax.ShapeDtypeStruct((count, tokens), jnp.float32),
                jax.ShapeDtypeStruct((count, NARROW, tokens), jnp.float32),
                jax.ShapeDtypeStruct((note_rows, 2 * NARROW), jnp.bfloat16),
            ][: 3 if with_note else 2],
            compiler_params=params,
            cost_estimate=pl.CostEstimate(
                flops=count * tokens, bytes_accessed=count * tokens, transcendentals=0
            ),
            name=name,
        )(rank, kept_tiles, kept_counts, part, flat_key, flat_value, patch_weight)

    flat_query, *_ = lax.optimization_barrier((flat_query, *parts))
    _, mapped, note = attend(flat_query, 0, "own_queries", with_note=True)
    note, ready = lax.optimization_barrier((note, ready))
    other_note = lax.ppermute(note, "sp", swap)
    forwarded = forward(ready)
    levels, shares = [], []
    for part, start in zip(other_queries, starts):
        part, _ = lax.optimization_barrier((part, levels[-1] if levels else note))
        part_level, share = attend(part, start, "other_queries")
        levels.append(part_level)
        shares.append(share)
    operands = (other_note, *levels, *shares)
    sent = pl.pallas_call(
        functools.partial(combine_kernel, len(levels)),
        grid=(1,),
        in_specs=[whole(*part.shape) for part in operands],
        out_specs=whole(NARROW + 2 * HEADS, tokens),
        out_shape=jax.ShapeDtypeStruct((NARROW + 2 * HEADS, tokens), jnp.bfloat16),
        compiler_params=params,
        name="combine",
    )(*operands)
    got = lax.ppermute(sent, "sp", swap)
    beside = pl.pallas_call(
        functools.partial(beside_kernel, grid),
        grid=(1,),
        in_specs=[smem, whole(*sent.shape), whole(*other_note.shape)],
        out_specs=whole(rim_tokens // 2, 2 * NARROW),
        out_shape=jax.ShapeDtypeStruct((rim_tokens // 2, 2 * NARROW), jnp.bfloat16),
        compiler_params=params,
        name="beside",
    )(rank, sent, other_note)
    message = pl.pallas_call(
        merge_kernel,
        grid=(1,),
        in_specs=[whole(*part.shape) for part in (got, mapped, beside)],
        out_specs=whole((tokens + rim_tokens) // 2, 2 * NARROW),
        out_shape=jax.ShapeDtypeStruct(((tokens + rim_tokens) // 2, 2 * NARROW), jnp.bfloat16),
        compiler_params=params,
        name="merge",
    )(got, mapped, beside)
    return message, forwarded, ready


def to_tiles(grid, tile_size):
    frame_count, row_count, col_count, feature_width = grid.shape
    tiled = grid.reshape(
        frame_count // TT, TT, row_count // TH, TH, col_count // TW, TW, feature_width
    ).transpose(0, 2, 4, 1, 3, 5, 6)
    return tiled.reshape(-1, tile_size, feature_width)


def from_tiles(tiles, frame_count, row_count, col_count):
    feature_width = tiles.shape[-1]
    grid = tiles.reshape(
        frame_count // TT, row_count // TH, col_count // TW, TT, TH, TW, feature_width
    ).transpose(0, 3, 1, 4, 2, 5, 6)
    return grid.reshape(frame_count, row_count, col_count, feature_width)


def attend_tiles(query_tiles, key_tiles, value_tiles, tile_index, live_count):
    head_count = query_tiles.shape[0]
    tile_size = query_tiles.shape[2]
    head_size = query_tiles.shape[3]
    keep_count = tile_index.shape[2]

    def one_tile(packed):
        query_block, index_block, count_block = packed
        key_sel = jax.vmap(lambda source, picks: source[picks])(key_tiles, index_block).reshape(
            head_count, keep_count * tile_size, head_size
        )
        value_sel = jax.vmap(lambda source, picks: source[picks])(value_tiles, index_block).reshape(
            head_count, keep_count * tile_size, head_size
        )
        scores = jnp.einsum(
            "hqd,hkd->hqk", query_block, key_sel, preferred_element_type=jnp.float32
        ) * head_size ** (-0.5)
        live = jnp.arange(keep_count, dtype=jnp.int32)[None, :] < count_block[:, None]
        live = jnp.repeat(live, tile_size, axis=1)[:, None, :]
        scores = jnp.where(live, scores, -1e30)
        row_top = jnp.max(scores, axis=-1, keepdims=True)
        exponent = jnp.where(live, jnp.exp(scores - row_top), 0.0)
        weights = (exponent / jnp.sum(exponent, axis=-1, keepdims=True)).astype(jnp.bfloat16)
        result = jnp.einsum("hqk,hkd->hqd", weights, value_sel, preferred_element_type=jnp.float32)
        return result.astype(jnp.bfloat16)

    return lax.map(
        one_tile,
        (
            query_tiles.transpose(1, 0, 2, 3),
            tile_index.transpose(1, 0, 2),
            live_count.transpose(1, 0),
        ),
    )


def exchanged_attention(queries, key_states, value_states, kept_tiles, kept_counts, patch_weight):
    frame_count, local_rows, token_cols, feature_count = queries.shape[2:]
    tokens = frame_count * local_rows * token_cols
    sp_count = lax.axis_size("sp")
    sp_rank = lax.axis_index("sp")
    local_heads = HEADS // sp_count
    clip_rows = local_rows * sp_count
    tile_size = TT * TH * TW
    mixed_query, mixed_key, mixed_value = (
        lax.all_to_all(part.reshape(tokens, feature_count), "sp", split_axis=1, concat_axis=0, tiled=True)
        for part in (queries, key_states, value_states)
    )
    own_width = mixed_query.shape[1]

    def head_tiles(mixed):
        grid = mixed.reshape(sp_count, frame_count, local_rows, token_cols, own_width).transpose(
            1, 0, 2, 3, 4
        )
        tiles = to_tiles(grid.reshape(frame_count, clip_rows, token_cols, own_width), tile_size)
        return tiles.reshape(tiles.shape[0], tile_size, local_heads, HD).transpose(2, 0, 1, 3)

    outputs = attend_tiles(
        head_tiles(mixed_query),
        head_tiles(mixed_key),
        head_tiles(mixed_value),
        lax.dynamic_slice_in_dim(kept_tiles, sp_rank * local_heads, local_heads, 0),
        lax.dynamic_slice_in_dim(kept_counts, sp_rank * local_heads, local_heads, 0),
    )
    tile_count = outputs.shape[0]
    attended = from_tiles(
        outputs.transpose(0, 2, 1, 3).reshape(tile_count, tile_size, own_width),
        frame_count,
        clip_rows,
        token_cols,
    )
    attended = attended.reshape(frame_count, sp_count, local_rows, token_cols, own_width).transpose(
        1, 0, 2, 3, 4
    )
    attended = attended.reshape(sp_count * tokens, own_width)
    restored = lax.all_to_all(attended, "sp", split_axis=0, concat_axis=1, tiled=True)
    latent = jnp.dot(restored, patch_weight, preferred_element_type=jnp.float32)
    latent = latent.astype(jnp.bfloat16)
    packed = jnp.concatenate([latent[: tokens // 2], latent[tokens // 2 :]], axis=1)
    grid = packed.reshape(frame_count // 2, local_rows, token_cols, 2 * NARROW)
    above = lax.ppermute(grid[:, -1], "sp", [(i, i + 1) for i in range(sp_count - 1)])
    below = lax.ppermute(grid[:, 0], "sp", [(i + 1, i) for i in range(sp_count - 1)])
    rims = [rim.reshape(-1, 2 * NARROW) for rim in (above, below)]
    return jnp.concatenate([packed, *rims], axis=0)


def spread_kernel(plain_ref, out_ref):
    empty = jnp.zeros((LAT, CH), jnp.bfloat16)
    for side in range(2):
        blocks = itertools.product(range(3), range(2), range(2), range(2), range(2))
        for position, (dt, rr, cc, u, w) in enumerate(blocks):
            dz = 2 * cc + w - (1 - side)
            for ro in range(2):
                dy = 2 * rr + u - ro
                inside = 0 <= dy < 3 and 0 <= dz < 3
                block = plain_ref[(dt * 3 + dy) * 3 + dz] if inside else empty
                out_ref[side, position * LAT : (position + 1) * LAT, ro * CH : (ro + 1) * CH] = block


def first_weights(first_kernel):
    return pl.pallas_call(
        spread_kernel,
        grid=(1,),
        in_specs=[pl.BlockSpec(first_kernel.shape, lambda i: (0, 0, 0))],
        out_specs=pl.BlockSpec((2, 12 * NARROW, 2 * CH), lambda i: (0, 0, 0)),
        out_shape=jax.ShapeDtypeStruct((2, 12 * NARROW, 2 * CH), jnp.bfloat16),
        name="spread_first_kernel",
    )(first_kernel)


def decode_kernel(
    frames,
    rows,
    cols,
    place_ref,
    message_refs,
    weight_hbm,
    shard_refs,
    out_ref,
    token_ref,
    pair_ref,
    first_ref,
    act_ref,
    wide_ref,
    weight_ref,
    kernel_ref,
    sems,
):
    at_first = place_ref[0] == 0
    at_last = place_ref[0] == place_ref[1] - 1
    step = place_ref[2]
    weight_copy = pltpu.make_async_copy(weight_hbm, weight_ref, sems.at[0])
    weight_copy.start()
    if len(shard_refs) == 1:
        shard_copies = [pltpu.make_async_copy(shard_refs[0], kernel_ref, sems.at[1])]
    else:
        shard_copies = [
            pltpu.make_async_copy(ref, kernel_ref.at[place_ref[3 + min(k, 3)]], sems.at[1 + k])
            for k, ref in enumerate(shard_refs)
        ]
    holder = place_ref[7 if len(shard_refs) > 1 else 3]

    def each_shard(act):
        for k, copy in enumerate(shard_copies):
            if k < 3:
                act(copy)
            else:
                pl.when(holder == k - 3)(functools.partial(act, copy))

    each_shard(lambda copy: copy.start())

    lane = lax.broadcasted_iota(jnp.int32, (1, 1, 1, 2 * NARROW), 3)

    message = message_refs[0][...]
    for k in range(1, len(message_refs)):
        message = jnp.where(step == k, message_refs[k][...], message)
    own_count = frames // 2 * rows * cols
    rim_count = frames // 2 * cols

    def unpacked(packed, height):
        plain = packed.astype(jnp.float32)
        turned = pltpu.roll(plain, NARROW, 1)
        shape = (frames // 2, height, cols, 2 * NARROW)
        plain, turned = plain.reshape(shape), turned.reshape(shape)
        early = jnp.where(lane < NARROW, plain, turned)
        late = jnp.where(lane < NARROW, turned, plain)
        return jnp.concatenate([early, late], axis=0)

    token_ref[:, 1 : 1 + rows, 8 : 8 + cols, :] = unpacked(message[:own_count], rows)
    above = unpacked(message[own_count : own_count + rim_count], 1)
    below = unpacked(message[-rim_count:], 1)
    for f in range(frames):
        edge = pltpu.roll(token_ref[f, 1, 8 : 8 + cols, :], 2 * LAT, 1)
        token_ref[f, 0, 8 : 8 + cols, :] = jnp.where(at_first, edge, above[f, 0])
        edge = pltpu.roll(token_ref[f, rows, 8 : 8 + cols, :], 2 * NARROW - 2 * LAT, 1)
        token_ref[f, rows + 1, 8 : 8 + cols, :] = jnp.where(at_last, edge, below[f, 0])
    for f in range(frames):
        for r in range(rows + 2):
            start = token_ref[f, r, 8:16, :]
            token_ref[f, r, 7:8, :] = pltpu.roll(start, LAT, 1)[0:1]
            end = token_ref[f, r, cols : 8 + cols, :]
            token_ref[f, r, 8 + cols : 9 + cols, :] = pltpu.roll(end, 2 * NARROW - LAT, 1)[7:8]

    for side in range(2):
        pair = jnp.where(
            lane < NARROW,
            token_ref[:, :, 7 + side : 7 + side + cols, :],
            token_ref[:, :, 8 + side : 8 + side + cols, :],
        ).astype(jnp.bfloat16)
        pair_ref[side, 2:] = pair
        pair_ref[side, 0] = pair[0]
        pair_ref[side, 1] = pair[0]

    weight_copy.wait()
    gaps = rows + 1
    for side in range(2):
        columns = jnp.concatenate(
            [
                pair_ref[side, dt : dt + frames, rr : rr + gaps].reshape(frames * gaps * cols, 2 * NARROW)
                for dt in range(3)
                for rr in range(2)
            ],
            axis=1,
        )
        first = jnp.dot(columns, weight_ref[side], preferred_element_type=jnp.float32) * VAE_SCALE
        first = first.astype(jnp.bfloat16).astype(jnp.float32)
        act = first / (1.0 + jnp.exp(-first))
        first = first.reshape(frames, gaps, cols, 2 * CH)
        act = act.reshape(frames, gaps, cols, 2 * CH)
        for f in range(frames):
            for g in range(gaps):
                for ro in range(2):
                    for part in range(CH // 128):
                        lanes = slice(ro * CH + part * 128, ro * CH + part * 128 + 128)
                        row = 2 * g + ro
                        into = pl.ds(8 + side, cols, stride=2)
                        first_ref[part, f, row, into, :] = first[f, g, :, lanes]
                        act_ref[part, f, row, into, :] = act[f, g, :, lanes]

    width = 2 * cols
    height = 2 * rows
    for part in range(CH // 128):
        for f in range(frames):
            act_ref[part, f, 0] = jnp.where(at_first, act_ref[part, f, 1], act_ref[part, f, 0])
            act_ref[part, f, height + 1] = jnp.where(
                at_last, act_ref[part, f, height], act_ref[part, f, height + 1]
            )
        act_ref[part, :, :, 7:8, :] = act_ref[part, :, :, 8:9, :]
        act_ref[part, :, :, 8 + width : 9 + width, :] = act_ref[part, :, :, 7 + width : 8 + width, :]
        for dz in range(3):
            lanes = slice(dz * CH + part * 128, dz * CH + part * 128 + 128)
            shifted = act_ref[part, :, :, 7 + dz : 7 + dz + width, :].astype(jnp.bfloat16)
            wide_ref[2:, :, :, lanes] = shifted
            wide_ref[0, :, :, lanes] = shifted[0]
            wide_ref[1, :, :, lanes] = shifted[0]

    each_shard(lambda copy: copy.wait())
    cells = frames * height * width
    total = None
    for dt in range(3):
        for dy in range(3):
            window = wide_ref[dt : dt + frames, dy : dy + height].reshape(cells, 3 * CH)
            weight = jnp.concatenate(
                [kernel_ref[:, (dt * 3 + dy) * 3 + dz].reshape(CH, CH) for dz in range(3)], axis=0
            )
            product = jnp.dot(window, weight, preferred_element_type=jnp.float32)
            total = product if total is None else total + product
    total = total.reshape(frames, height, width, CH)
    for part in range(CH // 128):
        lanes = slice(part * 128, part * 128 + 128)
        residual = first_ref[part, :, 1 : 1 + height, 8 : 8 + width, :]
        out_ref[:, :, :, lanes] = (total[:, :, :, lanes] + residual).astype(jnp.bfloat16)


def decode(frames, rows, cols, place, messages, weights, groups, shards):
    height, width = 2 * rows, 2 * cols
    count = len(messages)
    taps, depth = shards[0].shape[-3:-1]

    def whole(shape):
        return pl.BlockSpec(shape, lambda i, place: (0,) * len(shape))

    def body(place_ref, *refs):
        message_refs, refs = refs[:count], refs[count:]
        weight_hbm, shard_refs = refs[0], refs[1 : 1 + len(shards)]
        decode_kernel(
            frames, rows, cols, place_ref, message_refs, weight_hbm, shard_refs, *refs[1 + len(shards) :]
        )

    grid_spec = pltpu.PrefetchScalarGridSpec(
        num_scalar_prefetch=1,
        grid=(1,),
        in_specs=[whole(part.shape) for part in messages]
        + [pl.BlockSpec(memory_space=pl.ANY)] * (1 + len(shards)),
        out_specs=whole((frames, height, width, CH)),
        scratch_shapes=[
            pltpu.VMEM((frames, rows + 2, cols + 16, 2 * NARROW), jnp.float32),
            pltpu.VMEM((2, frames + 2, rows + 2, cols, 2 * NARROW), jnp.bfloat16),
            pltpu.VMEM((CH // 128, frames, height + 2, width + 16, 128), jnp.float32),
            pltpu.VMEM((CH // 128, frames, height + 2, width + 16, 128), jnp.float32),
            pltpu.VMEM((frames + 2, height + 2, width, 3 * CH), jnp.bfloat16),
            pltpu.VMEM(weights.shape, jnp.bfloat16),
            pltpu.VMEM((groups, taps, depth, CH), jnp.bfloat16),
            pltpu.SemaphoreType.DMA((1 + len(shards),)),
        ],
    )
    return pl.pallas_call(
        body,
        grid_spec=grid_spec,
        out_shape=jax.ShapeDtypeStruct((frames, height, width, CH), jnp.bfloat16),
        compiler_params=pltpu.CompilerParams(vmem_limit_bytes=32 * MIB),
        cost_estimate=pl.CostEstimate(
            flops=2 * frames * height * width * 27 * CH * CH,
            bytes_accessed=27 * CH * CH * 2 + frames * height * width * CH * 2,
            transcendentals=frames * height * width * CH,
        ),
        name="decode_block",
    )(place, *messages, weights, *shards)


def trade_shards(shard, segment_count):
    segments = range(segment_count)
    near = [(s * 4 + g, s * 4 + (g ^ (1 + s % 2))) for s in segments for g in range(4)]
    inner = [(s * 4 + g, s * 4 + (g ^ 3)) for s in segments[::2] for g in (1, 2)]
    return [lax.ppermute(shard, ("segment", "grp"), pairs) for pairs in (near, inner)]


def forward_shards(near, segment_count, ready):
    near, _ = lax.optimization_barrier((near, ready))
    segments = range(segment_count)
    outward = [(s * 4 + a, s * 4 + b) for s in segments[1::2] for a, b in ((1, 0), (2, 3))]
    return (
        lax.ppermute(near, ("segment", "grp"), outward),
        lax.ppermute(near, "segment", [(s, s ^ 1) for s in segments]),
    )


def share_shards(inner, outer, at_inner, segment_count, ready):
    inner, outer, _ = lax.optimization_barrier((inner, outer, ready))
    held = jnp.where(at_inner, inner, outer)
    pairs = [(s * 4 + g, (s ^ 1) * 4 + g) for s in range(segment_count) for g in ((1, 2), (0, 3))[s % 2]]
    return held, lax.ppermute(held, ("segment", "grp"), pairs)


def local(
    queries,
    key_states,
    value_states,
    kept_tiles,
    kept_counts,
    patch_weight,
    decode_slot,
    first_kernel,
    second_kernel,
):
    frames, rows, cols = queries.shape[2:5]
    sp_count = lax.axis_size("sp")
    sp_rank = lax.axis_index("sp")
    segment_count = lax.axis_size("segment")
    segment_rank = lax.axis_index("segment")

    weights = first_weights(first_kernel)
    picks = (decode_slot == segment_rank).astype(jnp.int32)
    source = jnp.sum(jnp.arange(segment_count, dtype=jnp.int32) * picks)
    step = lax.rem(segment_rank - source + segment_count, segment_count)
    group_count = lax.axis_size("grp")
    group = lax.axis_index("grp")
    core = lax.rem(segment_rank, 2)
    line = group_count == 4 and segment_count % 2 == 0
    places = [sp_rank, jnp.int32(sp_count), step]
    if line:
        at_inner = jnp.logical_or(group == 1, group == 2)
        places += [group, group ^ (1 + core), group ^ (2 - core), group ^ 3]
        places.append(jnp.where(at_inner, core, 1 - core))
        near, inner = trade_shards(second_kernel, segment_count)
        forward = functools.partial(forward_shards, near, segment_count)
    else:
        places += [jnp.int32(0)] * 2
        forward = lambda ready: None
    place = jnp.stack(places).astype(jnp.int32)

    arguments = (queries, key_states, value_states, kept_tiles, kept_counts, patch_weight)
    if sp_count == 2 and rows * sp_count == TH and frames == TT:
        message, forwarded, (weights, place) = split_attention(*arguments, (weights, place), forward)
    else:
        message = exchanged_attention(*arguments)
        forwarded = forward(message)
    if line:
        outer, swapped = forwarded
        last = share_shards(inner, outer, at_inner, segment_count, message)
        shards = [second_kernel, near, swapped, *last]
    else:
        shards = [lax.all_gather(second_kernel, "grp", axis=0, tiled=False)]
    messages = [message] + [
        lax.ppermute(message, "segment", [(i, (i + step) % segment_count) for i in range(segment_count)])
        for step in range(1, segment_count)
    ]
    return decode(frames, rows, cols, place, messages, weights, group_count, shards)[None, None]


def solution(mesh):
    return jax.shard_map(
        local,
        mesh=mesh,
        in_specs=(
            P("segment", "grp", None, "sp", None, None),
            P("segment", "grp", None, "sp", None, None),
            P("segment", "grp", None, "sp", None, None),
            P(),
            P(),
            P(),
            P(),
            P(),
            P(None, "grp", None),
        ),
        out_specs=P("segment", "grp", None, "sp", None, None),
        check_vma=False,
    )
```

```python
import functools
import itertools

import jax
import jax.numpy as jnp
from jax import lax
from jax.experimental import pallas as pl
from jax.experimental.pallas import tpu as pltpu
from jax.sharding import PartitionSpec as P

HEADS = 16
HD = 128
LAT = 16
CH = 256
TT = 4
TH = 8
TW = 8

VAE_SCALE = 1.0 / 0.476986
SCORE_UNIT = HD**-0.5 * 1.4426950408889634
HEAD_BLOCK = 4
HEAD_PARTS = (16,)
NARROW = 4 * LAT
MIB = 1 << 20


def partial_head(head, q, k, v, tiles_ref, counts_ref):
    keys, queries = k.shape[0], q.shape[0]
    tile_count, keep = tiles_ref.shape[:2]
    scores = lax.dot_general(k, q, (((1,), (1,)), ((), ())), preferred_element_type=jnp.float32)
    lane = lax.broadcasted_iota(jnp.int32, (1, queries), 1)
    lane_tile = lax.rem(lax.div(lane, TW), tile_count)
    rows = []
    for key_tile in range(tile_count):
        row = jnp.zeros((1, queries), jnp.float32)
        for query_tile in range(tile_count):
            live = jnp.bool_(False)
            for slot in range(keep):
                here = jnp.logical_and(
                    tiles_ref[query_tile, slot, head] == key_tile, slot < counts_ref[query_tile, head]
                )
                live = jnp.logical_or(live, here)
            row = jnp.where(lane_tile == query_tile, jnp.where(live, 0.0, -1e30), row)
        rows.append(row[None])
    bias = jnp.concatenate(rows, axis=0)
    scores = scores.reshape(keys // (tile_count * TW), tile_count, TW, queries) + bias[None]
    scores = scores.reshape(keys, queries)
    top = jnp.max(scores, axis=0, keepdims=True)
    power = jnp.exp2((scores - top) * SCORE_UNIT)
    total = jnp.sum(power, axis=0, keepdims=True)
    out = lax.dot_general(
        v, power.astype(jnp.bfloat16), (((0,), (0,)), ((), ())), preferred_element_type=jnp.float32
    )
    return top * SCORE_UNIT, total, out


def row_choice(frames, rows, cols, row, lanes, start):
    token = lax.broadcasted_iota(jnp.int32, (frames * rows * cols, lanes), 0)
    lane = lax.broadcasted_iota(jnp.int32, (frames * rows * cols, lanes), 1) - start
    wanted = lax.div(lane, cols) * (rows * cols) + row * cols + lax.rem(lane, cols)
    inside = jnp.logical_and(lane >= 0, lane < frames * cols)
    return jnp.where(jnp.logical_and(inside, token == wanted), 1.0, 0.0)


def attend_kernel(
    offset, grid, rank_ref, tiles_ref, counts_ref, q_ref, k_ref, v_ref, w_ref, level_ref, mapped_ref, *note_refs
):
    block = pl.program_id(0)
    if note_refs:
        note_ref = note_refs[0]
        frames, rows, cols = grid
        near = jnp.where(rank_ref[0] == 0, rows - 1, 0)
        choices = [
            row_choice(frames, rows, cols, near, 2 * NARROW, start).astype(jnp.bfloat16)
            for start in (0, NARROW)
        ]
    for i in range(HEAD_BLOCK):
        cols = slice(i * HD, (i + 1) * HD)
        row = block * HEAD_BLOCK + i
        top, total, out = partial_head(
            offset + row, q_ref[:, cols], k_ref[:, cols], v_ref[:, cols], tiles_ref, counts_ref
        )
        out = (out / total).astype(jnp.bfloat16)
        level_ref[pl.ds(row, 1), :] = top + jnp.log2(total)
        mapped = jnp.dot(w_ref[:, cols], out, preferred_element_type=jnp.float32)
        mapped_ref[i] = mapped
        if note_refs:
            rim = jnp.dot(mapped.astype(jnp.bfloat16), choices[i % 2], preferred_element_type=jnp.float32)
            if i % 2 == 0:
                even = rim
            else:
                pair = pl.multiple_of((row // 2) * NARROW, NARROW)
                note_ref[pl.ds(pair, NARROW), :] = (even + rim).astype(jnp.bfloat16)
    if note_refs:

        @pl.when(block == pl.num_programs(0) - 1)
        def _():
            rest = level_ref[...]
            rest = jnp.concatenate([rest[:, :128], rest[:, 128:]], axis=0)
            start = HEADS // 2 * NARROW
            for _ in range(3):
                part = rest.astype(jnp.bfloat16)
                note_ref[start : start + 2 * HEADS, :] = part
                rest = rest - part.astype(jnp.float32)
                start += 2 * HEADS


def combine_kernel(parts, note_ref, *refs):
    level_refs, mapped_refs, sent_ref = refs[:parts], refs[parts : 2 * parts], refs[-1]
    start = HEADS // 2 * NARROW
    theirs = [note_ref[start + k * 2 * HEADS : start + (k + 1) * 2 * HEADS, :] for k in range(3)]
    theirs = theirs[0].astype(jnp.float32) + theirs[1].astype(jnp.float32) + theirs[2].astype(jnp.float32)
    theirs = jnp.concatenate([theirs[:HEADS], theirs[HEADS:]], axis=1)
    mine = jnp.concatenate([ref[...] for ref in level_refs], axis=0)
    high = jnp.maximum(mine, theirs)
    level = high + jnp.log2(jnp.exp2(mine - high) + jnp.exp2(theirs - high))
    mine = jnp.exp2(mine - level)
    total = None
    head = 0
    for ref in mapped_refs:
        for i in range(ref.shape[0]):
            term = ref[i] * mine[head : head + 1]
            total = term if total is None else total + term
            head += 1
    theirs = jnp.exp2(theirs - level)
    high = theirs.astype(jnp.bfloat16)
    sent_ref[0:NARROW, :] = total.astype(jnp.bfloat16)
    sent_ref[NARROW : NARROW + HEADS, :] = high
    sent_ref[NARROW + HEADS :, :] = (theirs - high.astype(jnp.float32)).astype(jnp.bfloat16)


def unpacked_share(sent_ref):
    sent = sent_ref[...].astype(jnp.float32)
    return sent[:NARROW], sent[NARROW : NARROW + HEADS] + sent[NARROW + HEADS :]


def beside_kernel(grid, rank_ref, sent_ref, note_ref, beside_ref):
    frames, rows, cols = grid
    near = jnp.where(rank_ref[0] == 0, 0, rows - 1)
    choice = row_choice(frames, rows, cols, near, frames * cols, 0)
    near_row = jnp.dot(
        sent_ref[...], choice.astype(jnp.bfloat16), preferred_element_type=jnp.float32
    )
    beside = near_row[:NARROW]
    weights = near_row[NARROW : NARROW + HEADS] + near_row[NARROW + HEADS :]
    for head in range(HEADS):
        side = head % 2 * NARROW
        pair = head // 2 * NARROW
        mapped = note_ref[pair : pair + NARROW, side : side + NARROW].astype(jnp.float32)
        beside = beside + mapped * weights[head : head + 1]
    beside_ref[...] = packed_latents(beside)


def packed_latents(latents):
    half = latents.shape[1] // 2
    packed = jnp.concatenate([latents[:, :half], latents[:, half:]], axis=0)
    return packed.T.astype(jnp.bfloat16)


def merge_kernel(got_ref, mapped_ref, beside_ref, out_ref):
    total, weights = unpacked_share(got_ref)
    for head in range(HEADS):
        total = total + mapped_ref[head] * weights[head : head + 1]
    own = total.shape[1] // 2
    out_ref[0:own, :] = packed_latents(total)
    out_ref[own:, :] = beside_ref[...]


def split_attention(queries, key_states, value_states, kept_tiles, kept_counts, patch_weight, ready):
    frames, rows, cols, feature_count = queries.shape[2:]
    tokens = frames * rows * cols
    flat_query = queries.reshape(tokens, feature_count)
    flat_key = key_states.reshape(tokens, feature_count)
    flat_value = value_states.reshape(tokens, feature_count)
    swap = [(0, 1), (1, 0)]
    ends = list(itertools.accumulate(HEAD_PARTS))
    starts = [0] + ends[:-1]
    parts = []
    source = flat_query
    for start, end in zip(starts, ends):
        parts.append(source[:, start * HD : end * HD])
        if start == 0:
            source, _ = lax.optimization_barrier((source, parts[0]))
    other_queries = [lax.ppermute(part, "sp", swap) for part in parts]
    kept_tiles = kept_tiles.transpose(1, 2, 0)
    kept_counts = kept_counts.T
    patch_weight = patch_weight.T
    smem = pl.BlockSpec(memory_space=pltpu.SMEM)
    params = pltpu.CompilerParams(
        dimension_semantics=("arbitrary",), vmem_limit_bytes=24 * MIB
    )

    def whole(*shape):
        return pl.BlockSpec(shape, lambda i: (0,) * len(shape))

    grid = (frames, rows, cols)
    rank = lax.axis_index("sp").astype(jnp.int32).reshape(1)
    rim_tokens = frames * cols

    note_rows = HEADS // 2 * NARROW + 6 * HEADS

    def attend(part, start, name, with_note=False):
        count = part.shape[1] // HD
        first_block = start // HEAD_BLOCK
        heads = pl.BlockSpec((tokens, HEAD_BLOCK * HD), lambda i: (0, first_block + i))
        return pl.pallas_call(
            functools.partial(attend_kernel, start, grid),
            grid=(count // HEAD_BLOCK,),
            in_specs=[
                smem,
                smem,
                smem,
                pl.BlockSpec((tokens, HEAD_BLOCK * HD), lambda i: (0, i)),
                heads,
                heads,
                pl.BlockSpec((NARROW, HEAD_BLOCK * HD), lambda i: (0, first_block + i)),
            ],
            out_specs=[
                whole(count, tokens),
                pl.BlockSpec((HEAD_BLOCK, NARROW, tokens), lambda i: (i, 0, 0)),
                whole(note_rows, 2 * NARROW),
            ][: 3 if with_note else 2],
            out_shape=[
                jax.ShapeDtypeStruct((count, tokens), jnp.float32),
                jax.ShapeDtypeStruct((count, NARROW, tokens), jnp.float32),
                jax.ShapeDtypeStruct((note_rows, 2 * NARROW), jnp.bfloat16),
            ][: 3 if with_note else 2],
            compiler_params=params,
            cost_estimate=pl.CostEstimate(
                flops=count * tokens, bytes_accessed=count * tokens, transcendentals=0
            ),
            name=name,
        )(rank, kept_tiles, kept_counts, part, flat_key, flat_value, patch_weight)

    flat_query, *_ = lax.optimization_barrier((flat_query, *parts))
    _, mapped, note = attend(flat_query, 0, "own_queries", with_note=True)
    note, ready = lax.optimization_barrier((note, ready))
    other_note = lax.ppermute(note, "sp", swap)
    levels, shares = [], []
    for part, start in zip(other_queries, starts):
        part, _ = lax.optimization_barrier((part, levels[-1] if levels else note))
        part_level, share = attend(part, start, "other_queries")
        levels.append(part_level)
        shares.append(share)
    operands = (other_note, *levels, *shares)
    sent = pl.pallas_call(
        functools.partial(combine_kernel, len(levels)),
        grid=(1,),
        in_specs=[whole(*part.shape) for part in operands],
        out_specs=whole(NARROW + 2 * HEADS, tokens),
        out_shape=jax.ShapeDtypeStruct((NARROW + 2 * HEADS, tokens), jnp.bfloat16),
        compiler_params=params,
        name="combine",
    )(*operands)
    got = lax.ppermute(sent, "sp", swap)
    beside = pl.pallas_call(
        functools.partial(beside_kernel, grid),
        grid=(1,),
        in_specs=[smem, whole(*sent.shape), whole(*other_note.shape)],
        out_specs=whole(rim_tokens // 2, 2 * NARROW),
        out_shape=jax.ShapeDtypeStruct((rim_tokens // 2, 2 * NARROW), jnp.bfloat16),
        compiler_params=params,
        name="beside",
    )(rank, sent, other_note)
    message = pl.pallas_call(
        merge_kernel,
        grid=(1,),
        in_specs=[whole(*part.shape) for part in (got, mapped, beside)],
        out_specs=whole((tokens + rim_tokens) // 2, 2 * NARROW),
        out_shape=jax.ShapeDtypeStruct(((tokens + rim_tokens) // 2, 2 * NARROW), jnp.bfloat16),
        compiler_params=params,
        name="merge",
    )(got, mapped, beside)
    return message, ready


def to_tiles(grid, tile_size):
    frame_count, row_count, col_count, feature_width = grid.shape
    tiled = grid.reshape(
        frame_count // TT, TT, row_count // TH, TH, col_count // TW, TW, feature_width
    ).transpose(0, 2, 4, 1, 3, 5, 6)
    return tiled.reshape(-1, tile_size, feature_width)


def from_tiles(tiles, frame_count, row_count, col_count):
    feature_width = tiles.shape[-1]
    grid = tiles.reshape(
        frame_count // TT, row_count // TH, col_count // TW, TT, TH, TW, feature_width
    ).transpose(0, 3, 1, 4, 2, 5, 6)
    return grid.reshape(frame_count, row_count, col_count, feature_width)


def attend_tiles(query_tiles, key_tiles, value_tiles, tile_index, live_count):
    head_count = query_tiles.shape[0]
    tile_size = query_tiles.shape[2]
    head_size = query_tiles.shape[3]
    keep_count = tile_index.shape[2]

    def one_tile(packed):
        query_block, index_block, count_block = packed
        key_sel = jax.vmap(lambda source, picks: source[picks])(key_tiles, index_block).reshape(
            head_count, keep_count * tile_size, head_size
        )
        value_sel = jax.vmap(lambda source, picks: source[picks])(value_tiles, index_block).reshape(
            head_count, keep_count * tile_size, head_size
        )
        scores = jnp.einsum(
            "hqd,hkd->hqk", query_block, key_sel, preferred_element_type=jnp.float32
        ) * head_size ** (-0.5)
        live = jnp.arange(keep_count, dtype=jnp.int32)[None, :] < count_block[:, None]
        live = jnp.repeat(live, tile_size, axis=1)[:, None, :]
        scores = jnp.where(live, scores, -1e30)
        row_top = jnp.max(scores, axis=-1, keepdims=True)
        exponent = jnp.where(live, jnp.exp(scores - row_top), 0.0)
        weights = (exponent / jnp.sum(exponent, axis=-1, keepdims=True)).astype(jnp.bfloat16)
        result = jnp.einsum("hqk,hkd->hqd", weights, value_sel, preferred_element_type=jnp.float32)
        return result.astype(jnp.bfloat16)

    return lax.map(
        one_tile,
        (
            query_tiles.transpose(1, 0, 2, 3),
            tile_index.transpose(1, 0, 2),
            live_count.transpose(1, 0),
        ),
    )


def exchanged_attention(queries, key_states, value_states, kept_tiles, kept_counts, patch_weight):
    frame_count, local_rows, token_cols, feature_count = queries.shape[2:]
    tokens = frame_count * local_rows * token_cols
    sp_count = lax.axis_size("sp")
    sp_rank = lax.axis_index("sp")
    local_heads = HEADS // sp_count
    clip_rows = local_rows * sp_count
    tile_size = TT * TH * TW
    mixed_query, mixed_key, mixed_value = (
        lax.all_to_all(part.reshape(tokens, feature_count), "sp", split_axis=1, concat_axis=0, tiled=True)
        for part in (queries, key_states, value_states)
    )
    own_width = mixed_query.shape[1]

    def head_tiles(mixed):
        grid = mixed.reshape(sp_count, frame_count, local_rows, token_cols, own_width).transpose(
            1, 0, 2, 3, 4
        )
        tiles = to_tiles(grid.reshape(frame_count, clip_rows, token_cols, own_width), tile_size)
        return tiles.reshape(tiles.shape[0], tile_size, local_heads, HD).transpose(2, 0, 1, 3)

    outputs = attend_tiles(
        head_tiles(mixed_query),
        head_tiles(mixed_key),
        head_tiles(mixed_value),
        lax.dynamic_slice_in_dim(kept_tiles, sp_rank * local_heads, local_heads, 0),
        lax.dynamic_slice_in_dim(kept_counts, sp_rank * local_heads, local_heads, 0),
    )
    tile_count = outputs.shape[0]
    attended = from_tiles(
        outputs.transpose(0, 2, 1, 3).reshape(tile_count, tile_size, own_width),
        frame_count,
        clip_rows,
        token_cols,
    )
    attended = attended.reshape(frame_count, sp_count, local_rows, token_cols, own_width).transpose(
        1, 0, 2, 3, 4
    )
    attended = attended.reshape(sp_count * tokens, own_width)
    restored = lax.all_to_all(attended, "sp", split_axis=0, concat_axis=1, tiled=True)
    latent = jnp.dot(restored, patch_weight, preferred_element_type=jnp.float32)
    latent = latent.astype(jnp.bfloat16)
    packed = jnp.concatenate([latent[: tokens // 2], latent[tokens // 2 :]], axis=1)
    grid = packed.reshape(frame_count // 2, local_rows, token_cols, 2 * NARROW)
    above = lax.ppermute(grid[:, -1], "sp", [(i, i + 1) for i in range(sp_count - 1)])
    below = lax.ppermute(grid[:, 0], "sp", [(i + 1, i) for i in range(sp_count - 1)])
    rims = [rim.reshape(-1, 2 * NARROW) for rim in (above, below)]
    return jnp.concatenate([packed, *rims], axis=0)


def spread_kernel(plain_ref, out_ref):
    empty = jnp.zeros((LAT, CH), jnp.bfloat16)
    for side in range(2):
        blocks = itertools.product(range(3), range(2), range(2), range(2), range(2))
        for position, (dt, rr, cc, u, w) in enumerate(blocks):
            dz = 2 * cc + w - (1 - side)
            for ro in range(2):
                dy = 2 * rr + u - ro
                inside = 0 <= dy < 3 and 0 <= dz < 3
                block = plain_ref[(dt * 3 + dy) * 3 + dz] if inside else empty
                out_ref[side, position * LAT : (position + 1) * LAT, ro * CH : (ro + 1) * CH] = block


def first_weights(first_kernel):
    return pl.pallas_call(
        spread_kernel,
        grid=(1,),
        in_specs=[pl.BlockSpec(first_kernel.shape, lambda i: (0, 0, 0))],
        out_specs=pl.BlockSpec((2, 12 * NARROW, 2 * CH), lambda i: (0, 0, 0)),
        out_shape=jax.ShapeDtypeStruct((2, 12 * NARROW, 2 * CH), jnp.bfloat16),
        name="spread_first_kernel",
    )(first_kernel)


def decode_kernel(
    frames,
    rows,
    cols,
    place_ref,
    message_refs,
    weight_ref,
    shard_refs,
    out_ref,
    token_ref,
    pair_ref,
    first_ref,
    act_ref,
    wide_ref,
    kernel_ref,
    sems,
):
    at_first = place_ref[0] == 0
    at_last = place_ref[0] == place_ref[1] - 1
    step = place_ref[2]
    if len(shard_refs) == 1:
        shard_copies = [pltpu.make_async_copy(shard_refs[0], kernel_ref, sems.at[0])]
    else:
        shard_copies = [
            pltpu.make_async_copy(ref, kernel_ref.at[place_ref[3 + k]], sems.at[k])
            for k, ref in enumerate(shard_refs)
        ]
    direct = place_ref[3 + len(shard_refs)]

    def each_shard(act):
        for k, copy in enumerate(shard_copies):
            if len(shard_copies) - k > 2 or len(shard_copies) == 1:
                act(copy)
            else:
                pl.when(direct == len(shard_copies) - 1 - k)(functools.partial(act, copy))

    each_shard(lambda copy: copy.start())

    lane = lax.broadcasted_iota(jnp.int32, (1, 1, 1, 2 * NARROW), 3)

    message = message_refs[0][...]
    for k in range(1, len(message_refs)):
        message = jnp.where(step == k, message_refs[k][...], message)
    own_count = frames // 2 * rows * cols
    rim_count = frames // 2 * cols

    def unpacked(packed, height):
        plain = packed.astype(jnp.float32)
        turned = pltpu.roll(plain, NARROW, 1)
        shape = (frames // 2, height, cols, 2 * NARROW)
        plain, turned = plain.reshape(shape), turned.reshape(shape)
        early = jnp.where(lane < NARROW, plain, turned)
        late = jnp.where(lane < NARROW, turned, plain)
        return jnp.concatenate([early, late], axis=0)

    token_ref[:, 1 : 1 + rows, 8 : 8 + cols, :] = unpacked(message[:own_count], rows)
    above = unpacked(message[own_count : own_count + rim_count], 1)
    below = unpacked(message[-rim_count:], 1)
    for f in range(frames):
        edge = pltpu.roll(token_ref[f, 1, 8 : 8 + cols, :], 2 * LAT, 1)
        token_ref[f, 0, 8 : 8 + cols, :] = jnp.where(at_first, edge, above[f, 0])
        edge = pltpu.roll(token_ref[f, rows, 8 : 8 + cols, :], 2 * NARROW - 2 * LAT, 1)
        token_ref[f, rows + 1, 8 : 8 + cols, :] = jnp.where(at_last, edge, below[f, 0])
    for f in range(frames):
        for r in range(rows + 2):
            start = token_ref[f, r, 8:16, :]
            token_ref[f, r, 7:8, :] = pltpu.roll(start, LAT, 1)[0:1]
            end = token_ref[f, r, cols : 8 + cols, :]
            token_ref[f, r, 8 + cols : 9 + cols, :] = pltpu.roll(end, 2 * NARROW - LAT, 1)[7:8]

    for side in range(2):
        pair = jnp.where(
            lane < NARROW,
            token_ref[:, :, 7 + side : 7 + side + cols, :],
            token_ref[:, :, 8 + side : 8 + side + cols, :],
        ).astype(jnp.bfloat16)
        pair_ref[side, 2:] = pair
        pair_ref[side, 0] = pair[0]
        pair_ref[side, 1] = pair[0]

    gaps = rows + 1
    for side in range(2):
        columns = jnp.concatenate(
            [
                pair_ref[side, dt : dt + frames, rr : rr + gaps].reshape(frames * gaps * cols, 2 * NARROW)
                for dt in range(3)
                for rr in range(2)
            ],
            axis=1,
        )
        first = jnp.dot(columns, weight_ref[side], preferred_element_type=jnp.float32) * VAE_SCALE
        first = first.astype(jnp.bfloat16).astype(jnp.float32)
        act = first / (1.0 + jnp.exp(-first))
        first = first.reshape(frames, gaps, cols, 2 * CH)
        act = act.reshape(frames, gaps, cols, 2 * CH)
        for f in range(frames):
            for g in range(gaps):
                for ro in range(2):
                    for part in range(CH // 128):
                        lanes = slice(ro * CH + part * 128, ro * CH + part * 128 + 128)
                        row = 2 * g + ro
                        into = pl.ds(8 + side, cols, stride=2)
                        first_ref[part, f, row, into, :] = first[f, g, :, lanes]
                        act_ref[part, f, row, into, :] = act[f, g, :, lanes]

    width = 2 * cols
    height = 2 * rows
    for part in range(CH // 128):
        for f in range(frames):
            act_ref[part, f, 0] = jnp.where(at_first, act_ref[part, f, 1], act_ref[part, f, 0])
            act_ref[part, f, height + 1] = jnp.where(
                at_last, act_ref[part, f, height], act_ref[part, f, height + 1]
            )
        act_ref[part, :, :, 7:8, :] = act_ref[part, :, :, 8:9, :]
        act_ref[part, :, :, 8 + width : 9 + width, :] = act_ref[part, :, :, 7 + width : 8 + width, :]
        for dz in range(3):
            lanes = slice(dz * CH + part * 128, dz * CH + part * 128 + 128)
            shifted = act_ref[part, :, :, 7 + dz : 7 + dz + width, :].astype(jnp.bfloat16)
            wide_ref[2:, :, :, lanes] = shifted
            wide_ref[0, :, :, lanes] = shifted[0]
            wide_ref[1, :, :, lanes] = shifted[0]

    each_shard(lambda copy: copy.wait())
    cells = frames * height * width
    total = None
    for dt in range(3):
        for dy in range(3):
            window = wide_ref[dt : dt + frames, dy : dy + height].reshape(cells, 3 * CH)
            weight = jnp.concatenate(
                [kernel_ref[:, (dt * 3 + dy) * 3 + dz].reshape(CH, CH) for dz in range(3)], axis=0
            )
            product = jnp.dot(window, weight, preferred_element_type=jnp.float32)
            total = product if total is None else total + product
    total = total.reshape(frames, height, width, CH)
    for part in range(CH // 128):
        lanes = slice(part * 128, part * 128 + 128)
        residual = first_ref[part, :, 1 : 1 + height, 8 : 8 + width, :]
        out_ref[:, :, :, lanes] = (total[:, :, :, lanes] + residual).astype(jnp.bfloat16)


def decode(frames, rows, cols, place, messages, weights, groups, shards):
    height, width = 2 * rows, 2 * cols
    count = len(messages)
    taps, depth = shards[0].shape[-3:-1]

    def whole(shape):
        return pl.BlockSpec(shape, lambda i, place: (0,) * len(shape))

    def body(place_ref, *refs):
        message_refs, refs = refs[:count], refs[count:]
        weight_ref, shard_refs = refs[0], refs[1 : 1 + len(shards)]
        decode_kernel(
            frames, rows, cols, place_ref, message_refs, weight_ref, shard_refs, *refs[1 + len(shards) :]
        )

    grid_spec = pltpu.PrefetchScalarGridSpec(
        num_scalar_prefetch=1,
        grid=(1,),
        in_specs=[whole(part.shape) for part in messages]
        + [pl.BlockSpec(memory_space=pltpu.VMEM)]
        + [pl.BlockSpec(memory_space=pl.ANY)] * len(shards),
        out_specs=whole((frames, height, width, CH)),
        scratch_shapes=[
            pltpu.VMEM((frames, rows + 2, cols + 16, 2 * NARROW), jnp.float32),
            pltpu.VMEM((2, frames + 2, rows + 2, cols, 2 * NARROW), jnp.bfloat16),
            pltpu.VMEM((CH // 128, frames, height + 2, width + 16, 128), jnp.float32),
            pltpu.VMEM((CH // 128, frames, height + 2, width + 16, 128), jnp.float32),
            pltpu.VMEM((frames + 2, height + 2, width, 3 * CH), jnp.bfloat16),
            pltpu.VMEM((groups, taps, depth, CH), jnp.bfloat16),
            pltpu.SemaphoreType.DMA((len(shards),)),
        ],
    )
    return pl.pallas_call(
        body,
        grid_spec=grid_spec,
        out_shape=jax.ShapeDtypeStruct((frames, height, width, CH), jnp.bfloat16),
        compiler_params=pltpu.CompilerParams(vmem_limit_bytes=32 * MIB),
        cost_estimate=pl.CostEstimate(
            flops=2 * frames * height * width * 27 * CH * CH,
            bytes_accessed=27 * CH * CH * 2 + frames * height * width * CH * 2,
            transcendentals=frames * height * width * CH,
        ),
        name="decode_block",
    )(place, *messages, weights, *shards)


def trade_shards(shard, segment_count):
    segments = range(segment_count)
    near = [(s * 4 + g, s * 4 + (g ^ (1 + s % 2))) for s in segments for g in range(4)]
    far = [(s * 4 + g, s * 4 + (g ^ 3)) for s in segments for g in ((1, 2), (0, 3))[s % 2]]
    return [lax.ppermute(shard, ("segment", "grp"), pairs) for pairs in (near, far)]


def swap_shards(near, far, ready, segment_count):
    near, far, _ = lax.optimization_barrier((near, far, ready))
    segments = range(segment_count)
    pairs = [(s * 4 + g, (s ^ 1) * 4 + g) for s in segments for g in ((1, 2), (0, 3))[s % 2]]
    return (
        near,
        lax.ppermute(near, "segment", [(s, s ^ 1) for s in segments]),
        far,
        lax.ppermute(far, ("segment", "grp"), pairs),
    )


def local(
    queries,
    key_states,
    value_states,
    kept_tiles,
    kept_counts,
    patch_weight,
    decode_slot,
    first_kernel,
    second_kernel,
):
    frames, rows, cols = queries.shape[2:5]
    sp_count = lax.axis_size("sp")
    sp_rank = lax.axis_index("sp")
    segment_count = lax.axis_size("segment")
    segment_rank = lax.axis_index("segment")

    weights = first_weights(first_kernel)
    picks = (decode_slot == segment_rank).astype(jnp.int32)
    source = jnp.sum(jnp.arange(segment_count, dtype=jnp.int32) * picks)
    step = lax.rem(segment_rank - source + segment_count, segment_count)
    group_count = lax.axis_size("grp")
    group = lax.axis_index("grp")
    core = lax.rem(segment_rank, 2)
    line = group_count == 4 and segment_count % 2 == 0
    places = [sp_rank, jnp.int32(sp_count), step]
    if line:
        inner = jnp.logical_or(group == 1, group == 2)
        places += [group, group ^ (1 + core), group ^ (2 - core), group ^ 3, group ^ 3]
        places.append((inner == (core == 0)).astype(jnp.int32))
        traded = trade_shards(second_kernel, segment_count)
    else:
        places += [jnp.int32(0)] * 2
    place = jnp.stack(places).astype(jnp.int32)

    arguments = (queries, key_states, value_states, kept_tiles, kept_counts, patch_weight)
    if sp_count == 2 and rows * sp_count == TH and frames == TT:
        message, (weights, place) = split_attention(*arguments, (weights, place))
    else:
        message = exchanged_attention(*arguments)
    if line:
        shards = [second_kernel, *swap_shards(*traded, message, segment_count)]
    else:
        shards = [lax.all_gather(second_kernel, "grp", axis=0, tiled=False)]
    messages = [message] + [
        lax.ppermute(message, "segment", [(i, (i + step) % segment_count) for i in range(segment_count)])
        for step in range(1, segment_count)
    ]
    return decode(frames, rows, cols, place, messages, weights, group_count, shards)[None, None]


def solution(mesh):
    return jax.shard_map(
        local,
        mesh=mesh,
        in_specs=(
            P("segment", "grp", None, "sp", None, None),
            P("segment", "grp", None, "sp", None, None),
            P("segment", "grp", None, "sp", None, None),
            P(),
            P(),
            P(),
            P(),
            P(),
            P(None, "grp", None),
        ),
        out_specs=P("segment", "grp", None, "sp", None, None),
        check_vma=False,
    )
```
